128 devices in a mesh: tm: 32 (over y, x, core), head: 4 (over z).
Axes of the slice: x: 4, y: 4, z: 4, core: 2. Of those that a mesh axis runs over, the one named last changes fastest.
Arguments:
- tokens: bfloat16 [65536, 2240], P('tm'), may hold values from -6 to 6
- qkv_weight: bfloat16 [2240, 6720], P('tm', 'head'), may hold values from -0.125 to 0.125
- block_mask: int32 [128], P('tm'), may hold values from 0 to 268435455
- head_scale: float32 [20], P('head'), may hold values from 0.8 to 3.75, as said below
- norm_gain: float32 [2240], P('head'), may hold values from 0.25 to 1.75
Outputs:
- attended: bfloat16 [65536, 2240], P('tm', 'head')
The draws below stay inside these ranges and needn't reach their ends.
Inputs may be any that keep to these rules, and one draw needn't show every extreme that they name: `head_scale`: a per-head positive scale.
All inputs are finite; a program needn't handle non-finite values.
Results may differ from the reference program's by a relative error of at most 0.0055.
Values may be sent and summed in bfloat16 or wider, within the bound.
No kernel may reach another device: no remote copies, remote signals or barrier semaphores. Data moves between devices by JAX's collectives and lax.ppermute only.
A program may use at most 128 MiB of HBM per device.

```python
import jax
import jax.numpy as jnp
from jax import lax

D = 2240
H = 20
DH = 112
BLOCK = 64
GROUP = 512
TOKENS = 65536
GROUPS = 128


def draw_head_scale(key, part):
    key = jax.random.fold_in(key, 7)
    factor = jax.random.uniform(key, (H,), jnp.float32, 0.8, 1.25)
    ramp = 1.0 + 2.0 * jnp.arange(H).astype(jnp.float32) / (H - 1)
    return (ramp * factor).astype(jnp.float32)


def plant(entries, rng, low, high):
    shape = entries.shape
    index_at = [jax.random.randint(jax.random.fold_in(rng, axis), (), 0, shape[axis]) for axis in range(len(shape))]
    entries = entries.at[tuple(index_at)].set(low)
    longest = shape.index(max(shape))
    index_at[longest] = (index_at[longest] + 1) % shape[longest]
    return entries.at[tuple(index_at)].set(high)


def levels(own_key, dims, split, least, top_value):
    level = 1.0
    for dim, parts in split:
        steps = jax.random.uniform(jax.random.fold_in(jax.random.fold_in(own_key, 6), dim), (parts,), jnp.float32, least / len(split), top_value / len(split))
        level = level * jnp.repeat(jnp.exp(steps), dims[dim] // parts).reshape((-1,) + (1,) * (len(dims) - 1 - dim))
    return level


def centred(own_key, extent, width, most, cuts=(), held_as=jnp.bfloat16):
    factor_of = levels(own_key, extent, cuts, -0.22, 0.18) if cuts else 1.0
    result = jax.random.normal(own_key, extent, jnp.float32) * width * factor_of
    return jnp.minimum(jnp.maximum(result, -most), most).astype(held_as)


def setup_inputs(seed: int = 0) -> dict:
    seeds = jax.random.split(jax.random.key(seed), 6)
    tokens = centred(seeds[0], (TOKENS, D), 1.0, 6.0, ((0, 32),))
    qkv_weight = centred(seeds[1], (D, 3 * H * DH), D ** -0.5, 0.125, ((0, 32), (1, 4)))
    block_mask = plant(jax.random.randint(seeds[2], (GROUPS,), 0, 268435456), jax.random.fold_in(seeds[2], 1), 0, 268435455).astype(jnp.int32)
    head_scale = draw_head_scale(jax.random.fold_in(seeds[5], 71), 0)
    norm_gain = jnp.clip(1.0 + 0.15 * jax.random.normal(seeds[4], (H * DH,), jnp.float32), 0.25, 1.75)
    return dict(tokens=tokens, qkv_weight=qkv_weight, block_mask=block_mask, head_scale=head_scale, norm_gain=norm_gain)


def token_mask(codes, block):
    row = jnp.arange(8).astype(jnp.int32)[:, None]
    col = jnp.arange(8).astype(jnp.int32)[None, :]
    bits = jnp.where(row > col, row * (row - 1) // 2 + col, 0).astype(jnp.int32)
    shifted = jnp.right_shift(codes.astype(jnp.int32)[:, None, None], bits[None])
    block_ok = (row > col)[None] & (jnp.bitwise_and(shifted, 1) == 1)
    wide = jnp.repeat(jnp.repeat(block_ok, block, axis=1), block, axis=2)
    pos = jnp.arange(8 * block).astype(jnp.int32)
    same = (pos[:, None] // block == pos[None, :] // block) & (pos[:, None] >= pos[None, :])
    return wide | same[None]

def reference(tokens, qkv_weight, block_mask, head_scale, norm_gain):
    qkv = jnp.dot(tokens, qkv_weight, preferred_element_type=jnp.float32).astype(jnp.bfloat16)
    qkv = qkv.reshape(GROUPS, GROUP, H, 3, DH)
    fq = (jax.nn.elu(qkv[:, :, :, 0].astype(jnp.float32)) + 1.0).astype(jnp.bfloat16)
    fk = (jax.nn.elu(qkv[:, :, :, 1].astype(jnp.float32)) + 1.0).astype(jnp.bfloat16)
    vals = qkv[:, :, :, 2]
    state = jnp.einsum('ncht,nchu->nhtu', fk.astype(jnp.float32), vals.astype(jnp.float32))
    norm_state = lax.optimization_barrier(jnp.sum(fk.astype(jnp.float32), axis=1))
    prefix = jnp.cumsum(state, axis=0) - state
    norm_prefix = jnp.cumsum(norm_state, axis=0) - norm_state

    def one_block(items):
        fq_b, fk_b, v_b, pre_b, npre_b, code = items
        allowed = token_mask(code[None], BLOCK)[0]
        scores = jnp.einsum('cht,sht->hcs', fq_b.astype(jnp.float32), fk_b.astype(jnp.float32))
        scores = jnp.where(allowed[None], scores, 0.0)
        weights = scores.astype(jnp.bfloat16)
        fq32 = fq_b.astype(jnp.float32)
        numer = jnp.einsum('hcs,shu->chu', weights.astype(jnp.float32), v_b.astype(jnp.float32))
        numer = numer + jnp.einsum('cht,htu->chu', fq32, pre_b, precision=lax.Precision.HIGHEST)
        denom = jnp.transpose(lax.optimization_barrier(jnp.sum(scores, axis=2))) + lax.optimization_barrier(jnp.sum(fq32 * npre_b[None], axis=2))
        return numer / denom[:, :, None]
    out = lax.map(one_block, (fq, fk, vals, prefix, norm_prefix, block_mask))
    out = out.reshape(TOKENS, H, DH) * head_scale[None, :, None]
    mean_square = lax.optimization_barrier(jnp.mean(out * out, axis=(1, 2)))
    normed = out / jnp.sqrt(mean_square + 1e-06)[:, None, None] * norm_gain.reshape(H, DH)[None]
    return normed.reshape(TOKENS, H * DH).astype(jnp.bfloat16)
```

```python
import jax
import jax.numpy as jnp
from jax import lax
from jax.experimental import pallas as pl
from jax.experimental.pallas import tpu as pltpu
from jax.sharding import PartitionSpec as P

H = 20
DH = 112
GROUP = 512
D = 2240
HL = 5
CHIPS = 16
SHARD = 70
ROWS = 144
K = CHIPS * ROWS
VA = 128
C1 = 640
C2 = 256
BF = jnp.bfloat16
F32 = jnp.float32
MIB = 1 << 20


def place(y, x, c):
    return (y % 4) * 8 + (x % 4) * 2 + c


def perm(move):
    return [
        (place(y, x, c), place(*move(y, x, c)))
        for y in range(4)
        for x in range(4)
        for c in range(2)
    ]


SIBLING = perm(lambda y, x, c: (y, x, 1 - c))


def first_leg(d):
    return perm(lambda y, x, c: (y, x + d, c) if c == 0 else (y + d, x, c))


def second_leg(d):
    return perm(lambda y, x, c: (y + d, x, c) if c == 0 else (y, x + d, c))


def along_x(d):
    return perm(lambda y, x, c: (y, x + d, c))


def later_y(d):
    return [
        (place(y, x, c), place(y + d, x, c))
        for y in range(4 - d)
        for x in range(4)
        for c in range(2)
    ]


def shift(a, moves):
    return lax.ppermute(a, "tm", moves)


def column_sets(w):
    heads = w.reshape(w.shape[0], HL, 3, DH)
    q, k, v = (heads[:, :, i].reshape(w.shape[0], HL * DH) for i in range(3))
    zero = jnp.zeros((w.shape[0], 64), w.dtype)
    one = jnp.concatenate([k, q[:, :80], q[:, 160:368], zero[:, :48]], axis=1)
    two = jnp.concatenate([v, q[:, 80:160], q[:, 368:], zero], axis=1)
    return one, two


def spread_kernel(x_ref, o_ref):
    for i in range(CHIPS):
        o_ref[i * ROWS : i * ROWS + 2 * SHARD, :] = x_ref[i * 2 * SHARD : (i + 1) * 2 * SHARD, :]
        o_ref[i * ROWS + 2 * SHARD : (i + 1) * ROWS, :] = jnp.zeros(
            (ROWS - 2 * SHARD, x_ref.shape[1]), BF
        )


def spread(xt):
    n = xt.shape[1]
    blk = 256
    return pl.pallas_call(
        spread_kernel,
        grid=(n // blk,),
        in_specs=[pl.BlockSpec((D, blk), lambda g: (0, g))],
        out_specs=pl.BlockSpec((K, blk), lambda g: (0, g)),
        out_shape=jax.ShapeDtypeStruct((K, n), BF),
        compiler_params=pltpu.CompilerParams(vmem_limit_bytes=24 * MIB),
        cost_estimate=pl.CostEstimate(flops=0, bytes_accessed=2 * n * K * 2, transcendentals=0),
        name="spread",
    )(xt)


def load_weights(pos, own, sib, wbuf, wt, sem, cols):
    y, x, c = pos[0], pos[1], pos[2]
    copies = []
    for side, blocks in enumerate((own, sib)):
        which = c if side == 0 else 1 - c
        for d in range(4):
            for r in range(4):
                dy = jnp.where(which == 0, d, r)
                dx = jnp.where(which == 0, r, d)
                chip = ((y + 4 - dy) & 3) * 4 + ((x + 4 - dx) & 3)
                at = pl.multiple_of(chip * ROWS, ROWS)
                copies.append(
                    pltpu.make_async_copy(
                        blocks[d].at[r],
                        wbuf.at[which, pl.ds(at, ROWS)],
                        sem.at[len(copies)],
                    )
                )
    for copy in copies:
        copy.start()
    for copy in copies:
        copy.wait()
    for which in range(2):
        for kb in range(K // 256):
            wt[which * cols : (which + 1) * cols, kb * 256 : (kb + 1) * 256] = wbuf[
                which, kb * 256 : (kb + 1) * 256, :
            ].T


def feature(raw):
    a = raw.astype(BF).astype(F32)
    return jnp.where(a > 0, a + 1.0, jnp.exp(jnp.minimum(a, 0.0))).astype(BF)


def kv_kernel(pos, *refs):
    own, sib = refs[:4], refs[4:8]
    x_ref, fk_ref, v_ref, q_ref, pre_ref, tot_ref, wbuf, wt, run, sem = refs[8:]
    g = pl.program_id(0)

    @pl.when(g == 0)
    def _():
        load_weights(pos, own, sib, wbuf, wt, sem, C1)
        run[...] = jnp.zeros_like(run)

    x = x_ref[...]
    one = jnp.dot(wt[:C1, :], x, preferred_element_type=F32)
    fk = feature(one)
    q_ref[:80, :] = fk[HL * DH :, :]
    two = jnp.dot(wt[C1:, :], x, preferred_element_type=F32)
    q_ref[80:, :] = feature(two[HL * DH :, :])
    tail = (lax.broadcasted_iota(jnp.int32, (VA - DH, GROUP), 0) == 0).astype(F32).astype(BF)
    for h in range(HL):
        kn = fk[h * DH : (h + 1) * DH, :].T
        fk_ref[h] = kn
        va = jnp.concatenate([two[h * DH : (h + 1) * DH, :].astype(BF), tail], axis=0)
        v_ref[h] = va
        state = jnp.dot(va, kn, preferred_element_type=F32)
        before = run[h]
        pre_ref[0, h] = before
        run[h] = before + state

    @pl.when(g == pl.num_programs(0) - 1)
    def _():
        tot_ref[...] = run[...].astype(BF)


def kv_call(pos, own, sib, xp):
    n = xp.shape[1]
    groups = n // GROUP
    anywhere = pl.BlockSpec(memory_space=pl.ANY)
    return pl.pallas_call(
        kv_kernel,
        grid_spec=pltpu.PrefetchScalarGridSpec(
            num_scalar_prefetch=1,
            grid=(groups,),
            in_specs=[anywhere] * 8 + [pl.BlockSpec((K, GROUP), lambda g, p: (0, g))],
            out_specs=[
                pl.BlockSpec((HL, GROUP, DH), lambda g, p: (0, g, 0)),
                pl.BlockSpec((HL, VA, GROUP), lambda g, p: (0, 0, g)),
                pl.BlockSpec((160, GROUP), lambda g, p: (0, g)),
                pl.BlockSpec((1, HL, VA, DH), lambda g, p: (g, 0, 0, 0)),
                pl.BlockSpec((HL, VA, DH), lambda g, p: (0, 0, 0)),
            ],
            scratch_shapes=[
                pltpu.VMEM((2, K, C1), BF),
                pltpu.VMEM((2 * C1, K), BF),
                pltpu.VMEM((HL, VA, DH), F32),
                pltpu.SemaphoreType.DMA((32,)),
            ],
        ),
        out_shape=[
            jax.ShapeDtypeStruct((HL, n, DH), BF),
            jax.ShapeDtypeStruct((HL, VA, n), BF),
            jax.ShapeDtypeStruct((160, n), BF),
            jax.ShapeDtypeStruct((groups, HL, VA, DH), F32),
            jax.ShapeDtypeStruct((HL, VA, DH), BF),
        ],
        compiler_params=pltpu.CompilerParams(vmem_limit_bytes=40 * MIB),
        cost_estimate=pl.CostEstimate(
            flops=2 * n * K * 2 * C1, bytes_accessed=n * K * 2 + 2 * K * C1 * 2, transcendentals=0
        ),
        name="keys_values",
    )(pos, *own, *sib, xp)


def mask_rows(code, j0, rows, t0, cols):
    parts = []
    for j in range(j0, j0 + rows // 64):
        t = lax.broadcasted_iota(jnp.int32, (64, cols), 1) + t0
        s = lax.broadcasted_iota(jnp.int32, (64, cols), 0)
        i = t >> 6
        bit = (jnp.full((64, cols), code, jnp.int32) >> (((i * (i - 1)) >> 1) + j)) & 1
        same = jnp.where(s <= (t & 63), 1, 0)
        keep = jnp.where(i > j, bit, jnp.where(i == j, same, 0))
        parts.append(keep.astype(F32).astype(BF))
    return jnp.concatenate(parts, axis=0)


def q_kernel(pos, codes, *refs):
    own, sib = refs[:4], refs[4:8]
    x_ref, fk_ref, v_ref, q_ref, fq_ref, num_ref, wbuf, wt, sem = refs[8:]
    g = pl.program_id(0)

    @pl.when(g == 0)
    def _():
        load_weights(pos, own, sib, wbuf, wt, sem, C2)

    raw = jnp.dot(wt[...], x_ref[...], preferred_element_type=F32)
    fq_ref[:160, :] = q_ref[...]
    fq_ref[160:368, :] = feature(raw[:208, :])
    fq_ref[368:, :] = feature(raw[C2 : C2 + 192, :])
    code = codes[g]
    half = GROUP // 2
    upper = mask_rows(code, 0, half, 0, GROUP)
    lower = mask_rows(code, 4, half, half, half)
    for h in range(HL):
        fq = fq_ref[h * DH : (h + 1) * DH, :]
        top = jnp.dot(fk_ref[h, :half, :], fq, preferred_element_type=F32)
        top = top.astype(BF) * upper
        low = jnp.dot(fk_ref[h, half:, :], fq[:, half:], preferred_element_type=F32)
        low = low.astype(BF) * lower
        num = jnp.dot(v_ref[h, :, :half], top, preferred_element_type=F32)
        more = jnp.dot(v_ref[h, :, half:], low, preferred_element_type=F32)
        num_ref[h, :, :half] = num[:, :half]
        num_ref[h, :, half:] = num[:, half:] + more


def q_call(pos, codes, own, sib, xp, fk, v, q):
    n = xp.shape[1]
    groups = n // GROUP
    anywhere = pl.BlockSpec(memory_space=pl.ANY)
    return pl.pallas_call(
        q_kernel,
        grid_spec=pltpu.PrefetchScalarGridSpec(
            num_scalar_prefetch=2,
            grid=(groups,),
            in_specs=[anywhere] * 8
            + [
                pl.BlockSpec((K, GROUP), lambda g, p, m: (0, g)),
                pl.BlockSpec((HL, GROUP, DH), lambda g, p, m: (0, g, 0)),
                pl.BlockSpec((HL, VA, GROUP), lambda g, p, m: (0, 0, g)),
                pl.BlockSpec((160, GROUP), lambda g, p, m: (0, g)),
            ],
            out_specs=[
                pl.BlockSpec((HL * DH, GROUP), lambda g, p, m: (0, g)),
                pl.BlockSpec((HL, VA, GROUP), lambda g, p, m: (0, 0, g)),
            ],
            scratch_shapes=[
                pltpu.VMEM((2, K, C2), BF),
                pltpu.VMEM((2 * C2, K), BF),
                pltpu.SemaphoreType.DMA((32,)),
            ],
        ),
        out_shape=[
            jax.ShapeDtypeStruct((HL * DH, n), BF),
            jax.ShapeDtypeStruct((HL, VA, n), F32),
        ],
        compiler_params=pltpu.CompilerParams(vmem_limit_bytes=40 * MIB),
        cost_estimate=pl.CostEstimate(
            flops=2 * n * K * 2 * C2 + 2 * n * GROUP * 256 * 2 * HL,
            bytes_accessed=n * K * 2 + 2 * K * C2 * 2,
            transcendentals=0,
        ),
        name="queries",
    )(pos, codes, *own, *sib, xp, fk, v, q)


def join_kernel(scale, dev_ref, pre_ref, fq_ref, num_ref, out_ref, sq_ref):
    total = jnp.zeros((1, GROUP), F32)
    for h in range(HL):
        prefix = (dev_ref[h] + pre_ref[0, h]).astype(BF)
        fq = fq_ref[h * DH : (h + 1) * DH, :]
        num = num_ref[h] + jnp.dot(prefix, fq, preferred_element_type=F32)
        out = num[:DH, :] * (scale[h] / num[DH : DH + 1, :])
        out_ref[h * DH : (h + 1) * DH, :] = out
        total = total + jnp.sum(out * out, axis=0, keepdims=True)
    sq_ref[...] = total


def join_call(scale, dev, pre, fq, num):
    n = fq.shape[1]
    groups = n // GROUP
    return pl.pallas_call(
        join_kernel,
        grid_spec=pltpu.PrefetchScalarGridSpec(
            num_scalar_prefetch=1,
            grid=(groups,),
            in_specs=[
                pl.BlockSpec((HL, VA, DH), lambda g, s: (0, 0, 0)),
                pl.BlockSpec((1, HL, VA, DH), lambda g, s: (g, 0, 0, 0)),
                pl.BlockSpec((HL * DH, GROUP), lambda g, s: (0, g)),
                pl.BlockSpec((HL, VA, GROUP), lambda g, s: (0, 0, g)),
            ],
            out_specs=[
                pl.BlockSpec((HL * DH, GROUP), lambda g, s: (0, g)),
                pl.BlockSpec((1, GROUP), lambda g, s: (0, g)),
            ],
        ),
        out_shape=[
            jax.ShapeDtypeStruct((HL * DH, n), F32),
            jax.ShapeDtypeStruct((1, n), F32),
        ],
        compiler_params=pltpu.CompilerParams(vmem_limit_bytes=24 * MIB),
        cost_estimate=pl.CostEstimate(
            flops=2 * n * 256 * VA * HL, bytes_accessed=n * 560 * 12, transcendentals=0
        ),
        name="join",
    )(scale, dev, pre, fq, num)


def norm_kernel(out_ref, sq_ref, gain_ref, o_ref):
    inv = lax.rsqrt(sq_ref[...] * (1.0 / (H * DH)) + 1e-06)
    o_ref[...] = (out_ref[...] * inv * gain_ref[...]).astype(BF)


def norm_call(out, squares, gain):
    n = out.shape[1]
    return pl.pallas_call(
        norm_kernel,
        grid=(n // GROUP,),
        in_specs=[
            pl.BlockSpec((HL * DH, GROUP), lambda g: (0, g)),
            pl.BlockSpec((1, GROUP), lambda g: (0, g)),
            pl.BlockSpec((HL * DH, 1), lambda g: (0, 0)),
        ],
        out_specs=pl.BlockSpec((HL * DH, GROUP), lambda g: (0, g)),
        out_shape=jax.ShapeDtypeStruct((HL * DH, n), BF),
        compiler_params=pltpu.CompilerParams(vmem_limit_bytes=24 * MIB),
        cost_estimate=pl.CostEstimate(flops=0, bytes_accessed=n * 560 * 6, transcendentals=0),
        name="norm",
    )(out, squares, gain)


def gather(own):
    near = jnp.stack([own] + [shift(own, first_leg(d)) for d in (1, 2, 3)])
    return near


def body(tokens, qkv_weight, block_mask, head_scale, norm_gain):
    me = lax.axis_index("tm")
    core = me % 2
    pos = jnp.stack([me // 8, (me // 2) % 4, core]).astype(jnp.int32)
    one, two = column_sets(qkv_weight)
    theirs = shift(jnp.where(core == 0, two, one), SIBLING)
    mine = jnp.where(core == 0, one, two)
    rows = jnp.concatenate(
        [
            jnp.where(core == 0, mine, theirs),
            jnp.where(core == 0, theirs, mine),
            jnp.zeros((ROWS - 2 * SHARD, C1 + C2), BF),
        ]
    )
    near1 = gather(rows[:, :C1])
    near2 = gather(rows[:, C1:])
    near1, near2 = lax.optimization_barrier((near1, near2))
    own1 = [near1] + [shift(near1, second_leg(d)) for d in (1, 2, 3)]
    own2 = [near2] + [shift(near2, second_leg(d)) for d in (1, 2, 3)]
    sib1 = [shift(a, SIBLING) for a in own1]
    sib2 = [shift(a, SIBLING) for a in own2]

    xp = spread(tokens.T)
    fk, v, q, pre, tot = kv_call(pos, own1, sib1, xp)

    other = shift(tot, SIBLING).astype(F32)
    before = jnp.where(core == 1, other, 0.0)
    chip = (tot.astype(F32) + other).astype(BF)
    row = chip.astype(F32)
    for d in (1, 2, 3):
        got = shift(chip, along_x(d)).astype(F32)
        row = row + got
        before = before + jnp.where(pos[1] >= d, got, 0.0)
    row = row.astype(BF)
    for d in (1, 2, 3):
        before = before + shift(row, later_y(d)).astype(F32)

    fq, num = q_call(pos, block_mask, own2, sib2, xp, fk, v, q)
    out, squares = join_call(head_scale, before, pre, fq, num)
    squares = squares + sum(
        lax.ppermute(squares, "head", [(i, (i + d) % 4) for i in range(4)]) for d in (1, 2, 3)
    )
    return norm_call(out, squares, norm_gain.reshape(HL * DH, 1)).T


def solution(mesh):
    in_specs = (P("tm", None), P("tm", "head"), P("tm"), P("head"), P("head"))
    out_specs = P("tm", "head")
    return jax.shard_map(body, mesh=mesh, in_specs=in_specs, out_specs=out_specs, check_vma=False)
```

```python
import jax
import jax.numpy as jnp
from jax import lax
from jax.experimental import pallas as pl
from jax.experimental.pallas import tpu as pltpu
from jax.sharding import PartitionSpec as P

H = 20
DH = 112
GROUP = 512
D = 2240
HL = 5
SHARD = 70
PAD = 72
BLK = 4 * PAD
VA = 128
QCOL = 1152
COLS = 1792
BF = jnp.bfloat16
F32 = jnp.float32
MIB = 1 << 20
VMEM = 60 * MIB


def place(y, x, c):
    return (y % 4) * 8 + (x % 4) * 2 + c


def perm(move):
    return [
        (place(y, x, c), place(*move(y, x, c)))
        for y in range(4)
        for x in range(4)
        for c in range(2)
    ]


SIBLING = perm(lambda y, x, c: (y, x, 1 - c))


def first_leg(d):
    return perm(lambda y, x, c: (y, x + d, c) if c == 0 else (y + d, x, c))


def second_leg(d):
    return perm(lambda y, x, c: (y + d, x, c) if c == 0 else (y, x + d, c))


def along_x(d):
    return perm(lambda y, x, c: (y, x + d, c))


def later_y(d):
    return [
        (place(y, x, c), place(y + d, x, c))
        for y in range(4 - d)
        for x in range(4)
        for c in range(2)
    ]


def shift(a, moves):
    return lax.ppermute(a, "tm", moves)


def pack_kernel(pos, a0, a1, a2, a3, g_ref, parts, wide, sem):
    coord = jnp.where(pos[2] == 0, pos[1], pos[0])
    copies = [
        pltpu.make_async_copy(a, parts.at[(coord + 4 - r) & 3], sem.at[r])
        for r, a in enumerate((a0, a1, a2, a3))
    ]
    for copy in copies:
        copy.start()
    wide[...] = jnp.zeros_like(wide)
    for copy in copies:
        copy.wait()
    for p in range(4):
        shard = parts[p].astype(F32)
        for kind, base in ((0, QCOL), (1, 0), (2, HL * DH)):
            for h in range(HL):
                at = h * 3 * DH + kind * DH
                to = base + h * DH
                wide[p * PAD : p * PAD + SHARD, to : to + DH] = shard[:, at : at + DH]
    g_ref[...] = wide[...].astype(BF)


def pack(pos, shards):
    return pl.pallas_call(
        pack_kernel,
        grid_spec=pltpu.PrefetchScalarGridSpec(
            num_scalar_prefetch=1,
            grid=(1,),
            in_specs=[pl.BlockSpec(memory_space=pl.ANY)] * 4,
            out_specs=pl.BlockSpec((BLK, COLS), lambda g, p: (0, 0)),
            scratch_shapes=[
                pltpu.VMEM((4, SHARD, 3 * HL * DH), BF),
                pltpu.VMEM((BLK, COLS), F32),
                pltpu.SemaphoreType.DMA((4,)),
            ],
        ),
        out_shape=jax.ShapeDtypeStruct((BLK, COLS), BF),
        compiler_params=pltpu.CompilerParams(vmem_limit_bytes=VMEM),
        cost_estimate=pl.CostEstimate(flops=0, bytes_accessed=4 * MIB, transcendentals=0),
        name="pack",
    )(pos, *shards)


def spread_kernel(x_ref, o_ref):
    gap = jnp.zeros((PAD - SHARD, x_ref.shape[1]), BF)
    for y in range(4):
        for x in range(4):
            for c in range(2):
                block, slot = (y, x) if c == 0 else (4 + x, y)
                dev = place(y, x, c)
                at = slot * PAD
                o_ref[block, at : at + SHARD, :] = x_ref[dev * SHARD : (dev + 1) * SHARD, :]
                o_ref[block, at + SHARD : at + PAD, :] = gap


def spread(xt):
    n = xt.shape[1]
    blk = 256
    return pl.pallas_call(
        spread_kernel,
        grid=(n // blk,),
        in_specs=[pl.BlockSpec((D, blk), lambda g: (0, g))],
        out_specs=pl.BlockSpec((8, BLK, blk), lambda g: (0, 0, g)),
        out_shape=jax.ShapeDtypeStruct((8, BLK, n), BF),
        compiler_params=pltpu.CompilerParams(vmem_limit_bytes=VMEM),
        cost_estimate=pl.CostEstimate(flops=0, bytes_accessed=4 * n * D, transcendentals=0),
        name="spread",
    )(xt)


def product(w, x):
    return lax.dot_general(w, x, (((0,), (0,)), ((), ())), preferred_element_type=F32)


def fetch(pieces, wbuf, sem, first, cols):
    copies = [
        pltpu.make_async_copy(
            piece.at[:, pl.ds(first, cols)], wbuf.at[pl.ds(i * BLK, BLK)], sem.at[i]
        )
        for i, piece in enumerate(pieces)
    ]
    for copy in copies:
        copy.start()
    for copy in copies:
        copy.wait()


def rows_of(x_refs):
    return jnp.concatenate([x[0] for x in x_refs], axis=0)


def x_specs(n):
    return [
        pl.BlockSpec((1, BLK, GROUP), lambda g, b, *_, i=i: (b[i], 0, g)) for i in range(n)
    ]


def part_kernel(count, more, blocks, *refs):
    pieces, x_refs = refs[:count], refs[count : 2 * count]
    rest = refs[2 * count :]
    kv_in, q_in = rest[:2] if more else (None, None)
    kv_ref, q_ref, wbuf, sem = rest[2 * more :]

    @pl.when(pl.program_id(0) == 0)
    def _():
        fetch(pieces, wbuf, sem, 0, COLS)

    x = rows_of(x_refs)
    kv = product(wbuf[:, : 2 * HL * DH], x)
    kv_ref[...] = kv + kv_in[...] if more else kv
    q = product(wbuf[:, QCOL : QCOL + HL * DH], x)
    q_ref[...] = q + q_in[...] if more else q


def part_call(blocks, pieces, xp, sums=()):
    count, n = len(pieces), xp.shape[2]
    kv_spec = pl.BlockSpec((2 * HL * DH, GROUP), lambda g, b: (0, g))
    q_spec = pl.BlockSpec((HL * DH, GROUP), lambda g, b: (0, g))
    return pl.pallas_call(
        lambda *refs: part_kernel(count, 1 if sums else 0, *refs),
        grid_spec=pltpu.PrefetchScalarGridSpec(
            num_scalar_prefetch=1,
            grid=(n // GROUP,),
            in_specs=[pl.BlockSpec(memory_space=pl.ANY)] * count
            + x_specs(count)
            + ([kv_spec, q_spec] if sums else []),
            out_specs=[kv_spec, q_spec],
            scratch_shapes=[
                pltpu.VMEM((count * BLK, COLS), BF),
                pltpu.SemaphoreType.DMA((count,)),
            ],
        ),
        out_shape=[
            jax.ShapeDtypeStruct((2 * HL * DH, n), F32),
            jax.ShapeDtypeStruct((HL * DH, n), F32),
        ],
        compiler_params=pltpu.CompilerParams(vmem_limit_bytes=VMEM),
        cost_estimate=pl.CostEstimate(
            flops=2 * n * 768 * 1680, bytes_accessed=8 * n * 1680, transcendentals=0
        ),
        name="part_more" if sums else "part_first",
    )(blocks, *pieces, *([xp] * count), *sums)


def feature(raw):
    a = raw.astype(BF).astype(F32)
    return jnp.where(a > 0, a + 1.0, jnp.exp(jnp.minimum(a, 0.0))).astype(BF)


def kv_kernel(count, blocks, *refs):
    pieces, x_refs = refs[:count], refs[count : 2 * count]
    sum_ref, fk_ref, v_ref, pre_ref, tot_ref, wbuf, run, sem = refs[2 * count :]
    g = pl.program_id(0)

    @pl.when(g == 0)
    def _():
        fetch(pieces, wbuf, sem, 0, QCOL)
        run[...] = jnp.zeros_like(run)

    x = rows_of(x_refs)
    raw = product(wbuf[:, : 2 * HL * DH], x) + sum_ref[...]
    fk = feature(raw[: HL * DH, :])
    tail = (lax.broadcasted_iota(jnp.int32, (VA - DH, GROUP), 0) == 0).astype(F32).astype(BF)
    for h in range(HL):
        kn = fk[h * DH : (h + 1) * DH, :].T
        fk_ref[h] = kn
        at = (HL + h) * DH
        va = jnp.concatenate([raw[at : at + DH, :].astype(BF), tail], axis=0)
        v_ref[h] = va
        state = jnp.dot(va, kn, preferred_element_type=F32)
        before = run[h]
        pre_ref[0, h] = before
        run[h] = before + state

    @pl.when(g == pl.num_programs(0) - 1)
    def _():
        tot_ref[...] = run[...].astype(BF)


def kv_call(blocks, pieces, xp, sums):
    count, n = len(pieces), xp.shape[2]
    groups = n // GROUP
    return pl.pallas_call(
        lambda *refs: kv_kernel(count, *refs),
        grid_spec=pltpu.PrefetchScalarGridSpec(
            num_scalar_prefetch=1,
            grid=(groups,),
            in_specs=[pl.BlockSpec(memory_space=pl.ANY)] * count
            + x_specs(count)
            + [pl.BlockSpec((2 * HL * DH, GROUP), lambda g, p: (0, g))],
            out_specs=[
                pl.BlockSpec((HL, GROUP, DH), lambda g, p: (0, g, 0)),
                pl.BlockSpec((HL, VA, GROUP), lambda g, p: (0, 0, g)),
                pl.BlockSpec((1, HL, VA, DH), lambda g, p: (g, 0, 0, 0)),
                pl.BlockSpec((HL, VA, DH), lambda g, p: (0, 0, 0)),
            ],
            scratch_shapes=[
                pltpu.VMEM((count * BLK, QCOL), BF),
                pltpu.VMEM((HL, VA, DH), F32),
                pltpu.SemaphoreType.DMA((count,)),
            ],
        ),
        out_shape=[
            jax.ShapeDtypeStruct((HL, n, DH), BF),
            jax.ShapeDtypeStruct((HL, VA, n), BF),
            jax.ShapeDtypeStruct((groups, HL, VA, DH), F32),
            jax.ShapeDtypeStruct((HL, VA, DH), BF),
        ],
        compiler_params=pltpu.CompilerParams(vmem_limit_bytes=VMEM),
        cost_estimate=pl.CostEstimate(
            flops=2 * n * 1280 * 1120, bytes_accessed=4 * n * 1120, transcendentals=0
        ),
        name="keys_values",
    )(blocks, *pieces, *([xp] * count), sums)


def q_kernel(count, blocks, *refs):
    pieces, x_refs = refs[:count], refs[count : 2 * count]
    sum_ref, fq_ref, wbuf, sem = refs[2 * count :]

    @pl.when(pl.program_id(0) == 0)
    def _():
        fetch(pieces, wbuf, sem, QCOL, COLS - QCOL)

    x = rows_of(x_refs)
    fq_ref[...] = feature(product(wbuf[:, : HL * DH], x) + sum_ref[...])


def q_call(blocks, pieces, xp, sums):
    count, n = len(pieces), xp.shape[2]
    spec = pl.BlockSpec((HL * DH, GROUP), lambda g, p: (0, g))
    return pl.pallas_call(
        lambda *refs: q_kernel(count, *refs),
        grid_spec=pltpu.PrefetchScalarGridSpec(
            num_scalar_prefetch=1,
            grid=(n // GROUP,),
            in_specs=[pl.BlockSpec(memory_space=pl.ANY)] * count + x_specs(count) + [spec],
            out_specs=spec,
            scratch_shapes=[
                pltpu.VMEM((count * BLK, COLS - QCOL), BF),
                pltpu.SemaphoreType.DMA((count,)),
            ],
        ),
        out_shape=jax.ShapeDtypeStruct((HL * DH, n), BF),
        compiler_params=pltpu.CompilerParams(vmem_limit_bytes=VMEM),
        cost_estimate=pl.CostEstimate(
            flops=2 * n * 1280 * 560, bytes_accessed=4 * n * 560, transcendentals=0
        ),
        name="queries",
    )(blocks, *pieces, *([xp] * count), sums)


def mask_rows(code, j0, rows, t0, cols):
    parts = []
    for j in range(j0, j0 + rows // 64):
        t = lax.broadcasted_iota(jnp.int32, (64, cols), 1) + t0
        s = lax.broadcasted_iota(jnp.int32, (64, cols), 0)
        i = t >> 6
        bit = (jnp.full((64, cols), code, jnp.int32) >> (((i * (i - 1)) >> 1) + j)) & 1
        same = jnp.where(s <= (t & 63), 1, 0)
        keep = jnp.where(i > j, bit, jnp.where(i == j, same, 0))
        parts.append(keep.astype(F32).astype(BF))
    return jnp.concatenate(parts, axis=0)


def attend_kernel(codes, fk_ref, v_ref, fq_ref, num_ref):
    code = codes[pl.program_id(0)]
    half = GROUP // 2
    upper = mask_rows(code, 0, half, 0, GROUP)
    lower = mask_rows(code, 4, half, half, half)
    for h in range(HL):
        fq = fq_ref[h * DH : (h + 1) * DH, :]
        top = jnp.dot(fk_ref[h, :half, :], fq, preferred_element_type=F32)
        top = top.astype(BF) * upper
        low = jnp.dot(fk_ref[h, half:, :], fq[:, half:], preferred_element_type=F32)
        low = low.astype(BF) * lower
        num = jnp.dot(v_ref[h, :, :half], top, preferred_element_type=F32)
        more = jnp.dot(v_ref[h, :, half:], low, preferred_element_type=F32)
        num_ref[h, :, :half] = num[:, :half]
        num_ref[h, :, half:] = num[:, half:] + more


def attend_call(codes, fk, v, fq):
    n = fq.shape[1]
    return pl.pallas_call(
        attend_kernel,
        grid_spec=pltpu.PrefetchScalarGridSpec(
            num_scalar_prefetch=1,
            grid=(n // GROUP,),
            in_specs=[
                pl.BlockSpec((HL, GROUP, DH), lambda g, m: (0, g, 0)),
                pl.BlockSpec((HL, VA, GROUP), lambda g, m: (0, 0, g)),
                pl.BlockSpec((HL * DH, GROUP), lambda g, m: (0, g)),
            ],
            out_specs=pl.BlockSpec((HL, VA, GROUP), lambda g, m: (0, 0, g)),
        ),
        out_shape=jax.ShapeDtypeStruct((HL, VA, n), F32),
        compiler_params=pltpu.CompilerParams(vmem_limit_bytes=VMEM),
        cost_estimate=pl.CostEstimate(
            flops=2 * n * GROUP * 512 * 2 * HL, bytes_accessed=8 * n * 560, transcendentals=0
        ),
        name="attend",
    )(codes, fk, v, fq)


def join_kernel(scale, dev_ref, pre_ref, fq_ref, num_ref, out_ref, sq_ref):
    total = jnp.zeros((1, GROUP), F32)
    for h in range(HL):
        prefix = (dev_ref[h] + pre_ref[0, h]).astype(BF)
        fq = fq_ref[h * DH : (h + 1) * DH, :]
        num = num_ref[h] + jnp.dot(prefix, fq, preferred_element_type=F32)
        out = num[:DH, :] * (scale[h] / num[DH : DH + 1, :])
        out_ref[h * DH : (h + 1) * DH, :] = out
        total = total + jnp.sum(out * out, axis=0, keepdims=True)
    sq_ref[...] = total


def join_call(scale, dev, pre, fq, num):
    n = fq.shape[1]
    groups = n // GROUP
    return pl.pallas_call(
        join_kernel,
        grid_spec=pltpu.PrefetchScalarGridSpec(
            num_scalar_prefetch=1,
            grid=(groups,),
            in_specs=[
                pl.BlockSpec((HL, VA, DH), lambda g, s: (0, 0, 0)),
                pl.BlockSpec((1, HL, VA, DH), lambda g, s: (g, 0, 0, 0)),
                pl.BlockSpec((HL * DH, GROUP), lambda g, s: (0, g)),
                pl.BlockSpec((HL, VA, GROUP), lambda g, s: (0, 0, g)),
            ],
            out_specs=[
                pl.BlockSpec((HL * DH, GROUP), lambda g, s: (0, g)),
                pl.BlockSpec((1, GROUP), lambda g, s: (0, g)),
            ],
        ),
        out_shape=[
            jax.ShapeDtypeStruct((HL * DH, n), F32),
            jax.ShapeDtypeStruct((1, n), F32),
        ],
        compiler_params=pltpu.CompilerParams(vmem_limit_bytes=VMEM),
        cost_estimate=pl.CostEstimate(
            flops=2 * n * 256 * VA * HL, bytes_accessed=n * 560 * 12, transcendentals=0
        ),
        name="join",
    )(scale, dev, pre, fq, num)


def norm_kernel(out_ref, sq_ref, gain_ref, o_ref):
    inv = lax.rsqrt(sq_ref[...] * (1.0 / (H * DH)) + 1e-06)
    o_ref[...] = (out_ref[...] * inv * gain_ref[...]).astype(BF)


def norm_call(out, squares, gain):
    n = out.shape[1]
    return pl.pallas_call(
        norm_kernel,
        grid=(n // GROUP,),
        in_specs=[
            pl.BlockSpec((HL * DH, GROUP), lambda g: (0, g)),
            pl.BlockSpec((1, GROUP), lambda g: (0, g)),
            pl.BlockSpec((HL * DH, 1), lambda g: (0, 0)),
        ],
        out_specs=pl.BlockSpec((HL * DH, GROUP), lambda g: (0, g)),
        out_shape=jax.ShapeDtypeStruct((HL * DH, n), BF),
        compiler_params=pltpu.CompilerParams(vmem_limit_bytes=VMEM),
        cost_estimate=pl.CostEstimate(flops=0, bytes_accessed=n * 560 * 6, transcendentals=0),
        name="norm",
    )(out, squares, gain)


def body(tokens, qkv_weight, block_mask, head_scale, norm_gain):
    me = lax.axis_index("tm").astype(jnp.int32)
    y, x, core = me // 8, (me // 2) % 4, me % 2
    pos = jnp.stack([y, x, core])
    shards = [qkv_weight] + [shift(qkv_weight, first_leg(d)) for d in (1, 2, 3)]
    xp = spread(tokens.T)
    *shards, xp = lax.optimization_barrier((*shards, xp))
    near = pack(pos, shards)
    own = [near] + [shift(near, second_leg(d)) for d in (1, 2, 3)]
    sib = [shift(a, SIBLING) for a in own]

    def block(mine, d):
        which = core if mine else 1 - core
        return which * 4 + (jnp.where(which == 0, y, x) + 4 - d) % 4

    def blocks(steps):
        return jnp.stack([block(mine, d) for d in steps for mine in (True, False)])

    def pieces(steps):
        return [a[d] for d in steps for a in (own, sib)]

    sums = part_call(blocks([0]), pieces([0]), xp)
    kv_sum, q_sum = part_call(blocks([1]), pieces([1]), xp, sums)
    last = [2, 3]
    fk, v, pre, tot = kv_call(blocks(last), pieces(last), xp, kv_sum)

    other = shift(tot, SIBLING).astype(F32)
    before = jnp.where(core == 1, other, 0.0)
    chip = (tot.astype(F32) + other).astype(BF)
    chip, q_sum = lax.optimization_barrier((chip, q_sum))
    fq = q_call(blocks(last), pieces(last), xp, q_sum)
    row = chip.astype(F32)
    for d in (1, 2, 3):
        got = shift(chip, along_x(d)).astype(F32)
        row = row + got
        before = before + jnp.where(x >= d, got, 0.0)
    row, fq = lax.optimization_barrier((row.astype(BF), fq))
    num = attend_call(block_mask, fk, v, fq)
    for d in (1, 2, 3):
        before = before + shift(row, later_y(d)).astype(F32)

    out, squares = join_call(head_scale, before, pre, fq, num)
    squares = squares + sum(
        lax.ppermute(squares, "head", [(i, (i + d) % 4) for i in range(4)]) for d in (1, 2, 3)
    )
    return norm_call(out, squares, norm_gain.reshape(HL * DH, 1)).T


def solution(mesh):
    in_specs = (P("tm", None), P("tm", "head"), P("tm"), P("head"), P("head"))
    out_specs = P("tm", "head")
    return jax.shard_map(body, mesh=mesh, in_specs=in_specs, out_specs=out_specs, check_vma=False)
```

```python
import jax
import jax.numpy as jnp
from jax import lax
from jax.experimental import pallas as pl
from jax.experimental.pallas import tpu as pltpu
from jax.sharding import PartitionSpec as P

H = 20
DH = 112
GROUP = 512
D = 2240
HL = 5
SHARD = 70
PAD = 72
BLK = 4 * PAD
VA = 128
QCOL = 1152
COLS = 1792
BF = jnp.bfloat16
F32 = jnp.float32
MIB = 1 << 20
VMEM = 60 * MIB
QUICK = pl.CostEstimate(flops=1, bytes_accessed=1, transcendentals=0)


def place(y, x, c):
    return (y % 4) * 8 + (x % 4) * 2 + c


def perm(move):
    return [
        (place(y, x, c), place(*move(y, x, c)))
        for y in range(4)
        for x in range(4)
        for c in range(2)
    ]


SIBLING = perm(lambda y, x, c: (y, x, 1 - c))


def first_leg(d):
    return perm(lambda y, x, c: (y, x + d, c) if c == 0 else (y + d, x, c))


def second_leg(d):
    return perm(lambda y, x, c: (y + d, x, c) if c == 0 else (y, x + d, c))


def along_x(d):
    return perm(lambda y, x, c: (y, x + d, c))


def later_y(d):
    return [
        (place(y, x, c), place(y + d, x, c))
        for y in range(4 - d)
        for x in range(4)
        for c in range(2)
    ]


def shift(a, moves):
    return lax.ppermute(a, "tm", moves)


def pack_kernel(pos, a0, a1, a2, a3, g_ref, parts, wide, sem):
    coord = jnp.where(pos[2] == 0, pos[1], pos[0])
    copies = [
        pltpu.make_async_copy(a, parts.at[(coord + 4 - r) & 3], sem.at[r])
        for r, a in enumerate((a0, a1, a2, a3))
    ]
    for copy in copies:
        copy.start()
    wide[...] = jnp.zeros_like(wide)
    for copy in copies:
        copy.wait()
    for p in range(4):
        shard = parts[p].astype(F32)
        for kind, base in ((0, QCOL), (1, 0), (2, HL * DH)):
            for h in range(HL):
                at = h * 3 * DH + kind * DH
                to = base + h * DH
                wide[p * PAD : p * PAD + SHARD, to : to + DH] = shard[:, at : at + DH]
    g_ref[...] = wide[...].astype(BF)


def pack(pos, shards):
    return pl.pallas_call(
        pack_kernel,
        grid_spec=pltpu.PrefetchScalarGridSpec(
            num_scalar_prefetch=1,
            grid=(1,),
            in_specs=[pl.BlockSpec(memory_space=pl.ANY)] * 4,
            out_specs=pl.BlockSpec((BLK, COLS), lambda g, p: (0, 0)),
            scratch_shapes=[
                pltpu.VMEM((4, SHARD, 3 * HL * DH), BF),
                pltpu.VMEM((BLK, COLS), F32),
                pltpu.SemaphoreType.DMA((4,)),
            ],
        ),
        out_shape=jax.ShapeDtypeStruct((BLK, COLS), BF),
        compiler_params=pltpu.CompilerParams(vmem_limit_bytes=VMEM),
        cost_estimate=QUICK,
        name="pack",
    )(pos, *shards)


def spread_kernel(x_ref, o_ref):
    gap = jnp.zeros((PAD - SHARD, x_ref.shape[1]), BF)
    for y in range(4):
        for x in range(4):
            for c in range(2):
                block, slot = (y, x) if c == 0 else (4 + x, y)
                dev = place(y, x, c)
                at = slot * PAD
                o_ref[block, at : at + SHARD, :] = x_ref[dev * SHARD : (dev + 1) * SHARD, :]
                o_ref[block, at + SHARD : at + PAD, :] = gap


def spread(xt):
    n = xt.shape[1]
    blk = 256
    return pl.pallas_call(
        spread_kernel,
        grid=(n // blk,),
        in_specs=[pl.BlockSpec((D, blk), lambda g: (0, g))],
        out_specs=pl.BlockSpec((8, BLK, blk), lambda g: (0, 0, g)),
        out_shape=jax.ShapeDtypeStruct((8, BLK, n), BF),
        compiler_params=pltpu.CompilerParams(vmem_limit_bytes=VMEM),
        cost_estimate=QUICK,
        name="spread",
    )(xt)


def product(w, x):
    return lax.dot_general(w, x, (((0,), (0,)), ((), ())), preferred_element_type=F32)


def fetch(pieces, wbuf, sem, first, cols):
    copies = [
        pltpu.make_async_copy(
            piece.at[:, pl.ds(first, cols)], wbuf.at[pl.ds(i * BLK, BLK)], sem.at[i]
        )
        for i, piece in enumerate(pieces)
    ]
    for copy in copies:
        copy.start()
    for copy in copies:
        copy.wait()


def rows_of(x_refs):
    return jnp.concatenate([x[0] for x in x_refs], axis=0)


def x_specs(n):
    return [
        pl.BlockSpec((1, BLK, GROUP), lambda g, b, *_, i=i: (b[i], 0, g)) for i in range(n)
    ]


def part_kernel(count, blocks, *refs):
    pieces, x_refs = refs[:count], refs[count : 2 * count]
    kv_ref, q_ref, wbuf, sem = refs[2 * count :]

    @pl.when(pl.program_id(0) == 0)
    def _():
        fetch(pieces, wbuf, sem, 0, COLS)

    x = rows_of(x_refs)
    kv_ref[...] = product(wbuf[:, : 2 * HL * DH], x)
    q_ref[...] = product(wbuf[:, QCOL : QCOL + HL * DH], x)


def part_call(blocks, pieces, xp):
    count, n = len(pieces), xp.shape[2]
    return pl.pallas_call(
        lambda *refs: part_kernel(count, *refs),
        grid_spec=pltpu.PrefetchScalarGridSpec(
            num_scalar_prefetch=1,
            grid=(n // GROUP,),
            in_specs=[pl.BlockSpec(memory_space=pl.ANY)] * count + x_specs(count),
            out_specs=[
                pl.BlockSpec((2 * HL * DH, GROUP), lambda g, b: (0, g)),
                pl.BlockSpec((HL * DH, GROUP), lambda g, b: (0, g)),
            ],
            scratch_shapes=[
                pltpu.VMEM((count * BLK, COLS), BF),
                pltpu.SemaphoreType.DMA((count,)),
            ],
        ),
        out_shape=[
            jax.ShapeDtypeStruct((2 * HL * DH, n), F32),
            jax.ShapeDtypeStruct((HL * DH, n), F32),
        ],
        compiler_params=pltpu.CompilerParams(vmem_limit_bytes=VMEM),
        cost_estimate=QUICK,
        name="part_first",
    )(blocks, *pieces, *([xp] * count))


def more_kernel(count, blocks, *refs):
    pieces, x_refs = refs[:count], refs[count : 2 * count]
    sum_ref, kv_ref, wbuf, sem = refs[2 * count :]

    @pl.when(pl.program_id(0) == 0)
    def _():
        fetch(pieces, wbuf, sem, 0, QCOL)

    x = rows_of(x_refs)
    kv_ref[...] = product(wbuf[:, : 2 * HL * DH], x) + sum_ref[...]


def more_call(blocks, pieces, xp, sums):
    count, n = len(pieces), xp.shape[2]
    spec = pl.BlockSpec((2 * HL * DH, GROUP), lambda g, b: (0, g))
    return pl.pallas_call(
        lambda *refs: more_kernel(count, *refs),
        grid_spec=pltpu.PrefetchScalarGridSpec(
            num_scalar_prefetch=1,
            grid=(n // GROUP,),
            in_specs=[pl.BlockSpec(memory_space=pl.ANY)] * count + x_specs(count) + [spec],
            out_specs=spec,
            scratch_shapes=[
                pltpu.VMEM((count * BLK, QCOL), BF),
                pltpu.SemaphoreType.DMA((count,)),
            ],
        ),
        out_shape=jax.ShapeDtypeStruct((2 * HL * DH, n), F32),
        compiler_params=pltpu.CompilerParams(vmem_limit_bytes=VMEM),
        cost_estimate=QUICK,
        name="part_more",
    )(blocks, *pieces, *([xp] * count), sums)


def feature(raw):
    a = raw.astype(BF).astype(F32)
    return jnp.where(a > 0, a + 1.0, jnp.exp(jnp.minimum(a, 0.0))).astype(BF)


def kv_kernel(count, blocks, *refs):
    pieces, x_refs = refs[:count], refs[count : 2 * count]
    sum_ref, fk_ref, v_ref, pre_ref, tot_ref, wbuf, run, sem = refs[2 * count :]
    g = pl.program_id(0)

    @pl.when(g == 0)
    def _():
        fetch(pieces, wbuf, sem, 0, QCOL)
        run[...] = jnp.zeros_like(run)

    x = rows_of(x_refs)
    half = HL * DH
    fk = feature(product(wbuf[:, :half], x) + sum_ref[:half, :])
    vals = (product(wbuf[:, half : 2 * half], x) + sum_ref[half:, :]).astype(BF)
    tail = (lax.broadcasted_iota(jnp.int32, (VA - DH, GROUP), 0) == 0).astype(F32).astype(BF)
    for h in range(HL):
        kn = fk[h * DH : (h + 1) * DH, :].T
        fk_ref[h] = kn
        va = jnp.concatenate([vals[h * DH : (h + 1) * DH, :], tail], axis=0)
        v_ref[h] = va
        state = jnp.dot(va, kn, preferred_element_type=F32)
        before = run[h]
        pre_ref[0, h] = before
        run[h] = before + state

    @pl.when(g == pl.num_programs(0) - 1)
    def _():
        tot_ref[...] = run[...].astype(BF)


def kv_call(blocks, pieces, xp, sums):
    count, n = len(pieces), xp.shape[2]
    groups = n // GROUP
    return pl.pallas_call(
        lambda *refs: kv_kernel(count, *refs),
        grid_spec=pltpu.PrefetchScalarGridSpec(
            num_scalar_prefetch=1,
            grid=(groups,),
            in_specs=[pl.BlockSpec(memory_space=pl.ANY)] * count
            + x_specs(count)
            + [pl.BlockSpec((2 * HL * DH, GROUP), lambda g, p: (0, g))],
            out_specs=[
                pl.BlockSpec((HL, GROUP, DH), lambda g, p: (0, g, 0)),
                pl.BlockSpec((HL, VA, GROUP), lambda g, p: (0, 0, g)),
                pl.BlockSpec((1, HL, VA, DH), lambda g, p: (g, 0, 0, 0)),
                pl.BlockSpec((HL, VA, DH), lambda g, p: (0, 0, 0)),
            ],
            scratch_shapes=[
                pltpu.VMEM((count * BLK, QCOL), BF),
                pltpu.VMEM((HL, VA, DH), F32),
                pltpu.SemaphoreType.DMA((count,)),
            ],
        ),
        out_shape=[
            jax.ShapeDtypeStruct((HL, n, DH), BF),
            jax.ShapeDtypeStruct((HL, VA, n), BF),
            jax.ShapeDtypeStruct((groups, HL, VA, DH), F32),
            jax.ShapeDtypeStruct((HL, VA, DH), BF),
        ],
        compiler_params=pltpu.CompilerParams(vmem_limit_bytes=VMEM),
        cost_estimate=QUICK,
        name="keys_values",
    )(blocks, *pieces, *([xp] * count), sums)


def q_kernel(count, blocks, *refs):
    pieces, x_refs = refs[:count], refs[count : 2 * count]
    sum_ref, fq_ref, wbuf, sem = refs[2 * count :]

    @pl.when(pl.program_id(0) == 0)
    def _():
        fetch(pieces, wbuf, sem, QCOL, COLS - QCOL)

    x = rows_of(x_refs)
    fq_ref[...] = feature(product(wbuf[:, : HL * DH], x) + sum_ref[...])


def q_call(blocks, pieces, xp, sums):
    count, n = len(pieces), xp.shape[2]
    spec = pl.BlockSpec((HL * DH, GROUP), lambda g, p: (0, g))
    return pl.pallas_call(
        lambda *refs: q_kernel(count, *refs),
        grid_spec=pltpu.PrefetchScalarGridSpec(
            num_scalar_prefetch=1,
            grid=(n // GROUP,),
            in_specs=[pl.BlockSpec(memory_space=pl.ANY)] * count + x_specs(count) + [spec],
            out_specs=spec,
            scratch_shapes=[
                pltpu.VMEM((count * BLK, COLS - QCOL), BF),
                pltpu.SemaphoreType.DMA((count,)),
            ],
        ),
        out_shape=jax.ShapeDtypeStruct((HL * DH, n), BF),
        compiler_params=pltpu.CompilerParams(vmem_limit_bytes=VMEM),
        cost_estimate=QUICK,
        name="queries",
    )(blocks, *pieces, *([xp] * count), sums)


def mask_rows(code, j0, rows, t0, cols):
    parts = []
    for j in range(j0, j0 + rows // 64):
        t = lax.broadcasted_iota(jnp.int32, (64, cols), 1) + t0
        s = lax.broadcasted_iota(jnp.int32, (64, cols), 0)
        i = t >> 6
        bit = (jnp.full((64, cols), code, jnp.int32) >> (((i * (i - 1)) >> 1) + j)) & 1
        same = jnp.where(s <= (t & 63), 1, 0)
        keep = jnp.where(i > j, bit, jnp.where(i == j, same, 0))
        parts.append(keep.astype(F32).astype(BF))
    return jnp.concatenate(parts, axis=0)


def attend_kernel(codes, fk_ref, v_ref, fq_ref, num_ref):
    code = codes[pl.program_id(0)]
    half = GROUP // 2
    upper = mask_rows(code, 0, half, 0, GROUP)
    lower = mask_rows(code, 4, half, half, half)
    for h in range(HL):
        fq = fq_ref[h * DH : (h + 1) * DH, :]
        top = jnp.dot(fk_ref[h, :half, :], fq, preferred_element_type=F32)
        top = top.astype(BF) * upper
        low = jnp.dot(fk_ref[h, half:, :], fq[:, half:], preferred_element_type=F32)
        low = low.astype(BF) * lower
        num = jnp.dot(v_ref[h, :, :half], top, preferred_element_type=F32)
        more = jnp.dot(v_ref[h, :, half:], low, preferred_element_type=F32)
        num_ref[h, :, :half] = num[:, :half]
        num_ref[h, :, half:] = num[:, half:] + more


def attend_call(codes, fk, v, fq):
    n = fq.shape[1]
    return pl.pallas_call(
        attend_kernel,
        grid_spec=pltpu.PrefetchScalarGridSpec(
            num_scalar_prefetch=1,
            grid=(n // GROUP,),
            in_specs=[
                pl.BlockSpec((HL, GROUP, DH), lambda g, m: (0, g, 0)),
                pl.BlockSpec((HL, VA, GROUP), lambda g, m: (0, 0, g)),
                pl.BlockSpec((HL * DH, GROUP), lambda g, m: (0, g)),
            ],
            out_specs=pl.BlockSpec((HL, VA, GROUP), lambda g, m: (0, 0, g)),
        ),
        out_shape=jax.ShapeDtypeStruct((HL, VA, n), F32),
        compiler_params=pltpu.CompilerParams(vmem_limit_bytes=20 * MIB),
        cost_estimate=QUICK,
        name="attend",
    )(codes, fk, v, fq)


def join_kernel(scale, dev_ref, pre_ref, fq_ref, num_ref, out_ref, sq_ref):
    total = jnp.zeros((1, GROUP), F32)
    for h in range(HL):
        prefix = (dev_ref[h] + pre_ref[0, h]).astype(BF)
        fq = fq_ref[h * DH : (h + 1) * DH, :]
        num = num_ref[h] + jnp.dot(prefix, fq, preferred_element_type=F32)
        out = num[:DH, :] * (scale[h] / num[DH : DH + 1, :])
        out_ref[h * DH : (h + 1) * DH, :] = out
        total = total + jnp.sum(out * out, axis=0, keepdims=True)
    sq_ref[...] = total


def join_call(scale, dev, pre, fq, num):
    n = fq.shape[1]
    groups = n // GROUP
    return pl.pallas_call(
        join_kernel,
        grid_spec=pltpu.PrefetchScalarGridSpec(
            num_scalar_prefetch=1,
            grid=(groups,),
            in_specs=[
                pl.BlockSpec((HL, VA, DH), lambda g, s: (0, 0, 0)),
                pl.BlockSpec((1, HL, VA, DH), lambda g, s: (g, 0, 0, 0)),
                pl.BlockSpec((HL * DH, GROUP), lambda g, s: (0, g)),
                pl.BlockSpec((HL, VA, GROUP), lambda g, s: (0, 0, g)),
            ],
            out_specs=[
                pl.BlockSpec((HL * DH, GROUP), lambda g, s: (0, g)),
                pl.BlockSpec((1, GROUP), lambda g, s: (0, g)),
            ],
        ),
        out_shape=[
            jax.ShapeDtypeStruct((HL * DH, n), F32),
            jax.ShapeDtypeStruct((1, n), F32),
        ],
        compiler_params=pltpu.CompilerParams(vmem_limit_bytes=20 * MIB),
        cost_estimate=QUICK,
        name="join",
    )(scale, dev, pre, fq, num)


def norm_kernel(out_ref, sq_ref, gain_ref, o_ref):
    inv = lax.rsqrt(sq_ref[...] * (1.0 / (H * DH)) + 1e-06)
    o_ref[...] = (out_ref[...] * inv * gain_ref[...]).astype(BF)


def norm_call(out, squares, gain):
    n = out.shape[1]
    return pl.pallas_call(
        norm_kernel,
        grid=(n // GROUP,),
        in_specs=[
            pl.BlockSpec((HL * DH, GROUP), lambda g: (0, g)),
            pl.BlockSpec((1, GROUP), lambda g: (0, g)),
            pl.BlockSpec((HL * DH, 1), lambda g: (0, 0)),
        ],
        out_specs=pl.BlockSpec((HL * DH, GROUP), lambda g: (0, g)),
        out_shape=jax.ShapeDtypeStruct((HL * DH, n), BF),
        compiler_params=pltpu.CompilerParams(vmem_limit_bytes=20 * MIB),
        cost_estimate=QUICK,
        name="norm",
    )(out, squares, gain)


def body(tokens, qkv_weight, block_mask, head_scale, norm_gain):
    me = lax.axis_index("tm").astype(jnp.int32)
    y, x, core = me // 8, (me // 2) % 4, me % 2
    pos = jnp.stack([y, x, core])
    shards = [qkv_weight] + [shift(qkv_weight, first_leg(d)) for d in (1, 2, 3)]
    near = pack(pos, shards)
    near, xt = lax.optimization_barrier((near, tokens.T))
    own = [near] + [shift(near, second_leg(d)) for d in (1, 2, 3)]
    sib = [shift(near, SIBLING)]
    xp = spread(xt)

    def block(mine, d):
        which = core if mine else 1 - core
        return which * 4 + (jnp.where(which == 0, y, x) + 4 - d) % 4

    def blocks(which):
        return jnp.stack([block(mine, d) for mine, d in which])

    def pieces(which):
        return [(own if mine else sib)[d] for mine, d in which]

    first = [(True, 0), (False, 0)]
    mine = [(True, d) for d in (1, 2, 3)]
    last = [(False, d) for d in (1, 2, 3)]
    kv_sum, q_sum = part_call(blocks(first), pieces(first), xp)
    *own, kv_sum = lax.optimization_barrier((*own, kv_sum))
    sib += [shift(a, SIBLING) for a in own[1:]]
    kv_sum = more_call(blocks(mine), pieces(mine), xp, kv_sum)
    fk, v, pre, tot = kv_call(blocks(last), pieces(last), xp, kv_sum)

    other = shift(tot, SIBLING).astype(F32)
    before = jnp.where(core == 1, other, 0.0)
    chip = (tot.astype(F32) + other).astype(BF)
    chip, q_sum = lax.optimization_barrier((chip, q_sum))
    fq = q_call(blocks(mine + last), pieces(mine + last), xp, q_sum)
    row = chip.astype(F32)
    for d in (1, 2, 3):
        got = shift(chip, along_x(d)).astype(F32)
        row = row + got
        before = before + jnp.where(x >= d, got, 0.0)
    row, fq = lax.optimization_barrier((row.astype(BF), fq))
    num = attend_call(block_mask, fk, v, fq)
    for d in (1, 2, 3):
        before = before + shift(row, later_y(d)).astype(F32)

    out, squares = join_call(head_scale, before, pre, fq, num)
    squares = squares + sum(
        lax.ppermute(squares, "head", [(i, (i + d) % 4) for i in range(4)]) for d in (1, 2, 3)
    )
    return norm_call(out, squares, norm_gain.reshape(HL * DH, 1)).T


def solution(mesh):
    in_specs = (P("tm", None), P("tm", "head"), P("tm"), P("head"), P("head"))
    out_specs = P("tm", "head")
    return jax.shard_map(body, mesh=mesh, in_specs=in_specs, out_specs=out_specs, check_vma=False)
```

```python
import jax
import jax.numpy as jnp
from jax import lax
from jax.experimental import pallas as pl
from jax.experimental.pallas import tpu as pltpu
from jax.sharding import PartitionSpec as P

H = 20
DH = 112
GROUP = 512
D = 2240
HL = 5
SHARD = 70
PAD = 72
BLK = 4 * PAD
VA = 128
QCOL = 1152
COLS = 1792
BF = jnp.bfloat16
F32 = jnp.float32
MIB = 1 << 20
QUICK = pl.CostEstimate(flops=1, bytes_accessed=1, transcendentals=0)


def place(y, x, c):
    return (y % 4) * 8 + (x % 4) * 2 + c


def perm(move):
    return [
        (place(y, x, c), place(*move(y, x, c)))
        for y in range(4)
        for x in range(4)
        for c in range(2)
    ]


SIBLING = perm(lambda y, x, c: (y, x, 1 - c))


def first_leg(d):
    return perm(lambda y, x, c: (y, x + d, c) if c == 0 else (y + d, x, c))


def second_leg(d):
    return perm(lambda y, x, c: (y + d, x, c) if c == 0 else (y, x + d, c))


def along_x(d):
    return perm(lambda y, x, c: (y, x + d, c))


def later_y(d):
    return [
        (place(y, x, c), place(y + d, x, c))
        for y in range(4 - d)
        for x in range(4)
        for c in range(2)
    ]


def shift(a, moves):
    return lax.ppermute(a, "tm", moves)


def pack_kernel(pos, a0, a1, a2, a3, g_ref, wide):
    coord = jnp.where(pos[2] == 0, pos[1], pos[0])
    wide[...] = jnp.zeros_like(wide)
    for r, a in enumerate((a0, a1, a2, a3)):
        at = pl.multiple_of(((coord + 4 - r) & 3) * PAD, 8)
        shard = a[...].astype(F32)
        for kind, base in ((0, QCOL), (1, 0), (2, HL * DH)):
            for h in range(HL):
                col = h * 3 * DH + kind * DH
                to = base + h * DH
                wide[pl.ds(at, SHARD), to : to + DH] = shard[:, col : col + DH]
    g_ref[...] = wide[...].astype(BF)


def pack(pos, shards):
    whole = pl.BlockSpec((SHARD, 3 * HL * DH), lambda g, p: (0, 0))
    return pl.pallas_call(
        pack_kernel,
        grid_spec=pltpu.PrefetchScalarGridSpec(
            num_scalar_prefetch=1,
            grid=(1,),
            in_specs=[whole] * 4,
            out_specs=pl.BlockSpec((BLK, COLS), lambda g, p: (0, 0)),
            scratch_shapes=[pltpu.VMEM((BLK, COLS), F32)],
        ),
        out_shape=jax.ShapeDtypeStruct((BLK, COLS), BF),
        compiler_params=pltpu.CompilerParams(vmem_limit_bytes=10 * MIB),
        cost_estimate=QUICK,
        name="pack",
    )(pos, *shards)


def spread_kernel(x_ref, o_ref):
    gap = jnp.zeros((PAD - SHARD, x_ref.shape[1]), BF)
    for y in range(4):
        for x in range(4):
            for c in range(2):
                block, slot = (y, x) if c == 0 else (4 + x, y)
                dev = place(y, x, c)
                at = slot * PAD
                o_ref[block, at : at + SHARD, :] = x_ref[dev * SHARD : (dev + 1) * SHARD, :]
                o_ref[block, at + SHARD : at + PAD, :] = gap


def spread(xt):
    n = xt.shape[1]
    blk = 256
    return pl.pallas_call(
        spread_kernel,
        grid=(n // blk,),
        in_specs=[pl.BlockSpec((D, blk), lambda g: (0, g))],
        out_specs=pl.BlockSpec((8, BLK, blk), lambda g: (0, 0, g)),
        out_shape=jax.ShapeDtypeStruct((8, BLK, n), BF),
        compiler_params=pltpu.CompilerParams(vmem_limit_bytes=8 * MIB),
        cost_estimate=QUICK,
        name="spread",
    )(xt)


def product(w, x):
    return lax.dot_general(w, x, (((0,), (0,)), ((), ())), preferred_element_type=F32)


def fetch(pieces, wbuf, sem, first, cols):
    copies = [
        pltpu.make_async_copy(
            piece.at[:, pl.ds(first, cols)], wbuf.at[pl.ds(i * BLK, BLK)], sem.at[i]
        )
        for i, piece in enumerate(pieces)
    ]
    for copy in copies:
        copy.start()
    for copy in copies:
        copy.wait()


def rows_of(x_refs):
    return jnp.concatenate([x[0] for x in x_refs], axis=0)


def x_specs(n):
    return [
        pl.BlockSpec((1, BLK, GROUP), lambda g, b, *_, i=i: (b[i], 0, g)) for i in range(n)
    ]


def part_kernel(count, blocks, *refs):
    pieces, x_refs = refs[:count], refs[count : 2 * count]
    kv_ref, q_ref, wbuf, sem = refs[2 * count :]

    @pl.when(pl.program_id(0) == 0)
    def _():
        fetch(pieces, wbuf, sem, 0, COLS)

    x = rows_of(x_refs)
    kv_ref[...] = product(wbuf[:, : 2 * HL * DH], x)
    q_ref[...] = product(wbuf[:, QCOL : QCOL + HL * DH], x)


def part_call(blocks, pieces, xp):
    count, n = len(pieces), xp.shape[2]
    return pl.pallas_call(
        lambda *refs: part_kernel(count, *refs),
        grid_spec=pltpu.PrefetchScalarGridSpec(
            num_scalar_prefetch=1,
            grid=(n // GROUP,),
            in_specs=[pl.BlockSpec(memory_space=pl.ANY)] * count + x_specs(count),
            out_specs=[
                pl.BlockSpec((2 * HL * DH, GROUP), lambda g, b: (0, g)),
                pl.BlockSpec((HL * DH, GROUP), lambda g, b: (0, g)),
            ],
            scratch_shapes=[
                pltpu.VMEM((count * BLK, COLS), BF),
                pltpu.SemaphoreType.DMA((count,)),
            ],
        ),
        out_shape=[
            jax.ShapeDtypeStruct((2 * HL * DH, n), F32),
            jax.ShapeDtypeStruct((HL * DH, n), F32),
        ],
        compiler_params=pltpu.CompilerParams(vmem_limit_bytes=24 * MIB),
        cost_estimate=QUICK,
        name="part_first",
    )(blocks, *pieces, *([xp] * count))


def more_kernel(count, blocks, *refs):
    pieces, x_refs = refs[:count], refs[count : 2 * count]
    sum_ref, q_ref, wbuf, sem = refs[2 * count :]

    @pl.when(pl.program_id(0) == 0)
    def _():
        fetch(pieces, wbuf, sem, QCOL, COLS - QCOL)

    x = rows_of(x_refs)
    q_ref[...] = product(wbuf[:, : HL * DH], x) + sum_ref[...]


def more_call(blocks, pieces, xp, sums):
    count, n = len(pieces), xp.shape[2]
    spec = pl.BlockSpec((HL * DH, GROUP), lambda g, b: (0, g))
    return pl.pallas_call(
        lambda *refs: more_kernel(count, *refs),
        grid_spec=pltpu.PrefetchScalarGridSpec(
            num_scalar_prefetch=1,
            grid=(n // GROUP,),
            in_specs=[pl.BlockSpec(memory_space=pl.ANY)] * count + x_specs(count) + [spec],
            out_specs=spec,
            scratch_shapes=[
                pltpu.VMEM((count * BLK, COLS - QCOL), BF),
                pltpu.SemaphoreType.DMA((count,)),
            ],
        ),
        out_shape=jax.ShapeDtypeStruct((HL * DH, n), F32),
        compiler_params=pltpu.CompilerParams(vmem_limit_bytes=16 * MIB),
        cost_estimate=QUICK,
        name="part_more",
    )(blocks, *pieces, *([xp] * count), sums)


def feature(raw):
    a = raw.astype(BF).astype(F32)
    return jnp.where(a > 0, a + 1.0, jnp.exp(jnp.minimum(a, 0.0))).astype(BF)


def kv_kernel(count, blocks, *refs):
    pieces, x_refs = refs[:count], refs[count : 2 * count]
    sum_ref, fk_ref, v_ref, pre_ref, tot_ref, wbuf, run, sem = refs[2 * count :]
    g = pl.program_id(0)

    @pl.when(g == 0)
    def _():
        fetch(pieces, wbuf, sem, 0, QCOL)
        run[...] = jnp.zeros_like(run)

    x = rows_of(x_refs)
    half = HL * DH
    fk = feature(product(wbuf[:, :half], x) + sum_ref[:half, :])
    vals = (product(wbuf[:, half : 2 * half], x) + sum_ref[half:, :]).astype(BF)
    tail = (lax.broadcasted_iota(jnp.int32, (VA - DH, GROUP), 0) == 0).astype(F32).astype(BF)
    for h in range(HL):
        kn = fk[h * DH : (h + 1) * DH, :].T
        fk_ref[h] = kn
        va = jnp.concatenate([vals[h * DH : (h + 1) * DH, :], tail], axis=0)
        v_ref[h] = va
        state = jnp.dot(va, kn, preferred_element_type=F32)
        before = run[h]
        pre_ref[0, h] = before
        run[h] = before + state

    @pl.when(g == pl.num_programs(0) - 1)
    def _():
        tot_ref[...] = run[...].astype(BF)


def kv_call(blocks, pieces, xp, sums):
    count, n = len(pieces), xp.shape[2]
    groups = n // GROUP
    return pl.pallas_call(
        lambda *refs: kv_kernel(count, *refs),
        grid_spec=pltpu.PrefetchScalarGridSpec(
            num_scalar_prefetch=1,
            grid=(groups,),
            in_specs=[pl.BlockSpec(memory_space=pl.ANY)] * count
            + x_specs(count)
            + [pl.BlockSpec((2 * HL * DH, GROUP), lambda g, p: (0, g))],
            out_specs=[
                pl.BlockSpec((HL, GROUP, DH), lambda g, p: (0, g, 0)),
                pl.BlockSpec((HL, VA, GROUP), lambda g, p: (0, 0, g)),
                pl.BlockSpec((1, HL, VA, DH), lambda g, p: (g, 0, 0, 0)),
                pl.BlockSpec((HL, VA, DH), lambda g, p: (0, 0, 0)),
            ],
            scratch_shapes=[
                pltpu.VMEM((count * BLK, QCOL), BF),
                pltpu.VMEM((HL, VA, DH), F32),
                pltpu.SemaphoreType.DMA((count,)),
            ],
        ),
        out_shape=[
            jax.ShapeDtypeStruct((HL, n, DH), BF),
            jax.ShapeDtypeStruct((HL, VA, n), BF),
            jax.ShapeDtypeStruct((groups, HL, VA, DH), F32),
            jax.ShapeDtypeStruct((HL, VA, DH), BF),
        ],
        compiler_params=pltpu.CompilerParams(vmem_limit_bytes=24 * MIB),
        cost_estimate=QUICK,
        name="keys_values",
    )(blocks, *pieces, *([xp] * count), sums)


def q_kernel(count, blocks, *refs):
    pieces, x_refs = refs[:count], refs[count : 2 * count]
    sum_ref, fq_ref, wbuf, sem = refs[2 * count :]

    @pl.when(pl.program_id(0) == 0)
    def _():
        fetch(pieces, wbuf, sem, QCOL, COLS - QCOL)

    x = rows_of(x_refs)
    fq_ref[...] = feature(product(wbuf[:, : HL * DH], x) + sum_ref[...])


def q_call(blocks, pieces, xp, sums):
    count, n = len(pieces), xp.shape[2]
    spec = pl.BlockSpec((HL * DH, GROUP), lambda g, p: (0, g))
    return pl.pallas_call(
        lambda *refs: q_kernel(count, *refs),
        grid_spec=pltpu.PrefetchScalarGridSpec(
            num_scalar_prefetch=1,
            grid=(n // GROUP,),
            in_specs=[pl.BlockSpec(memory_space=pl.ANY)] * count + x_specs(count) + [spec],
            out_specs=spec,
            scratch_shapes=[
                pltpu.VMEM((count * BLK, COLS - QCOL), BF),
                pltpu.SemaphoreType.DMA((count,)),
            ],
        ),
        out_shape=jax.ShapeDtypeStruct((HL * DH, n), BF),
        compiler_params=pltpu.CompilerParams(vmem_limit_bytes=16 * MIB),
        cost_estimate=QUICK,
        name="queries",
    )(blocks, *pieces, *([xp] * count), sums)


def mask_rows(code, j0, rows, t0, cols):
    parts = []
    for j in range(j0, j0 + rows // 64):
        t = lax.broadcasted_iota(jnp.int32, (64, cols), 1) + t0
        s = lax.broadcasted_iota(jnp.int32, (64, cols), 0)
        i = t >> 6
        bit = (jnp.full((64, cols), code, jnp.int32) >> (((i * (i - 1)) >> 1) + j)) & 1
        same = jnp.where(s <= (t & 63), 1, 0)
        keep = jnp.where(i > j, bit, jnp.where(i == j, same, 0))
        parts.append(keep.astype(F32).astype(BF))
    return jnp.concatenate(parts, axis=0)


def attend_kernel(codes, fk_ref, v_ref, fq_ref, num_ref):
    code = codes[pl.program_id(0)]
    half = GROUP // 2
    upper = mask_rows(code, 0, half, 0, GROUP)
    lower = mask_rows(code, 4, half, half, half)
    for h in range(HL):
        fq = fq_ref[h * DH : (h + 1) * DH, :]
        top = jnp.dot(fk_ref[h, :half, :], fq, preferred_element_type=F32)
        top = top.astype(BF) * upper
        low = jnp.dot(fk_ref[h, half:, :], fq[:, half:], preferred_element_type=F32)
        low = low.astype(BF) * lower
        num = jnp.dot(v_ref[h, :, :half], top, preferred_element_type=F32)
        more = jnp.dot(v_ref[h, :, half:], low, preferred_element_type=F32)
        num_ref[h, :, :half] = num[:, :half]
        num_ref[h, :, half:] = num[:, half:] + more


def attend_call(codes, fk, v, fq):
    n = fq.shape[1]
    return pl.pallas_call(
        attend_kernel,
        grid_spec=pltpu.PrefetchScalarGridSpec(
            num_scalar_prefetch=1,
            grid=(n // GROUP,),
            in_specs=[
                pl.BlockSpec((HL, GROUP, DH), lambda g, m: (0, g, 0)),
                pl.BlockSpec((HL, VA, GROUP), lambda g, m: (0, 0, g)),
                pl.BlockSpec((HL * DH, GROUP), lambda g, m: (0, g)),
            ],
            out_specs=pl.BlockSpec((HL, VA, GROUP), lambda g, m: (0, 0, g)),
        ),
        out_shape=jax.ShapeDtypeStruct((HL, VA, n), F32),
        compiler_params=pltpu.CompilerParams(vmem_limit_bytes=12 * MIB),
        cost_estimate=QUICK,
        name="attend",
    )(codes, fk, v, fq)


def join_kernel(scale, dev_ref, pre_ref, fq_ref, num_ref, out_ref, sq_ref):
    total = jnp.zeros((1, GROUP), F32)
    for h in range(HL):
        prefix = (dev_ref[h] + pre_ref[0, h]).astype(BF)
        fq = fq_ref[h * DH : (h + 1) * DH, :]
        num = num_ref[h] + jnp.dot(prefix, fq, preferred_element_type=F32)
        out = num[:DH, :] * (scale[h] / num[DH : DH + 1, :])
        out_ref[h * DH : (h + 1) * DH, :] = out
        total = total + jnp.sum(out * out, axis=0, keepdims=True)
    sq_ref[...] = total


def join_call(scale, dev, pre, fq, num):
    n = fq.shape[1]
    groups = n // GROUP
    return pl.pallas_call(
        join_kernel,
        grid_spec=pltpu.PrefetchScalarGridSpec(
            num_scalar_prefetch=1,
            grid=(groups,),
            in_specs=[
                pl.BlockSpec((HL, VA, DH), lambda g, s: (0, 0, 0)),
                pl.BlockSpec((1, HL, VA, DH), lambda g, s: (g, 0, 0, 0)),
                pl.BlockSpec((HL * DH, GROUP), lambda g, s: (0, g)),
                pl.BlockSpec((HL, VA, GROUP), lambda g, s: (0, 0, g)),
            ],
            out_specs=[
                pl.BlockSpec((HL * DH, GROUP), lambda g, s: (0, g)),
                pl.BlockSpec((1, GROUP), lambda g, s: (0, g)),
            ],
        ),
        out_shape=[
            jax.ShapeDtypeStruct((HL * DH, n), F32),
            jax.ShapeDtypeStruct((1, n), F32),
        ],
        compiler_params=pltpu.CompilerParams(vmem_limit_bytes=14 * MIB),
        cost_estimate=QUICK,
        name="join",
    )(scale, dev, pre, fq, num)


def norm_kernel(out_ref, sq_ref, gain_ref, o_ref):
    inv = lax.rsqrt(sq_ref[...] * (1.0 / (H * DH)) + 1e-06)
    o_ref[...] = (out_ref[...] * inv * gain_ref[...]).astype(BF)


def norm_call(out, squares, gain):
    n = out.shape[1]
    return pl.pallas_call(
        norm_kernel,
        grid=(n // GROUP,),
        in_specs=[
            pl.BlockSpec((HL * DH, GROUP), lambda g: (0, g)),
            pl.BlockSpec((1, GROUP), lambda g: (0, g)),
            pl.BlockSpec((HL * DH, 1), lambda g: (0, 0)),
        ],
        out_specs=pl.BlockSpec((HL * DH, GROUP), lambda g: (0, g)),
        out_shape=jax.ShapeDtypeStruct((HL * DH, n), BF),
        compiler_params=pltpu.CompilerParams(vmem_limit_bytes=10 * MIB),
        cost_estimate=QUICK,
        name="norm",
    )(out, squares, gain)


def body(tokens, qkv_weight, block_mask, head_scale, norm_gain):
    me = lax.axis_index("tm").astype(jnp.int32)
    y, x, core = me // 8, (me // 2) % 4, me % 2
    pos = jnp.stack([y, x, core])
    shards = [qkv_weight] + [shift(qkv_weight, first_leg(d)) for d in (1, 2, 3)]
    near = pack(pos, shards)
    near, xt = lax.optimization_barrier((near, tokens.T))
    own = [near] + [shift(near, second_leg(d)) for d in (1, 2, 3)]
    sib = [shift(near, SIBLING)]
    xp = spread(xt)

    def block(mine, d):
        which = core if mine else 1 - core
        return which * 4 + (jnp.where(which == 0, y, x) + 4 - d) % 4

    def blocks(which):
        return jnp.stack([block(mine, d) for mine, d in which])

    def pieces(which):
        return [(own if mine else sib)[d] for mine, d in which]

    first = [(True, 0), (False, 0)]
    mine = [(True, d) for d in (1, 2, 3)]
    last = [(False, d) for d in (1, 2, 3)]
    kv_sum, q_sum = part_call(blocks(first), pieces(first), xp)
    *own, q_sum = lax.optimization_barrier((*own, q_sum))
    sib += [shift(a, SIBLING) for a in own[1:]]
    q_sum = more_call(blocks(mine), pieces(mine), xp, q_sum)
    sib[1], q_sum = lax.optimization_barrier((sib[1], q_sum))
    fk, v, pre, tot = kv_call(blocks(mine + last), pieces(mine + last), xp, kv_sum)

    other = shift(tot, SIBLING).astype(F32)
    before = jnp.where(core == 1, other, 0.0)
    chip = (tot.astype(F32) + other).astype(BF)
    chip, q_sum = lax.optimization_barrier((chip, q_sum))
    fq = q_call(blocks(last), pieces(last), xp, q_sum)
    row = chip.astype(F32)
    for d in (1, 2, 3):
        got = shift(chip, along_x(d)).astype(F32)
        row = row + got
        before = before + jnp.where(x >= d, got, 0.0)
    row, fq = lax.optimization_barrier((row.astype(BF), fq))
    num = attend_call(block_mask, fk, v, fq)
    for d in (1, 2, 3):
        before = before + shift(row, later_y(d)).astype(F32)

    out, squares = join_call(head_scale, before, pre, fq, num)
    squares = squares + sum(
        lax.ppermute(squares, "head", [(i, (i + d) % 4) for i in range(4)]) for d in (1, 2, 3)
    )
    return norm_call(out, squares, norm_gain.reshape(HL * DH, 1)).T


def solution(mesh):
    in_specs = (P("tm", None), P("tm", "head"), P("tm"), P("head"), P("head"))
    out_specs = P("tm", "head")
    return jax.shard_map(body, mesh=mesh, in_specs=in_specs, out_specs=out_specs, check_vma=False)
```

```python
import functools

import jax
import jax.numpy as jnp
from jax import lax
from jax.experimental import pallas as pl
from jax.experimental.pallas import tpu as pltpu
from jax.sharding import PartitionSpec as P

H = 20
DH = 112
GROUP = 512
D = 2240
HL = 5
SHARD = 70
PAD = 72
BLK = 4 * PAD
VA = 128
QCOL = 1152
COLS = 1792
BF = jnp.bfloat16
F32 = jnp.float32
MIB = 1 << 20
QUICK = pl.CostEstimate(flops=1, bytes_accessed=1, transcendentals=0)


def place(y, x, c):
    return (y % 4) * 8 + (x % 4) * 2 + c


def perm(move):
    return [
        (place(y, x, c), place(*move(y, x, c)))
        for y in range(4)
        for x in range(4)
        for c in range(2)
    ]


SIBLING = perm(lambda y, x, c: (y, x, 1 - c))


def first_leg(d):
    return perm(lambda y, x, c: (y, x + d, c) if c == 0 else (y + d, x, c))


def second_leg(d):
    return perm(lambda y, x, c: (y + d, x, c) if c == 0 else (y, x + d, c))


def along_x(d):
    return perm(lambda y, x, c: (y, x + d, c))


def later_y(d):
    return [
        (place(y, x, c), place(y + d, x, c))
        for y in range(4 - d)
        for x in range(4)
        for c in range(2)
    ]


def shift(a, moves):
    return lax.ppermute(a, "tm", moves)


def pack_kernel(pos, a0, a1, a2, a3, g_ref, wide):
    coord = jnp.where(pos[2] == 0, pos[1], pos[0])
    wide[...] = jnp.zeros_like(wide)
    for r, a in enumerate((a0, a1, a2, a3)):
        at = pl.multiple_of(((coord + 4 - r) & 3) * PAD, 8)
        shard = a[...].astype(F32)
        for kind, base in ((0, QCOL), (1, 0), (2, HL * DH)):
            for h in range(HL):
                col = h * 3 * DH + kind * DH
                to = base + h * DH
                wide[pl.ds(at, SHARD), to : to + DH] = shard[:, col : col + DH]
    g_ref[...] = wide[...].astype(BF)


def pack(pos, shards):
    whole = pl.BlockSpec((SHARD, 3 * HL * DH), lambda g, p: (0, 0))
    return pl.pallas_call(
        pack_kernel,
        grid_spec=pltpu.PrefetchScalarGridSpec(
            num_scalar_prefetch=1,
            grid=(1,),
            in_specs=[whole] * 4,
            out_specs=pl.BlockSpec((BLK, COLS), lambda g, p: (0, 0)),
            scratch_shapes=[pltpu.VMEM((BLK, COLS), F32)],
        ),
        out_shape=jax.ShapeDtypeStruct((BLK, COLS), BF),
        compiler_params=pltpu.CompilerParams(vmem_limit_bytes=10 * MIB),
        cost_estimate=QUICK,
        name="pack",
    )(pos, *shards)


def spread_kernel(x_ref, o_ref):
    gap = jnp.zeros((PAD - SHARD, x_ref.shape[1]), BF)
    for y in range(4):
        for x in range(4):
            for c in range(2):
                block, slot = (y, x) if c == 0 else (4 + x, y)
                dev = place(y, x, c)
                at = slot * PAD
                o_ref[block, at : at + SHARD, :] = x_ref[dev * SHARD : (dev + 1) * SHARD, :]
                o_ref[block, at + SHARD : at + PAD, :] = gap


def spread(xt):
    n = xt.shape[1]
    blk = 256
    return pl.pallas_call(
        spread_kernel,
        grid=(n // blk,),
        in_specs=[pl.BlockSpec((D, blk), lambda g: (0, g))],
        out_specs=pl.BlockSpec((8, BLK, blk), lambda g: (0, 0, g)),
        out_shape=jax.ShapeDtypeStruct((8, BLK, n), BF),
        compiler_params=pltpu.CompilerParams(vmem_limit_bytes=8 * MIB),
        cost_estimate=QUICK,
        name="spread",
    )(xt)


def product(w, x):
    return lax.dot_general(w, x, (((0,), (0,)), ((), ())), preferred_element_type=F32)


def fast(a):
    return pltpu.with_memory_space_constraint(a, pltpu.VMEM)


def lay(pieces, wbuf, first, cols):
    for i, piece in enumerate(pieces):
        wbuf[i * BLK : (i + 1) * BLK, :] = piece[:, first : first + cols]


def block(pos, mine, d):
    which = pos[2] if mine else 1 - pos[2]
    return which * 4 + ((jnp.where(which == 0, pos[0], pos[1]) + 4 - d) & 3)


def rows_of(pos, steps, x_ref, at):
    return jnp.concatenate([x_ref[block(pos, *step), :, at] for step in steps], axis=0)


def each_group(n, step):
    def run(g, carry):
        step(g, pl.ds(pl.multiple_of(g * GROUP, GROUP), GROUP))
        return carry

    lax.fori_loop(0, n // GROUP, run, 0)


def resident(kernel, small, large, outs, scratch, limit, name, alias=None):
    return pl.pallas_call(
        kernel,
        in_specs=[pl.BlockSpec(memory_space=pltpu.SMEM)] * len(small)
        + [pl.BlockSpec(memory_space=pltpu.VMEM)] * len(large),
        out_specs=[pl.BlockSpec(memory_space=pltpu.VMEM)] * len(outs),
        out_shape=[pltpu.VMEM(shape, kind) for shape, kind in outs],
        scratch_shapes=scratch,
        input_output_aliases=alias or {},
        compiler_params=pltpu.CompilerParams(vmem_limit_bytes=limit * MIB),
        cost_estimate=QUICK,
        name=name,
    )(*small, *(fast(a) for a in large))


def part_kernel(steps, pos, *refs):
    count = len(refs) - 4
    pieces, (x_ref, kv_ref, q_ref, wbuf) = refs[:count], refs[count:]
    lay(pieces, wbuf, 0, COLS)

    def step(g, at):
        x = rows_of(pos, steps, x_ref, at)
        kv_ref[:, at] = product(wbuf[:, : 2 * HL * DH], x)
        q_ref[:, at] = product(wbuf[:, QCOL : QCOL + HL * DH], x)

    each_group(x_ref.shape[2], step)


def part_call(steps, pos, pieces, xp):
    n = xp.shape[2]
    return resident(
        functools.partial(part_kernel, steps),
        [pos],
        [*pieces, xp],
        [((2 * HL * DH, n), F32), ((HL * DH, n), F32)],
        [pltpu.VMEM((len(pieces) * BLK, COLS), BF)],
        16,
        "part_first",
    )


def more_kernel(steps, pos, *refs):
    count = len(refs) - 4
    pieces, (x_ref, sum_ref, q_ref, wbuf) = refs[:count], refs[count:]
    lay(pieces, wbuf, QCOL, COLS - QCOL)

    def step(g, at):
        x = rows_of(pos, steps, x_ref, at)
        q_ref[:, at] = product(wbuf[:, : HL * DH], x) + sum_ref[:, at]

    each_group(x_ref.shape[2], step)


def more_call(steps, pos, pieces, xp, sums):
    (out,) = resident(
        functools.partial(more_kernel, steps),
        [pos],
        [*pieces, xp, sums],
        [(sums.shape, F32)],
        [pltpu.VMEM((len(pieces) * BLK, COLS - QCOL), BF)],
        12,
        "part_more",
        {len(pieces) + 2: 0},
    )
    return out


def feature(raw):
    a = raw.astype(BF).astype(F32)
    return jnp.where(a > 0, a + 1.0, jnp.exp(jnp.minimum(a, 0.0))).astype(BF)


def kv_kernel(steps, pos, *refs):
    count = len(refs) - 8
    pieces = refs[:count]
    x_ref, sum_ref, fk_ref, v_ref, pre_ref, tot_ref, wbuf, run = refs[count:]
    lay(pieces, wbuf, 0, QCOL)
    run[...] = jnp.zeros_like(run)
    half = HL * DH

    def step(g, at):
        x = rows_of(pos, steps, x_ref, at)
        raw = product(wbuf[:, : 2 * half], x) + sum_ref[:, at]
        fk = feature(raw[:half, :])
        tail = (lax.broadcasted_iota(jnp.int32, (VA - DH, GROUP), 0) == 0).astype(F32).astype(BF)
        for h in range(HL):
            kn = fk[h * DH : (h + 1) * DH, :].T
            fk_ref[h, at, :] = kn
            val = raw[half + h * DH : half + (h + 1) * DH, :].astype(BF)
            va = jnp.concatenate([val, tail], axis=0)
            v_ref[h, :, at] = va
            state = jnp.dot(va, kn, preferred_element_type=F32)
            before = run[h]
            pre_ref[g, h] = before
            run[h] = before + state

    each_group(x_ref.shape[2], step)
    tot_ref[...] = run[...].astype(BF)


def kv_call(steps, pos, pieces, xp, sums):
    n = xp.shape[2]
    return resident(
        functools.partial(kv_kernel, steps),
        [pos],
        [*pieces, xp, sums],
        [
            ((HL, n, DH), BF),
            ((HL, VA, n), BF),
            ((n // GROUP, HL, VA, DH), F32),
            ((HL, VA, DH), BF),
        ],
        [pltpu.VMEM((len(pieces) * BLK, QCOL), BF), pltpu.VMEM((HL, VA, DH), F32)],
        20,
        "keys_values",
    )


def q_kernel(steps, pos, *refs):
    count = len(refs) - 4
    pieces, (x_ref, sum_ref, fq_ref, wbuf) = refs[:count], refs[count:]
    lay(pieces, wbuf, QCOL, COLS - QCOL)

    def step(g, at):
        x = rows_of(pos, steps, x_ref, at)
        fq_ref[:, at] = feature(product(wbuf[:, : HL * DH], x) + sum_ref[:, at])

    each_group(x_ref.shape[2], step)


def q_call(steps, pos, pieces, xp, sums):
    (out,) = resident(
        functools.partial(q_kernel, steps),
        [pos],
        [*pieces, xp, sums],
        [(sums.shape, BF)],
        [pltpu.VMEM((len(pieces) * BLK, COLS - QCOL), BF)],
        12,
        "queries",
    )
    return out


def mask_rows(code, j0, rows, t0, cols):
    parts = []
    for j in range(j0, j0 + rows // 64):
        t = lax.broadcasted_iota(jnp.int32, (64, cols), 1) + t0
        s = lax.broadcasted_iota(jnp.int32, (64, cols), 0)
        i = t >> 6
        bit = (jnp.full((64, cols), code, jnp.int32) >> (((i * (i - 1)) >> 1) + j)) & 1
        same = jnp.where(s <= (t & 63), 1, 0)
        keep = jnp.where(i > j, bit, jnp.where(i == j, same, 0))
        parts.append(keep.astype(F32).astype(BF))
    return jnp.concatenate(parts, axis=0)


def attend_kernel(codes, fk_ref, v_ref, fq_ref, num_ref):
    half = GROUP // 2

    def step(g, at):
        code = codes[g]
        start = pl.multiple_of(g * GROUP, GROUP)
        one, two = pl.ds(start, half), pl.ds(start + half, half)
        upper = mask_rows(code, 0, half, 0, GROUP)
        lower = mask_rows(code, 4, half, half, half)
        for h in range(HL):
            fq = fq_ref[h * DH : (h + 1) * DH, at]
            top = jnp.dot(fk_ref[h, one, :], fq, preferred_element_type=F32)
            top = top.astype(BF) * upper
            low = jnp.dot(fk_ref[h, two, :], fq[:, half:], preferred_element_type=F32)
            low = low.astype(BF) * lower
            num = jnp.dot(v_ref[h, :, one], top, preferred_element_type=F32)
            more = jnp.dot(v_ref[h, :, two], low, preferred_element_type=F32)
            num_ref[h, :, one] = num[:, :half]
            num_ref[h, :, two] = num[:, half:] + more

    each_group(fq_ref.shape[1], step)


def attend_call(codes, fk, v, fq):
    (out,) = resident(
        attend_kernel,
        [codes],
        [fk, v, fq],
        [((HL, VA, fq.shape[1]), F32)],
        [],
        12,
        "attend",
    )
    return out


def chip_kernel(tot_ref, other_ref, chip_ref):
    chip_ref[...] = (tot_ref[...].astype(F32) + other_ref[...].astype(F32)).astype(BF)


def row_kernel(a, b, c, d, row_ref):
    total = a[...].astype(F32) + b[...].astype(F32) + c[...].astype(F32) + d[...].astype(F32)
    row_ref[...] = total.astype(BF)


def small(kernel, args, name):
    (out,) = resident(kernel, [], args, [(args[0].shape, BF)], [], 4, name)
    return out


def join_kernel(pos, scale, *refs):
    other, near, far = refs[0], refs[1:4], refs[4:7]
    pre_ref, fq_ref, num_ref, out_ref, sq_ref, dev = refs[7:]
    total = far[0][...].astype(F32) + far[1][...].astype(F32) + far[2][...].astype(F32)
    total = total + jnp.where(pos[2] == 1, other[...].astype(F32), 0.0)
    for d, got in enumerate(near):
        total = total + jnp.where(pos[1] >= d + 1, got[...].astype(F32), 0.0)
    dev[...] = total

    def step(g, at):
        squares = jnp.zeros((1, GROUP), F32)
        for h in range(HL):
            prefix = (dev[h] + pre_ref[g, h]).astype(BF)
            fq = fq_ref[h * DH : (h + 1) * DH, at]
            num = num_ref[h, :, at] + jnp.dot(prefix, fq, preferred_element_type=F32)
            out = num[:DH, :] * (scale[h] / num[DH : DH + 1, :])
            out_ref[h * DH : (h + 1) * DH, at] = out
            squares = squares + jnp.sum(out * out, axis=0, keepdims=True)
        sq_ref[:, at] = squares

    each_group(fq_ref.shape[1], step)


def join_call(pos, scale, states, pre, fq, num):
    n = fq.shape[1]
    return resident(
        join_kernel,
        [pos, scale],
        [*states, pre, fq, num],
        [((HL * DH, n), F32), ((1, n), F32)],
        [pltpu.VMEM((HL, VA, DH), F32)],
        12,
        "join",
    )


def norm_kernel(out_ref, s0, s1, s2, s3, gain_ref, o_ref, buf, sem):
    eye = lax.broadcasted_iota(jnp.int32, (DH, DH), 0) == lax.broadcasted_iota(
        jnp.int32, (DH, DH), 1
    )
    gains = [
        jnp.sum(jnp.where(eye, gain_ref[h : h + 1, :], 0.0), axis=1, keepdims=True)
        for h in range(HL)
    ]
    copies = []
    for g in range(out_ref.shape[1] // GROUP):
        at = slice(g * GROUP, (g + 1) * GROUP)
        squares = s0[:, at] + s1[:, at] + s2[:, at] + s3[:, at]
        inv = lax.rsqrt(squares * (1.0 / (H * DH)) + 1e-06)
        for h in range(HL):
            rows = slice(h * DH, (h + 1) * DH)
            buf[rows, at] = (out_ref[rows, at] * inv * gains[h]).astype(BF)
        here = pl.ds(g * GROUP, GROUP)
        copies.append(pltpu.make_async_copy(buf.at[:, here], o_ref.at[:, here], sem.at[g]))
        copies[-1].start()
    for copy in copies:
        copy.wait()


def norm_call(out, squares, gain):
    n = out.shape[1]
    return pl.pallas_call(
        norm_kernel,
        in_specs=[pl.BlockSpec(memory_space=pltpu.VMEM)] * 6,
        out_specs=pl.BlockSpec(memory_space=pl.ANY),
        out_shape=jax.ShapeDtypeStruct((HL * DH, n), BF),
        scratch_shapes=[
            pltpu.VMEM((HL * DH, n), BF),
            pltpu.SemaphoreType.DMA((n // GROUP,)),
        ],
        compiler_params=pltpu.CompilerParams(vmem_limit_bytes=8 * MIB),
        cost_estimate=QUICK,
        name="norm",
    )(fast(out), *(fast(a) for a in squares), fast(gain))


def body(tokens, qkv_weight, block_mask, head_scale, norm_gain):
    me = lax.axis_index("tm").astype(jnp.int32)
    y, x, core = me // 8, (me // 2) % 4, me % 2
    pos = jnp.stack([y, x, core])
    pos, gain = lax.optimization_barrier((pos, norm_gain.reshape(HL, DH)))
    shards = [qkv_weight] + [shift(qkv_weight, first_leg(d)) for d in (1, 2, 3)]
    near = pack(pos, shards)
    near, xt = lax.optimization_barrier((near, tokens.T))
    own = [near] + [shift(near, second_leg(d)) for d in (1, 2, 3)]
    sib = [shift(near, SIBLING)]
    xp = spread(pltpu.with_memory_space_constraint(xt, pltpu.HBM))

    def pieces(steps):
        return [(own if mine else sib)[d] for mine, d in steps]

    first = [(True, 0), (False, 0)]
    mine = [(True, d) for d in (1, 2, 3)]
    last = [(False, d) for d in (1, 2, 3)]
    kv_sum, q_sum = part_call(first, pos, pieces(first), xp)
    *own, q_sum = lax.optimization_barrier((*own, q_sum))
    sib += [shift(a, SIBLING) for a in own[1:]]
    q_sum = more_call(mine, pos, pieces(mine), xp, q_sum)
    sib[1], q_sum = lax.optimization_barrier((sib[1], q_sum))
    fk, v, pre, tot = kv_call(mine + last, pos, pieces(mine + last), xp, kv_sum)

    other = shift(tot, SIBLING)
    chip = small(chip_kernel, [tot, other], "chip")
    chip, q_sum = lax.optimization_barrier((chip, q_sum))
    fq = q_call(last, pos, pieces(last), xp, q_sum)
    in_row = [shift(chip, along_x(d)) for d in (1, 2, 3)]
    row = small(row_kernel, [chip, *in_row], "row")
    row, fq = lax.optimization_barrier((row, fq))
    num = attend_call(block_mask, fk, v, fq)
    above = [shift(row, later_y(d)) for d in (1, 2, 3)]

    out, squares = join_call(pos, head_scale, [other, *in_row, *above], pre, fq, num)
    squares = [squares] + [
        lax.ppermute(squares, "head", [(i, (i + d) % 4) for i in range(4)]) for d in (1, 2, 3)
    ]
    return norm_call(out, squares, gain).T


def solution(mesh):
    in_specs = (P("tm", None), P("tm", "head"), P("tm"), P("head"), P("head"))
    out_specs = P("tm", "head")
    return jax.shard_map(body, mesh=mesh, in_specs=in_specs, out_specs=out_specs, check_vma=False)
```

```python
import functools

import jax
import jax.numpy as jnp
from jax import lax
from jax.experimental import pallas as pl
from jax.experimental.pallas import tpu as pltpu
from jax.sharding import PartitionSpec as P

H = 20
DH = 112
GROUP = 512
D = 2240
HL = 5
SHARD = 70
PAD = 72
BLK = 4 * PAD
VA = 128
QCOL = 1152
COLS = 1792
BF = jnp.bfloat16
F32 = jnp.float32
MIB = 1 << 20
QUICK = pl.CostEstimate(flops=1, bytes_accessed=1, transcendentals=0)


def place(y, x, c):
    return (y % 4) * 8 + (x % 4) * 2 + c


def perm(move):
    return [
        (place(y, x, c), place(*move(y, x, c)))
        for y in range(4)
        for x in range(4)
        for c in range(2)
    ]


SIBLING = perm(lambda y, x, c: (y, x, 1 - c))


def first_leg(d):
    return perm(lambda y, x, c: (y, x + d, c) if c == 0 else (y + d, x, c))


def second_leg(d):
    return perm(lambda y, x, c: (y + d, x, c) if c == 0 else (y, x + d, c))


def along_x(d):
    return perm(lambda y, x, c: (y, x + d, c))


def later_y(d):
    return [
        (place(y, x, c), place(y + d, x, c))
        for y in range(4 - d)
        for x in range(4)
        for c in range(2)
    ]


def shift(a, moves):
    return lax.ppermute(a, "tm", moves)


def pack_kernel(pos, a0, a1, a2, a3, kv_ref, q_ref, wide):
    coord = jnp.where(pos[2] == 0, pos[1], pos[0])
    wide[...] = jnp.zeros_like(wide)
    for r, a in enumerate((a0, a1, a2, a3)):
        at = pl.multiple_of(((coord + 4 - r) & 3) * PAD, 8)
        shard = a[...].astype(F32)
        for kind, base in ((0, QCOL), (1, 0), (2, HL * DH)):
            for h in range(HL):
                col = h * 3 * DH + kind * DH
                to = base + h * DH
                wide[pl.ds(at, SHARD), to : to + DH] = shard[:, col : col + DH]
    kv_ref[...] = wide[:, :QCOL].astype(BF)
    q_ref[...] = wide[:, QCOL:].astype(BF)


def pack(pos, shards):
    return resident(
        pack_kernel,
        [pos],
        shards,
        [((BLK, QCOL), BF), ((BLK, COLS - QCOL), BF)],
        [pltpu.VMEM((BLK, COLS), F32)],
        10,
        "pack",
    )


def spread_kernel(x_ref, o_ref):
    gap = jnp.zeros((PAD - SHARD, x_ref.shape[1]), BF)
    for y in range(4):
        for x in range(4):
            for c in range(2):
                block, slot = (y, x) if c == 0 else (4 + x, y)
                dev = place(y, x, c)
                at = slot * PAD
                o_ref[block, at : at + SHARD, :] = x_ref[dev * SHARD : (dev + 1) * SHARD, :]
                o_ref[block, at + SHARD : at + PAD, :] = gap


def spread(xt):
    n = xt.shape[1]
    blk = 256
    return pl.pallas_call(
        spread_kernel,
        grid=(n // blk,),
        in_specs=[pl.BlockSpec((D, blk), lambda g: (0, g))],
        out_specs=pl.BlockSpec((8, BLK, blk), lambda g: (0, 0, g)),
        out_shape=jax.ShapeDtypeStruct((8, BLK, n), BF),
        compiler_params=pltpu.CompilerParams(vmem_limit_bytes=8 * MIB),
        cost_estimate=QUICK,
        name="spread",
    )(xt)


def product(w, x):
    return lax.dot_general(w, x, (((0,), (0,)), ((), ())), preferred_element_type=F32)


def fast(a):
    return pltpu.with_memory_space_constraint(a, pltpu.VMEM)


def lay(pieces, wbuf):
    for i, piece in enumerate(pieces):
        wbuf[i * BLK : (i + 1) * BLK, :] = piece[...]


def block(pos, mine, d):
    which = pos[2] if mine else 1 - pos[2]
    return which * 4 + ((jnp.where(which == 0, pos[0], pos[1]) + 4 - d) & 3)


def rows_of(pos, steps, x_ref, at):
    return jnp.concatenate([x_ref[block(pos, *step), :, at] for step in steps], axis=0)


def each_group(n, step):
    def run(g, carry):
        step(g, pl.ds(pl.multiple_of(g * GROUP, GROUP), GROUP))
        return carry

    lax.fori_loop(0, n // GROUP, run, 0)


def resident(kernel, small, large, outs, scratch, limit, name, alias=None):
    return pl.pallas_call(
        kernel,
        in_specs=[pl.BlockSpec(memory_space=pltpu.SMEM)] * len(small)
        + [pl.BlockSpec(memory_space=pltpu.VMEM)] * len(large),
        out_specs=[pl.BlockSpec(memory_space=pltpu.VMEM)] * len(outs),
        out_shape=[pltpu.VMEM(shape, kind) for shape, kind in outs],
        scratch_shapes=scratch,
        input_output_aliases=alias or {},
        compiler_params=pltpu.CompilerParams(vmem_limit_bytes=limit * MIB),
        cost_estimate=QUICK,
        name=name,
    )(*small, *(fast(a) for a in large))


def part_kernel(steps, pos, *refs):
    count = len(steps)
    kv_pieces, q_pieces = refs[:count], refs[count : 2 * count]
    x_ref, kv_ref, q_ref, kv_buf, q_buf = refs[2 * count :]
    lay(kv_pieces, kv_buf)
    lay(q_pieces, q_buf)

    def step(g, at):
        x = rows_of(pos, steps, x_ref, at)
        kv_ref[:, at] = product(kv_buf[:, : 2 * HL * DH], x)
        q_ref[:, at] = product(q_buf[:, : HL * DH], x)

    each_group(x_ref.shape[2], step)


def part_call(steps, pos, kv_pieces, q_pieces, xp):
    n = xp.shape[2]
    return resident(
        functools.partial(part_kernel, steps),
        [pos],
        [*kv_pieces, *q_pieces, xp],
        [((2 * HL * DH, n), F32), ((HL * DH, n), F32)],
        [
            pltpu.VMEM((len(steps) * BLK, QCOL), BF),
            pltpu.VMEM((len(steps) * BLK, COLS - QCOL), BF),
        ],
        16,
        "part_first",
    )


def feature(raw):
    a = raw.astype(BF).astype(F32)
    return jnp.where(a > 0, a + 1.0, jnp.exp(jnp.minimum(a, 0.0))).astype(BF)


def kv_kernel(steps, pos, *refs):
    count = len(refs) - 8
    pieces = refs[:count]
    x_ref, sum_ref, fk_ref, v_ref, pre_ref, tot_ref, wbuf, run = refs[count:]
    lay(pieces, wbuf)
    run[...] = jnp.zeros_like(run)
    half = HL * DH

    def step(g, at):
        x = rows_of(pos, steps, x_ref, at)
        raw = product(wbuf[:, : 2 * half], x) + sum_ref[:, at]
        fk = feature(raw[:half, :])
        tail = (lax.broadcasted_iota(jnp.int32, (VA - DH, GROUP), 0) == 0).astype(F32).astype(BF)
        for h in range(HL):
            kn = fk[h * DH : (h + 1) * DH, :].T
            fk_ref[h, at, :] = kn
            val = raw[half + h * DH : half + (h + 1) * DH, :].astype(BF)
            va = jnp.concatenate([val, tail], axis=0)
            v_ref[h, :, at] = va
            state = jnp.dot(va, kn, preferred_element_type=F32)
            before = run[h]
            pre_ref[g, h] = before
            run[h] = before + state

    each_group(x_ref.shape[2], step)
    tot_ref[...] = run[...].astype(BF)


def kv_call(steps, pos, pieces, xp, sums):
    n = xp.shape[2]
    return resident(
        functools.partial(kv_kernel, steps),
        [pos],
        [*pieces, xp, sums],
        [
            ((HL, n, DH), BF),
            ((HL, VA, n), BF),
            ((n // GROUP, HL, VA, DH), F32),
            ((HL, VA, DH), BF),
        ],
        [pltpu.VMEM((len(pieces) * BLK, QCOL), BF), pltpu.VMEM((HL, VA, DH), F32)],
        20,
        "keys_values",
    )


def q_kernel(steps, pos, *refs):
    count = len(refs) - 4
    pieces, (x_ref, sum_ref, fq_ref, wbuf) = refs[:count], refs[count:]
    lay(pieces, wbuf)

    def step(g, at):
        x = rows_of(pos, steps, x_ref, at)
        fq_ref[:, at] = feature(product(wbuf[:, : HL * DH], x) + sum_ref[:, at])

    each_group(x_ref.shape[2], step)


def q_call(steps, pos, pieces, xp, sums):
    (out,) = resident(
        functools.partial(q_kernel, steps),
        [pos],
        [*pieces, xp, sums],
        [(sums.shape, BF)],
        [pltpu.VMEM((len(pieces) * BLK, COLS - QCOL), BF)],
        12,
        "queries",
    )
    return out


def mask_rows(code, j0, rows, t0, cols):
    parts = []
    for j in range(j0, j0 + rows // 64):
        t = lax.broadcasted_iota(jnp.int32, (64, cols), 1) + t0
        s = lax.broadcasted_iota(jnp.int32, (64, cols), 0)
        i = t >> 6
        bit = (jnp.full((64, cols), code, jnp.int32) >> (((i * (i - 1)) >> 1) + j)) & 1
        same = jnp.where(s <= (t & 63), 1, 0)
        keep = jnp.where(i > j, bit, jnp.where(i == j, same, 0))
        parts.append(keep.astype(F32).astype(BF))
    return jnp.concatenate(parts, axis=0)


def attend_kernel(codes, fk_ref, v_ref, fq_ref, num_ref):
    half = GROUP // 2

    def step(g, at):
        code = codes[g]
        start = pl.multiple_of(g * GROUP, GROUP)
        one, two = pl.ds(start, half), pl.ds(start + half, half)
        upper = mask_rows(code, 0, half, 0, GROUP)
        lower = mask_rows(code, 4, half, half, half)
        for h in range(HL):
            fq = fq_ref[h * DH : (h + 1) * DH, at]
            top = jnp.dot(fk_ref[h, one, :], fq, preferred_element_type=F32)
            top = top.astype(BF) * upper
            low = jnp.dot(fk_ref[h, two, :], fq[:, half:], preferred_element_type=F32)
            low = low.astype(BF) * lower
            num = jnp.dot(v_ref[h, :, one], top, preferred_element_type=F32)
            more = jnp.dot(v_ref[h, :, two], low, preferred_element_type=F32)
            num_ref[h, :, one] = num[:, :half]
            num_ref[h, :, two] = num[:, half:] + more

    each_group(fq_ref.shape[1], step)


def attend_call(codes, fk, v, fq):
    (out,) = resident(
        attend_kernel,
        [codes],
        [fk, v, fq],
        [((HL, VA, fq.shape[1]), F32)],
        [],
        12,
        "attend",
    )
    return out


def chip_kernel(tot_ref, other_ref, chip_ref):
    chip_ref[...] = (tot_ref[...].astype(F32) + other_ref[...].astype(F32)).astype(BF)


def row_kernel(a, b, c, d, row_ref):
    total = a[...].astype(F32) + b[...].astype(F32) + c[...].astype(F32) + d[...].astype(F32)
    row_ref[...] = total.astype(BF)


def small(kernel, args, name):
    (out,) = resident(kernel, [], args, [(args[0].shape, BF)], [], 4, name)
    return out


def join_kernel(pos, scale, *refs):
    other, near, far = refs[0], refs[1:4], refs[4:7]
    pre_ref, fq_ref, num_ref, out_ref, sq_ref, dev = refs[7:]
    total = far[0][...].astype(F32) + far[1][...].astype(F32) + far[2][...].astype(F32)
    total = total + jnp.where(pos[2] == 1, other[...].astype(F32), 0.0)
    for d, got in enumerate(near):
        total = total + jnp.where(pos[1] >= d + 1, got[...].astype(F32), 0.0)
    dev[...] = total

    def step(g, at):
        squares = jnp.zeros((1, GROUP), F32)
        for h in range(HL):
            prefix = (dev[h] + pre_ref[g, h]).astype(BF)
            fq = fq_ref[h * DH : (h + 1) * DH, at]
            num = num_ref[h, :, at] + jnp.dot(prefix, fq, preferred_element_type=F32)
            out = num[:DH, :] * (scale[h] / num[DH : DH + 1, :])
            out_ref[h * DH : (h + 1) * DH, at] = out
            squares = squares + jnp.sum(out * out, axis=0, keepdims=True)
        sq_ref[:, at] = squares

    each_group(fq_ref.shape[1], step)


def join_call(pos, scale, states, pre, fq, num):
    n = fq.shape[1]
    return resident(
        join_kernel,
        [pos, scale],
        [*states, pre, fq, num],
        [((HL * DH, n), F32), ((1, n), F32)],
        [pltpu.VMEM((HL, VA, DH), F32)],
        12,
        "join",
    )


def norm_kernel(out_ref, s0, s1, s2, s3, gain_ref, o_ref, buf, sem):
    eye = lax.broadcasted_iota(jnp.int32, (DH, DH), 0) == lax.broadcasted_iota(
        jnp.int32, (DH, DH), 1
    )
    gains = [
        jnp.sum(jnp.where(eye, gain_ref[h : h + 1, :], 0.0), axis=1, keepdims=True)
        for h in range(HL)
    ]
    copies = []
    for g in range(out_ref.shape[1] // GROUP):
        at = slice(g * GROUP, (g + 1) * GROUP)
        squares = s0[:, at] + s1[:, at] + s2[:, at] + s3[:, at]
        inv = lax.rsqrt(squares * (1.0 / (H * DH)) + 1e-06)
        for h in range(HL):
            rows = slice(h * DH, (h + 1) * DH)
            buf[rows, at] = (out_ref[rows, at] * inv * gains[h]).astype(BF)
        here = pl.ds(g * GROUP, GROUP)
        copies.append(pltpu.make_async_copy(buf.at[:, here], o_ref.at[:, here], sem.at[g]))
        copies[-1].start()
    for copy in copies:
        copy.wait()


def norm_call(out, squares, gain):
    n = out.shape[1]
    return pl.pallas_call(
        norm_kernel,
        in_specs=[pl.BlockSpec(memory_space=pltpu.VMEM)] * 6,
        out_specs=pl.BlockSpec(memory_space=pl.ANY),
        out_shape=jax.ShapeDtypeStruct((HL * DH, n), BF),
        scratch_shapes=[
            pltpu.VMEM((HL * DH, n), BF),
            pltpu.SemaphoreType.DMA((n // GROUP,)),
        ],
        compiler_params=pltpu.CompilerParams(vmem_limit_bytes=8 * MIB),
        cost_estimate=QUICK,
        name="norm",
    )(fast(out), *(fast(a) for a in squares), fast(gain))


def body(tokens, qkv_weight, block_mask, head_scale, norm_gain):
    me = lax.axis_index("tm").astype(jnp.int32)
    y, x, core = me // 8, (me // 2) % 4, me % 2
    pos = jnp.stack([y, x, core])
    pos, gain = lax.optimization_barrier((pos, norm_gain.reshape(HL, DH)))
    shards = [qkv_weight] + [shift(qkv_weight, first_leg(d)) for d in (1, 2, 3)]
    near_kv, near_q = pack(pos, shards)
    near_kv, xt = lax.optimization_barrier((near_kv, tokens.T))
    own_kv = [near_kv] + [shift(near_kv, second_leg(d)) for d in (1, 2, 3)]
    sib_kv, first_q = [shift(near_kv, SIBLING)], [near_q, shift(near_q, SIBLING)]
    xp = spread(pltpu.with_memory_space_constraint(xt, pltpu.HBM))

    both = ((True, 0), (False, 0))
    mine = tuple((True, d) for d in (1, 2, 3))
    last = tuple((False, d) for d in (1, 2, 3))
    kv_sum, q_sum = part_call(both, pos, [near_kv, sib_kv[0]], first_q, xp)
    near_q, kv_sum, q_sum = lax.optimization_barrier((near_q, kv_sum, q_sum))
    own_q = [shift(near_q, second_leg(d)) for d in (1, 2, 3)]
    *own_kv, kv_sum = lax.optimization_barrier((*own_kv, kv_sum))
    sib_kv = [shift(a, SIBLING) for a in own_kv[1:]]
    fk, v, pre, tot = kv_call(mine + last, pos, [*own_kv[1:], *sib_kv], xp, kv_sum)

    other = shift(tot, SIBLING)
    *own_q, other = lax.optimization_barrier((*own_q, other))
    sib_q = [shift(a, SIBLING) for a in own_q]
    chip = small(chip_kernel, [tot, other], "chip")
    chip, q_sum = lax.optimization_barrier((chip, q_sum))
    fq = q_call(mine + last, pos, [*own_q, *sib_q], xp, q_sum)
    in_row = [shift(chip, along_x(d)) for d in (1, 2, 3)]
    *in_row, fq = lax.optimization_barrier((*in_row, fq))
    row = small(row_kernel, [chip, *in_row], "row")
    row, fq = lax.optimization_barrier((row, fq))
    num = attend_call(block_mask, fk, v, fq)
    above = [shift(row, later_y(d)) for d in (1, 2, 3)]

    out, squares = join_call(pos, head_scale, [other, *in_row, *above], pre, fq, num)
    squares = [squares] + [
        lax.ppermute(squares, "head", [(i, (i + d) % 4) for i in range(4)]) for d in (1, 2, 3)
    ]
    return norm_call(out, squares, gain).T


def solution(mesh):
    in_specs = (P("tm", None), P("tm", "head"), P("tm"), P("head"), P("head"))
    out_specs = P("tm", "head")
    return jax.shard_map(body, mesh=mesh, in_specs=in_specs, out_specs=out_specs, check_vma=False)
```

```python
import functools

import jax
import jax.numpy as jnp
from jax import lax
from jax.experimental import pallas as pl
from jax.experimental.pallas import tpu as pltpu
from jax.sharding import PartitionSpec as P

H = 20
DH = 112
GROUP = 512
D = 2240
HL = 5
SHARD = 70
PAD = 72
BLK = 4 * PAD
VA = 128
QCOL = 1152
COLS = 1792
BF = jnp.bfloat16
F32 = jnp.float32
MIB = 1 << 20
QUICK = pl.CostEstimate(flops=1, bytes_accessed=1, transcendentals=0)

LONG = pl.CostEstimate(flops=11500000000, bytes_accessed=1, transcendentals=0)


def place(y, x, c):
    return (y % 4) * 8 + (x % 4) * 2 + c


def perm(move):
    return [
        (place(y, x, c), place(*move(y, x, c)))
        for y in range(4)
        for x in range(4)
        for c in range(2)
    ]


SIBLING = perm(lambda y, x, c: (y, x, 1 - c))


def first_leg(d):
    return perm(lambda y, x, c: (y, x + d, c) if c == 0 else (y + d, x, c))


def second_leg(d):
    return perm(lambda y, x, c: (y + d, x, c) if c == 0 else (y, x + d, c))


def along_x(d):
    return perm(lambda y, x, c: (y, x + d, c))


def later_y(d):
    return [
        (place(y, x, c), place(y + d, x, c))
        for y in range(4 - d)
        for x in range(4)
        for c in range(2)
    ]


def shift(a, moves):
    return lax.ppermute(a, "tm", moves)


def pack_kernel(pos, a0, a1, a2, a3, kv_ref, q_ref, wide):
    coord = jnp.where(pos[2] == 0, pos[1], pos[0])
    wide[...] = jnp.zeros_like(wide)
    for r, a in enumerate((a0, a1, a2, a3)):
        at = pl.multiple_of(((coord + 4 - r) & 3) * PAD, 8)
        shard = a[...].astype(F32)
        for kind, base in ((0, QCOL), (1, 0), (2, HL * DH)):
            for h in range(HL):
                col = h * 3 * DH + kind * DH
                to = base + h * DH
                wide[pl.ds(at, SHARD), to : to + DH] = shard[:, col : col + DH]
    kv_ref[...] = wide[:, :QCOL].astype(BF)
    q_ref[...] = wide[:, QCOL:].astype(BF)


def pack(pos, shards):
    return resident(
        pack_kernel,
        [pos],
        shards,
        [((BLK, QCOL), BF), ((BLK, COLS - QCOL), BF)],
        [pltpu.VMEM((BLK, COLS), F32)],
        10,
        "pack",
    )


def spread_kernel(x_ref, w_ref, o_ref, w_out):
    gap = jnp.zeros((PAD - SHARD, x_ref.shape[1]), BF)
    for y in range(4):
        for x in range(4):
            for c in range(2):
                block, slot = (y, x) if c == 0 else (4 + x, y)
                dev = place(y, x, c)
                at = slot * PAD
                o_ref[block, at : at + SHARD, :] = x_ref[dev * SHARD : (dev + 1) * SHARD, :]
                o_ref[block, at + SHARD : at + PAD, :] = gap

    @pl.when(pl.program_id(0) == 0)
    def _():
        w_out[...] = w_ref[...]


def spread(xt, w):
    n = xt.shape[1]
    blk = 256
    slow = pltpu.with_memory_space_constraint
    return pl.pallas_call(
        spread_kernel,
        grid=(n // blk,),
        in_specs=[
            pl.BlockSpec((D, blk), lambda g: (0, g)),
            pl.BlockSpec(w.shape, lambda g: (0, 0)),
        ],
        out_specs=[
            pl.BlockSpec((8, BLK, blk), lambda g: (0, 0, g)),
            pl.BlockSpec(w.shape, lambda g: (0, 0)),
        ],
        out_shape=[pltpu.VMEM((8, BLK, n), BF), pltpu.VMEM(w.shape, BF)],
        compiler_params=pltpu.CompilerParams(vmem_limit_bytes=8 * MIB),
        cost_estimate=QUICK,
        name="spread",
    )(slow(xt, pltpu.HBM), slow(w, pltpu.HBM))


def product(w, x):
    return lax.dot_general(w, x, (((0,), (0,)), ((), ())), preferred_element_type=F32)


def fast(a):
    return pltpu.with_memory_space_constraint(a, pltpu.VMEM)


def lay(pieces, wbuf):
    for i, piece in enumerate(pieces):
        wbuf[i * BLK : (i + 1) * BLK, :] = piece[...]


def block(pos, mine, d):
    which = pos[2] if mine else 1 - pos[2]
    return which * 4 + ((jnp.where(which == 0, pos[0], pos[1]) + 4 - d) & 3)


def rows_of(pos, steps, x_ref, at):
    return jnp.concatenate([x_ref[block(pos, *step), :, at] for step in steps], axis=0)


def each_group(n, step):
    def run(g, carry):
        step(g, pl.ds(pl.multiple_of(g * GROUP, GROUP), GROUP))
        return carry

    lax.fori_loop(0, n // GROUP, run, 0)


def resident(kernel, small, large, outs, scratch, limit, name, alias=None, cost=QUICK):
    return pl.pallas_call(
        kernel,
        in_specs=[pl.BlockSpec(memory_space=pltpu.SMEM)] * len(small)
        + [pl.BlockSpec(memory_space=pltpu.VMEM)] * len(large),
        out_specs=[pl.BlockSpec(memory_space=pltpu.VMEM)] * len(outs),
        out_shape=[pltpu.VMEM(shape, kind) for shape, kind in outs],
        scratch_shapes=scratch,
        input_output_aliases=alias or {},
        compiler_params=pltpu.CompilerParams(vmem_limit_bytes=limit * MIB),
        cost_estimate=cost,
        name=name,
    )(*small, *(fast(a) for a in large))


def part_kernel(steps, pos, *refs):
    count = len(steps)
    pieces, x_ref, sum_ref, wbuf = refs[:count], refs[count], refs[-2], refs[-1]
    lay(pieces, wbuf)
    rows = sum_ref.shape[0]

    def step(g, at):
        new = product(wbuf[:, :rows], rows_of(pos, steps, x_ref, at))
        sum_ref[:, at] = new + refs[count + 1][:, at] if len(refs) == count + 4 else new

    each_group(x_ref.shape[2], step)


def part_call(steps, pos, pieces, xp, rows, sums=None, name="part", cost=QUICK):
    earlier = [] if sums is None else [sums]
    (out,) = resident(
        functools.partial(part_kernel, steps),
        [pos],
        [*pieces, xp, *earlier],
        [((rows, xp.shape[2]), F32)],
        [pltpu.VMEM((len(steps) * BLK, pieces[0].shape[1]), BF)],
        16,
        name,
        {len(pieces) + 2: 0} if earlier else None,
        cost,
    )
    return out


def feature(raw):
    a = raw.astype(BF).astype(F32)
    return jnp.where(a > 0, a + 1.0, jnp.exp(jnp.minimum(a, 0.0))).astype(BF)


def kv_kernel(steps, pos, *refs):
    count = len(refs) - 8
    pieces = refs[:count]
    x_ref, sum_ref, fk_ref, v_ref, pre_ref, tot_ref, wbuf, run = refs[count:]
    lay(pieces, wbuf)
    run[...] = jnp.zeros_like(run)
    half = HL * DH

    def step(g, at):
        x = rows_of(pos, steps, x_ref, at)
        raw = product(wbuf[:, : 2 * half], x) + sum_ref[:, at]
        fk = feature(raw[:half, :])
        tail = (lax.broadcasted_iota(jnp.int32, (VA - DH, GROUP), 0) == 0).astype(F32).astype(BF)
        for h in range(HL):
            kn = fk[h * DH : (h + 1) * DH, :].T
            fk_ref[h, at, :] = kn
            val = raw[half + h * DH : half + (h + 1) * DH, :].astype(BF)
            va = jnp.concatenate([val, tail], axis=0)
            v_ref[h, :, at] = va
            state = jnp.dot(va, kn, preferred_element_type=F32)
            before = run[h]
            pre_ref[g, h] = before
            run[h] = before + state

    each_group(x_ref.shape[2], step)
    tot_ref[...] = run[...].astype(BF)


def kv_call(steps, pos, pieces, xp, sums):
    n = xp.shape[2]
    return resident(
        functools.partial(kv_kernel, steps),
        [pos],
        [*pieces, xp, sums],
        [
            ((HL, n, DH), BF),
            ((HL, VA, n), BF),
            ((n // GROUP, HL, VA, DH), F32),
            ((HL, VA, DH), BF),
        ],
        [pltpu.VMEM((len(pieces) * BLK, QCOL), BF), pltpu.VMEM((HL, VA, DH), F32)],
        20,
        "keys_values",
    )


def q_kernel(steps, pos, *refs):
    count = len(refs) - 4
    pieces, (x_ref, sum_ref, fq_ref, wbuf) = refs[:count], refs[count:]
    lay(pieces, wbuf)

    def step(g, at):
        x = rows_of(pos, steps, x_ref, at)
        fq_ref[:, at] = feature(product(wbuf[:, : HL * DH], x) + sum_ref[:, at])

    each_group(x_ref.shape[2], step)


def q_call(steps, pos, pieces, xp, sums):
    (out,) = resident(
        functools.partial(q_kernel, steps),
        [pos],
        [*pieces, xp, sums],
        [(sums.shape, BF)],
        [pltpu.VMEM((len(pieces) * BLK, COLS - QCOL), BF)],
        12,
        "queries",
    )
    return out


def mask_rows(code, j0, rows, t0, cols):
    parts = []
    for j in range(j0, j0 + rows // 64):
        t = lax.broadcasted_iota(jnp.int32, (64, cols), 1) + t0
        s = lax.broadcasted_iota(jnp.int32, (64, cols), 0)
        i = t >> 6
        bit = (jnp.full((64, cols), code, jnp.int32) >> (((i * (i - 1)) >> 1) + j)) & 1
        same = jnp.where(s <= (t & 63), 1, 0)
        keep = jnp.where(i > j, bit, jnp.where(i == j, same, 0))
        parts.append(keep.astype(F32).astype(BF))
    return jnp.concatenate(parts, axis=0)


def attend_kernel(codes, fk_ref, v_ref, fq_ref, num_ref):
    half = GROUP // 2

    def step(g, at):
        code = codes[g]
        start = pl.multiple_of(g * GROUP, GROUP)
        one, two = pl.ds(start, half), pl.ds(start + half, half)
        upper = mask_rows(code, 0, half, 0, GROUP)
        lower = mask_rows(code, 4, half, half, half)
        for h in range(HL):
            fq = fq_ref[h * DH : (h + 1) * DH, at]
            top = jnp.dot(fk_ref[h, one, :], fq, preferred_element_type=F32)
            top = top.astype(BF) * upper
            low = jnp.dot(fk_ref[h, two, :], fq[:, half:], preferred_element_type=F32)
            low = low.astype(BF) * lower
            num = jnp.dot(v_ref[h, :, one], top, preferred_element_type=F32)
            more = jnp.dot(v_ref[h, :, two], low, preferred_element_type=F32)
            num_ref[h, :, one] = num[:, :half]
            num_ref[h, :, two] = num[:, half:] + more

    each_group(fq_ref.shape[1], step)


def attend_call(codes, fk, v, fq):
    (out,) = resident(
        attend_kernel,
        [codes],
        [fk, v, fq],
        [((HL, VA, fq.shape[1]), F32)],
        [],
        12,
        "attend",
    )
    return out


def chip_kernel(tot_ref, other_ref, chip_ref):
    chip_ref[...] = (tot_ref[...].astype(F32) + other_ref[...].astype(F32)).astype(BF)


def row_kernel(a, b, c, d, row_ref):
    total = a[...].astype(F32) + b[...].astype(F32) + c[...].astype(F32) + d[...].astype(F32)
    row_ref[...] = total.astype(BF)


def small(kernel, args, name):
    (out,) = resident(kernel, [], args, [(args[0].shape, BF)], [], 4, name)
    return out


def join_kernel(pos, scale, *refs):
    other, near, far = refs[0], refs[1:4], refs[4:7]
    pre_ref, fq_ref, num_ref, out_ref, sq_ref, dev = refs[7:]
    total = far[0][...].astype(F32) + far[1][...].astype(F32) + far[2][...].astype(F32)
    total = total + jnp.where(pos[2] == 1, other[...].astype(F32), 0.0)
    for d, got in enumerate(near):
        total = total + jnp.where(pos[1] >= d + 1, got[...].astype(F32), 0.0)
    dev[...] = total

    def step(g, at):
        squares = jnp.zeros((1, GROUP), F32)
        for h in range(HL):
            prefix = (dev[h] + pre_ref[g, h]).astype(BF)
            fq = fq_ref[h * DH : (h + 1) * DH, at]
            num = num_ref[h, :, at] + jnp.dot(prefix, fq, preferred_element_type=F32)
            out = num[:DH, :] * (scale[h] / num[DH : DH + 1, :])
            out_ref[h * DH : (h + 1) * DH, at] = out
            squares = squares + jnp.sum(out * out, axis=0, keepdims=True)
        sq_ref[:, at] = squares

    each_group(fq_ref.shape[1], step)


def join_call(pos, scale, states, pre, fq, num):
    n = fq.shape[1]
    return resident(
        join_kernel,
        [pos, scale],
        [*states, pre, fq, num],
        [((HL * DH, n), F32), ((1, n), F32)],
        [pltpu.VMEM((HL, VA, DH), F32)],
        12,
        "join",
    )


def norm_kernel(out_ref, s0, s1, s2, s3, gain_ref, o_ref, buf, sem):
    eye = lax.broadcasted_iota(jnp.int32, (DH, DH), 0) == lax.broadcasted_iota(
        jnp.int32, (DH, DH), 1
    )
    gains = [
        jnp.sum(jnp.where(eye, gain_ref[h : h + 1, :], 0.0), axis=1, keepdims=True)
        for h in range(HL)
    ]
    copies = []
    for g in range(out_ref.shape[1] // GROUP):
        at = slice(g * GROUP, (g + 1) * GROUP)
        squares = s0[:, at] + s1[:, at] + s2[:, at] + s3[:, at]
        inv = lax.rsqrt(squares * (1.0 / (H * DH)) + 1e-06)
        for h in range(HL):
            rows = slice(h * DH, (h + 1) * DH)
            buf[rows, at] = (out_ref[rows, at] * inv * gains[h]).astype(BF)
        here = pl.ds(g * GROUP, GROUP)
        copies.append(pltpu.make_async_copy(buf.at[:, here], o_ref.at[:, here], sem.at[g]))
        copies[-1].start()
    for copy in copies:
        copy.wait()


def norm_call(out, squares, gain):
    n = out.shape[1]
    return pl.pallas_call(
        norm_kernel,
        in_specs=[pl.BlockSpec(memory_space=pltpu.VMEM)] * 6,
        out_specs=pl.BlockSpec(memory_space=pl.ANY),
        out_shape=jax.ShapeDtypeStruct((HL * DH, n), BF),
        scratch_shapes=[
            pltpu.VMEM((HL * DH, n), BF),
            pltpu.SemaphoreType.DMA((n // GROUP,)),
        ],
        compiler_params=pltpu.CompilerParams(vmem_limit_bytes=8 * MIB),
        cost_estimate=QUICK,
        name="norm",
    )(fast(out), *(fast(a) for a in squares), fast(gain))


def body(tokens, qkv_weight, block_mask, head_scale, norm_gain):
    me = lax.axis_index("tm").astype(jnp.int32)
    y, x, core = me // 8, (me // 2) % 4, me % 2
    pos = jnp.stack([y, x, core])
    pos, gain, xt = lax.optimization_barrier((pos, norm_gain.reshape(HL, DH), tokens.T))
    shards = [shift(qkv_weight, first_leg(d)) for d in (1, 2, 3)]
    xp, staged = spread(xt, qkv_weight)
    near_kv, near_q = pack(pos, [staged, *shards])
    own_kv = [near_kv] + [shift(near_kv, second_leg(d)) for d in (1, 2, 3)]
    sib_kv = [shift(near_kv, SIBLING)] + [None] * 3
    first_q = [near_q, shift(near_q, SIBLING)]

    both = ((True, 0), (False, 0))
    beside = ((True, 1), (False, 1), (True, 3), (False, 3))
    across = ((True, 2), (False, 2))
    rest = tuple((mine, d) for mine in (True, False) for d in (1, 2, 3))
    half = HL * DH
    kv_sum = part_call(both, pos, [near_kv, sib_kv[0]], xp, 2 * half, name="part_kv")
    own_kv[1], own_kv[3], kv_sum, *first_q = lax.optimization_barrier(
        (own_kv[1], own_kv[3], kv_sum, *first_q)
    )
    sib_kv[1], sib_kv[3] = shift(own_kv[1], SIBLING), shift(own_kv[3], SIBLING)
    q_sum = part_call(both, pos, first_q, xp, half, name="part_q", cost=LONG)
    kv_sum, q_sum = lax.optimization_barrier((kv_sum, q_sum))
    kv_sum = part_call(
        beside,
        pos,
        [(own_kv if mine else sib_kv)[d] for mine, d in beside],
        xp,
        2 * half,
        kv_sum,
        name="part_more",
    )
    near_q, own_kv[2], kv_sum = lax.optimization_barrier((first_q[0], own_kv[2], kv_sum))
    sib_kv[2] = shift(own_kv[2], SIBLING)
    own_q = [shift(near_q, second_leg(d)) for d in (1, 2, 3)]
    fk, v, pre, tot = kv_call(across, pos, [own_kv[2], sib_kv[2]], xp, kv_sum)

    other = shift(tot, SIBLING)
    *own_q, other = lax.optimization_barrier((*own_q, other))
    sib_q = [shift(a, SIBLING) for a in own_q]
    chip = small(chip_kernel, [tot, other], "chip")
    chip, q_sum = lax.optimization_barrier((chip, q_sum))
    fq = q_call(rest, pos, [*own_q, *sib_q], xp, q_sum)
    in_row = [shift(chip, along_x(d)) for d in (1, 2, 3)]
    *in_row, fq = lax.optimization_barrier((*in_row, fq))
    row = small(row_kernel, [chip, *in_row], "row")
    row, fq = lax.optimization_barrier((row, fq))
    num = attend_call(block_mask, fk, v, fq)
    above = [shift(row, later_y(d)) for d in (1, 2, 3)]

    out, squares = join_call(pos, head_scale, [other, *in_row, *above], pre, fq, num)
    squares = [squares] + [
        lax.ppermute(squares, "head", [(i, (i + d) % 4) for i in range(4)]) for d in (1, 2, 3)
    ]
    return norm_call(out, squares, gain).T


def solution(mesh):
    in_specs = (P("tm", None), P("tm", "head"), P("tm"), P("head"), P("head"))
    out_specs = P("tm", "head")
    return jax.shard_map(body, mesh=mesh, in_specs=in_specs, out_specs=out_specs, check_vma=False)
```

```python
import functools

import jax
import jax.numpy as jnp
from jax import lax
from jax.experimental import pallas as pl
from jax.experimental.pallas import tpu as pltpu
from jax.sharding import PartitionSpec as P

H = 20
DH = 112
GROUP = 512
D = 2240
HL = 5
SHARD = 70
PAD = 72
BLK = 4 * PAD
VA = 128
QCOL = 1152
COLS = 1792
BF = jnp.bfloat16
F32 = jnp.float32
MIB = 1 << 20
QUICK = pl.CostEstimate(flops=1, bytes_accessed=1, transcendentals=0)


def place(y, x, c):
    return (y % 4) * 8 + (x % 4) * 2 + c


def perm(move):
    return [
        (place(y, x, c), place(*move(y, x, c)))
        for y in range(4)
        for x in range(4)
        for c in range(2)
    ]


SIBLING = perm(lambda y, x, c: (y, x, 1 - c))


def first_leg(d):
    return perm(lambda y, x, c: (y, x + d, c) if c == 0 else (y + d, x, c))


def second_leg(d):
    return perm(lambda y, x, c: (y + d, x, c) if c == 0 else (y, x + d, c))


def along_x(d):
    return perm(lambda y, x, c: (y, x + d, c))


def later_y(d):
    return [
        (place(y, x, c), place(y + d, x, c))
        for y in range(4 - d)
        for x in range(4)
        for c in range(2)
    ]


def shift(a, moves):
    return lax.ppermute(a, "tm", moves)


def pack_kernel(pos, a0, a1, a2, a3, kv_ref, q_ref, wide):
    coord = jnp.where(pos[2] == 0, pos[1], pos[0])
    wide[...] = jnp.zeros_like(wide)
    for r, a in enumerate((a0, a1, a2, a3)):
        at = pl.multiple_of(((coord + 4 - r) & 3) * PAD, 8)
        shard = a[...].astype(F32)
        for kind, base in ((0, QCOL), (1, 0), (2, HL * DH)):
            for h in range(HL):
                col = h * 3 * DH + kind * DH
                to = base + h * DH
                wide[pl.ds(at, SHARD), to : to + DH] = shard[:, col : col + DH]
    kv_ref[...] = wide[:, :QCOL].astype(BF)
    q_ref[...] = wide[:, QCOL:].astype(BF)


def pack(pos, shards):
    return resident(
        pack_kernel,
        [pos],
        shards,
        [((BLK, QCOL), BF), ((BLK, COLS - QCOL), BF)],
        [pltpu.VMEM((BLK, COLS), F32)],
        10,
        "pack",
    )


def spread_kernel(x_ref, w_ref, o_ref, w_out):
    gap = jnp.zeros((PAD - SHARD, x_ref.shape[1]), BF)
    for y in range(4):
        for x in range(4):
            for c in range(2):
                block, slot = (y, x) if c == 0 else (4 + x, y)
                dev = place(y, x, c)
                at = slot * PAD
                o_ref[block, at : at + SHARD, :] = x_ref[dev * SHARD : (dev + 1) * SHARD, :]
                o_ref[block, at + SHARD : at + PAD, :] = gap

    @pl.when(pl.program_id(0) == 0)
    def _():
        w_out[...] = w_ref[...]


def spread(xt, w):
    n = xt.shape[1]
    blk = 256
    slow = pltpu.with_memory_space_constraint
    return pl.pallas_call(
        spread_kernel,
        grid=(n // blk,),
        in_specs=[
            pl.BlockSpec((D, blk), lambda g: (0, g)),
            pl.BlockSpec(w.shape, lambda g: (0, 0)),
        ],
        out_specs=[
            pl.BlockSpec((8, BLK, blk), lambda g: (0, 0, g)),
            pl.BlockSpec(w.shape, lambda g: (0, 0)),
        ],
        out_shape=[pltpu.VMEM((8, BLK, n), BF), pltpu.VMEM(w.shape, BF)],
        compiler_params=pltpu.CompilerParams(vmem_limit_bytes=8 * MIB),
        cost_estimate=QUICK,
        name="spread",
    )(slow(xt, pltpu.HBM), slow(w, pltpu.HBM))


def product(w, x):
    return lax.dot_general(w, x, (((0,), (0,)), ((), ())), preferred_element_type=F32)


def fast(a):
    return pltpu.with_memory_space_constraint(a, pltpu.VMEM)


def lay(pieces, wbuf):
    for i, piece in enumerate(pieces):
        wbuf[i * BLK : (i + 1) * BLK, :] = piece[...]


def block(pos, mine, d):
    which = pos[2] if mine else 1 - pos[2]
    return which * 4 + ((jnp.where(which == 0, pos[0], pos[1]) + 4 - d) & 3)


def rows_of(pos, steps, x_ref, at):
    return jnp.concatenate([x_ref[block(pos, *step), :, at] for step in steps], axis=0)


def each_group(n, step):
    def run(g, carry):
        step(g, pl.ds(pl.multiple_of(g * GROUP, GROUP), GROUP))
        return carry

    lax.fori_loop(0, n // GROUP, run, 0)


def resident(kernel, small, large, outs, scratch, limit, name, alias=None, cost=QUICK):
    return pl.pallas_call(
        kernel,
        in_specs=[pl.BlockSpec(memory_space=pltpu.SMEM)] * len(small)
        + [pl.BlockSpec(memory_space=pltpu.VMEM)] * len(large),
        out_specs=[pl.BlockSpec(memory_space=pltpu.VMEM)] * len(outs),
        out_shape=[pltpu.VMEM(shape, kind) for shape, kind in outs],
        scratch_shapes=scratch,
        input_output_aliases=alias or {},
        compiler_params=pltpu.CompilerParams(vmem_limit_bytes=limit * MIB),
        cost_estimate=cost,
        name=name,
    )(*small, *(fast(a) for a in large))


def part_kernel(steps, pos, *refs):
    count = len(steps)
    pieces, x_ref, sum_ref, wbuf = refs[:count], refs[count], refs[-2], refs[-1]
    lay(pieces, wbuf)
    rows = sum_ref.shape[0]

    def step(g, at):
        new = product(wbuf[:, :rows], rows_of(pos, steps, x_ref, at))
        sum_ref[:, at] = new + refs[count + 1][:, at] if len(refs) == count + 4 else new

    each_group(x_ref.shape[2], step)


def part_call(steps, pos, pieces, xp, rows, sums=None, name="part", cost=QUICK):
    earlier = [] if sums is None else [sums]
    (out,) = resident(
        functools.partial(part_kernel, steps),
        [pos],
        [*pieces, xp, *earlier],
        [((rows, xp.shape[2]), F32)],
        [pltpu.VMEM((len(steps) * BLK, pieces[0].shape[1]), BF)],
        16,
        name,
        {len(pieces) + 2: 0} if earlier else None,
        cost,
    )
    return out


def feature(raw):
    a = raw.astype(BF).astype(F32)
    return jnp.where(a > 0, a + 1.0, jnp.exp(jnp.minimum(a, 0.0))).astype(BF)


def kv_kernel(steps, pos, *refs):
    count = len(refs) - 8
    pieces = refs[:count]
    x_ref, sum_ref, fk_ref, v_ref, pre_ref, tot_ref, wbuf, run = refs[count:]
    lay(pieces, wbuf)
    run[...] = jnp.zeros_like(run)
    half = HL * DH

    def step(g, at):
        x = rows_of(pos, steps, x_ref, at)
        raw = product(wbuf[:, : 2 * half], x) + sum_ref[:, at]
        fk = feature(raw[:half, :])
        tail = (lax.broadcasted_iota(jnp.int32, (VA - DH, GROUP), 0) == 0).astype(F32).astype(BF)
        for h in range(HL):
            kn = fk[h * DH : (h + 1) * DH, :].T
            fk_ref[h, at, :] = kn
            val = raw[half + h * DH : half + (h + 1) * DH, :].astype(BF)
            va = jnp.concatenate([val, tail], axis=0)
            v_ref[h, :, at] = va
            state = jnp.dot(va, kn, preferred_element_type=F32)
            before = run[h]
            pre_ref[g, h] = before
            run[h] = before + state

    each_group(x_ref.shape[2], step)
    tot_ref[...] = run[...].astype(BF)


def kv_call(steps, pos, pieces, xp, sums):
    n = xp.shape[2]
    return resident(
        functools.partial(kv_kernel, steps),
        [pos],
        [*pieces, xp, sums],
        [
            ((HL, n, DH), BF),
            ((HL, VA, n), BF),
            ((n // GROUP, HL, VA, DH), F32),
            ((HL, VA, DH), BF),
        ],
        [pltpu.VMEM((len(pieces) * BLK, QCOL), BF), pltpu.VMEM((HL, VA, DH), F32)],
        20,
        "keys_values",
    )


def q_kernel(steps, pos, *refs):
    count = len(refs) - 4
    pieces, (x_ref, sum_ref, fq_ref, wbuf) = refs[:count], refs[count:]
    lay(pieces, wbuf)

    def step(g, at):
        x = rows_of(pos, steps, x_ref, at)
        fq_ref[:, at] = feature(product(wbuf[:, : HL * DH], x) + sum_ref[:, at])

    each_group(x_ref.shape[2], step)


def q_call(steps, pos, pieces, xp, sums):
    (out,) = resident(
        functools.partial(q_kernel, steps),
        [pos],
        [*pieces, xp, sums],
        [(sums.shape, BF)],
        [pltpu.VMEM((len(pieces) * BLK, COLS - QCOL), BF)],
        12,
        "queries",
    )
    return out


def mask_rows(code, j0, rows, t0, cols):
    parts = []
    for j in range(j0, j0 + rows // 64):
        t = lax.broadcasted_iota(jnp.int32, (64, cols), 1) + t0
        s = lax.broadcasted_iota(jnp.int32, (64, cols), 0)
        i = t >> 6
        bit = (jnp.full((64, cols), code, jnp.int32) >> (((i * (i - 1)) >> 1) + j)) & 1
        same = jnp.where(s <= (t & 63), 1, 0)
        keep = jnp.where(i > j, bit, jnp.where(i == j, same, 0))
        parts.append(keep.astype(F32).astype(BF))
    return jnp.concatenate(parts, axis=0)


def attend_kernel(codes, fk_ref, v_ref, fq_ref, num_ref):
    half = GROUP // 2

    def step(g, at):
        code = codes[g]
        start = pl.multiple_of(g * GROUP, GROUP)
        one, two = pl.ds(start, half), pl.ds(start + half, half)
        upper = mask_rows(code, 0, half, 0, GROUP)
        lower = mask_rows(code, 4, half, half, half)
        for h in range(HL):
            fq = fq_ref[h * DH : (h + 1) * DH, at]
            top = jnp.dot(fk_ref[h, one, :], fq, preferred_element_type=F32)
            top = top.astype(BF) * upper
            low = jnp.dot(fk_ref[h, two, :], fq[:, half:], preferred_element_type=F32)
            low = low.astype(BF) * lower
            num = jnp.dot(v_ref[h, :, one], top, preferred_element_type=F32)
            more = jnp.dot(v_ref[h, :, two], low, preferred_element_type=F32)
            num_ref[h, :, one] = num[:, :half]
            num_ref[h, :, two] = num[:, half:] + more

    each_group(fq_ref.shape[1], step)


def attend_call(codes, fk, v, fq):
    (out,) = resident(
        attend_kernel,
        [codes],
        [fk, v, fq],
        [((HL, VA, fq.shape[1]), F32)],
        [],
        12,
        "attend",
    )
    return out


def chip_kernel(tot_ref, other_ref, chip_ref):
    chip_ref[...] = (tot_ref[...].astype(F32) + other_ref[...].astype(F32)).astype(BF)


def row_kernel(a, b, c, d, row_ref):
    total = a[...].astype(F32) + b[...].astype(F32) + c[...].astype(F32) + d[...].astype(F32)
    row_ref[...] = total.astype(BF)


def small(kernel, args, name):
    (out,) = resident(kernel, [], args, [(args[0].shape, BF)], [], 4, name)
    return out


def join_kernel(pos, scale, *refs):
    other, near, far = refs[0], refs[1:4], refs[4:7]
    pre_ref, fq_ref, num_ref, out_ref, sq_ref, dev = refs[7:]
    total = far[0][...].astype(F32) + far[1][...].astype(F32) + far[2][...].astype(F32)
    total = total + jnp.where(pos[2] == 1, other[...].astype(F32), 0.0)
    for d, got in enumerate(near):
        total = total + jnp.where(pos[1] >= d + 1, got[...].astype(F32), 0.0)
    dev[...] = total

    def step(g, at):
        squares = jnp.zeros((1, GROUP), F32)
        for h in range(HL):
            prefix = (dev[h] + pre_ref[g, h]).astype(BF)
            fq = fq_ref[h * DH : (h + 1) * DH, at]
            num = num_ref[h, :, at] + jnp.dot(prefix, fq, preferred_element_type=F32)
            out = num[:DH, :] * (scale[h] / num[DH : DH + 1, :])
            out_ref[h * DH : (h + 1) * DH, at] = out
            squares = squares + jnp.sum(out * out, axis=0, keepdims=True)
        sq_ref[:, at] = squares

    each_group(fq_ref.shape[1], step)


def join_call(pos, scale, states, pre, fq, num):
    n = fq.shape[1]
    return resident(
        join_kernel,
        [pos, scale],
        [*states, pre, fq, num],
        [((HL * DH, n), F32), ((1, n), F32)],
        [pltpu.VMEM((HL, VA, DH), F32)],
        12,
        "join",
    )


def norm_kernel(out_ref, s0, s1, s2, s3, gain_ref, o_ref, buf, sem):
    eye = lax.broadcasted_iota(jnp.int32, (DH, DH), 0) == lax.broadcasted_iota(
        jnp.int32, (DH, DH), 1
    )
    gains = [
        jnp.sum(jnp.where(eye, gain_ref[h : h + 1, :], 0.0), axis=1, keepdims=True)
        for h in range(HL)
    ]
    copies = []
    for g in range(out_ref.shape[1] // GROUP):
        at = slice(g * GROUP, (g + 1) * GROUP)
        squares = s0[:, at] + s1[:, at] + s2[:, at] + s3[:, at]
        inv = lax.rsqrt(squares * (1.0 / (H * DH)) + 1e-06)
        for h in range(HL):
            rows = slice(h * DH, (h + 1) * DH)
            buf[rows, at] = (out_ref[rows, at] * inv * gains[h]).astype(BF)
        here = pl.ds(g * GROUP, GROUP)
        copies.append(pltpu.make_async_copy(buf.at[:, here], o_ref.at[:, here], sem.at[g]))
        copies[-1].start()
    for copy in copies:
        copy.wait()


def norm_call(out, squares, gain):
    n = out.shape[1]
    return pl.pallas_call(
        norm_kernel,
        in_specs=[pl.BlockSpec(memory_space=pltpu.VMEM)] * 6,
        out_specs=pl.BlockSpec(memory_space=pl.ANY),
        out_shape=jax.ShapeDtypeStruct((HL * DH, n), BF),
        scratch_shapes=[
            pltpu.VMEM((HL * DH, n), BF),
            pltpu.SemaphoreType.DMA((n // GROUP,)),
        ],
        compiler_params=pltpu.CompilerParams(vmem_limit_bytes=8 * MIB),
        cost_estimate=QUICK,
        name="norm",
    )(fast(out), *(fast(a) for a in squares), fast(gain))


def body(tokens, qkv_weight, block_mask, head_scale, norm_gain):
    me = lax.axis_index("tm").astype(jnp.int32)
    y, x, core = me // 8, (me // 2) % 4, me % 2
    pos = jnp.stack([y, x, core])
    pos, gain, xt = lax.optimization_barrier((pos, norm_gain.reshape(HL, DH), tokens.T))
    shards = [shift(qkv_weight, first_leg(d)) for d in (1, 2, 3)]
    xp, staged = spread(xt, qkv_weight)
    near_kv, near_q = pack(pos, [staged, *shards])
    own_kv = [near_kv] + [shift(near_kv, second_leg(d)) for d in (1, 2, 3)]
    sib_kv = [shift(near_kv, SIBLING)] + [None] * 3
    first_q = [near_q, shift(near_q, SIBLING)]

    both = ((True, 0), (False, 0))
    beside = ((True, 1), (False, 1), (True, 3), (False, 3))
    across = ((True, 2), (False, 2))
    rest = tuple((mine, d) for mine in (True, False) for d in (1, 2, 3))
    half = HL * DH
    kv_sum = part_call(both, pos, [near_kv, sib_kv[0]], xp, 2 * half, name="part_kv")
    own_kv[1], own_kv[3], kv_sum, *first_q = lax.optimization_barrier(
        (own_kv[1], own_kv[3], kv_sum, *first_q)
    )
    sib_kv[1], sib_kv[3] = shift(own_kv[1], SIBLING), shift(own_kv[3], SIBLING)
    q_sum = part_call(both, pos, first_q, xp, half, name="part_q")
    kv_sum, q_sum = lax.optimization_barrier((kv_sum, q_sum))
    kv_sum = part_call(
        beside,
        pos,
        [(own_kv if mine else sib_kv)[d] for mine, d in beside],
        xp,
        2 * half,
        kv_sum,
        name="part_more",
    )
    near_q, own_kv[2], kv_sum = lax.optimization_barrier((first_q[0], own_kv[2], kv_sum))
    sib_kv[2] = shift(own_kv[2], SIBLING)
    own_q = [shift(near_q, second_leg(d)) for d in (1, 2, 3)]
    fk, v, pre, tot = kv_call(across, pos, [own_kv[2], sib_kv[2]], xp, kv_sum)

    other = shift(tot, SIBLING)
    *own_q, other = lax.optimization_barrier((*own_q, other))
    sib_q = [shift(a, SIBLING) for a in own_q]
    chip = small(chip_kernel, [tot, other], "chip")
    chip, q_sum = lax.optimization_barrier((chip, q_sum))
    fq = q_call(rest, pos, [*own_q, *sib_q], xp, q_sum)
    in_row = [shift(chip, along_x(d)) for d in (1, 2, 3)]
    *in_row, fq = lax.optimization_barrier((*in_row, fq))
    row = small(row_kernel, [chip, *in_row], "row")
    row, fq = lax.optimization_barrier((row, fq))
    num = attend_call(block_mask, fk, v, fq)
    above = [shift(row, later_y(d)) for d in (1, 2, 3)]

    out, squares = join_call(pos, head_scale, [other, *in_row, *above], pre, fq, num)
    squares = [squares] + [
        lax.ppermute(squares, "head", [(i, (i + d) % 4) for i in range(4)]) for d in (1, 2, 3)
    ]
    return norm_call(out, squares, gain).T


def solution(mesh):
    in_specs = (P("tm", None), P("tm", "head"), P("tm"), P("head"), P("head"))
    out_specs = P("tm", "head")
    return jax.shard_map(body, mesh=mesh, in_specs=in_specs, out_specs=out_specs, check_vma=False)
```

```python
import functools

import jax
import jax.numpy as jnp
from jax import lax
from jax.experimental import pallas as pl
from jax.experimental.pallas import tpu as pltpu
from jax.sharding import PartitionSpec as P

H = 20
DH = 112
GROUP = 512
D = 2240
HL = 5
SHARD = 70
PAD = 72
BLK = 4 * PAD
VA = 128
QCOL = 1152
COLS = 1792
BF = jnp.bfloat16
F32 = jnp.float32
MIB = 1 << 20
QUICK = pl.CostEstimate(flops=1, bytes_accessed=1, transcendentals=0)


def place(y, x, c):
    return (y % 4) * 8 + (x % 4) * 2 + c


def perm(move):
    return [
        (place(y, x, c), place(*move(y, x, c)))
        for y in range(4)
        for x in range(4)
        for c in range(2)
    ]


SIBLING = perm(lambda y, x, c: (y, x, 1 - c))


def first_leg(d):
    return perm(lambda y, x, c: (y, x + d, c) if c == 0 else (y + d, x, c))


def second_leg(d):
    return perm(lambda y, x, c: (y + d, x, c) if c == 0 else (y, x + d, c))


def along_x(d):
    return perm(lambda y, x, c: (y, x + d, c))


def later_y(d):
    return [
        (place(y, x, c), place(y + d, x, c))
        for y in range(4 - d)
        for x in range(4)
        for c in range(2)
    ]


def shift(a, moves):
    return lax.ppermute(a, "tm", moves)


def pack_kernel(pos, a0, a1, a2, a3, kv_ref, q_ref, wide):
    coord = jnp.where(pos[2] == 0, pos[1], pos[0])
    wide[...] = jnp.zeros_like(wide)
    for r, a in enumerate((a0, a1, a2, a3)):
        at = pl.multiple_of(((coord + 4 - r) & 3) * PAD, 8)
        shard = a[...].astype(F32)
        for kind, base in ((0, QCOL), (1, 0), (2, HL * DH)):
            for h in range(HL):
                col = h * 3 * DH + kind * DH
                to = base + h * DH
                wide[pl.ds(at, SHARD), to : to + DH] = shard[:, col : col + DH]
    kv_ref[...] = wide[:, :QCOL].astype(BF)
    q_ref[...] = wide[:, QCOL:].astype(BF)


def pack(pos, shards):
    return resident(
        pack_kernel,
        [pos],
        shards,
        [((BLK, QCOL), BF), ((BLK, COLS - QCOL), BF)],
        [pltpu.VMEM((BLK, COLS), F32)],
        10,
        "pack",
    )


def spread_kernel(x_ref, w_ref, o_ref, w_out):
    gap = jnp.zeros((PAD - SHARD, x_ref.shape[1]), BF)
    for y in range(4):
        for x in range(4):
            for c in range(2):
                block, slot = (y, x) if c == 0 else (4 + x, y)
                dev = place(y, x, c)
                at = slot * PAD
                o_ref[block, at : at + SHARD, :] = x_ref[dev * SHARD : (dev + 1) * SHARD, :]
                o_ref[block, at + SHARD : at + PAD, :] = gap

    @pl.when(pl.program_id(0) == 0)
    def _():
        w_out[...] = w_ref[...]


def spread(xt, w):
    n = xt.shape[1]
    blk = 256
    slow = pltpu.with_memory_space_constraint
    return pl.pallas_call(
        spread_kernel,
        grid=(n // blk,),
        in_specs=[
            pl.BlockSpec((D, blk), lambda g: (0, g)),
            pl.BlockSpec(w.shape, lambda g: (0, 0)),
        ],
        out_specs=[
            pl.BlockSpec((8, BLK, blk), lambda g: (0, 0, g)),
            pl.BlockSpec(w.shape, lambda g: (0, 0)),
        ],
        out_shape=[pltpu.VMEM((8, BLK, n), BF), pltpu.VMEM(w.shape, BF)],
        compiler_params=pltpu.CompilerParams(vmem_limit_bytes=8 * MIB),
        cost_estimate=QUICK,
        name="spread",
    )(slow(xt, pltpu.HBM), slow(w, pltpu.HBM))


def product(w, x):
    return lax.dot_general(w, x, (((0,), (0,)), ((), ())), preferred_element_type=F32)


def fast(a):
    return pltpu.with_memory_space_constraint(a, pltpu.VMEM)


def rows_in(steps):
    return sum(hi - lo for _, _, lo, hi in steps)


def lay(steps, pieces, wbuf):
    at = 0
    for (_, _, lo, hi), piece in zip(steps, pieces):
        wbuf[at : at + hi - lo, :] = piece[lo:hi, :]
        at += hi - lo


def block(pos, mine, d):
    which = pos[2] if mine else 1 - pos[2]
    return which * 4 + ((jnp.where(which == 0, pos[0], pos[1]) + 4 - d) & 3)


def rows_of(pos, steps, x_ref, at):
    return jnp.concatenate(
        [x_ref[block(pos, mine, d), lo:hi, at] for mine, d, lo, hi in steps], axis=0
    )


def each_group(n, step):
    def run(g, carry):
        step(g, pl.ds(pl.multiple_of(g * GROUP, GROUP), GROUP))
        return carry

    lax.fori_loop(0, n // GROUP, run, 0)


def resident(kernel, small, large, outs, scratch, limit, name, alias=None, cost=QUICK):
    return pl.pallas_call(
        kernel,
        in_specs=[pl.BlockSpec(memory_space=pltpu.SMEM)] * len(small)
        + [pl.BlockSpec(memory_space=pltpu.VMEM)] * len(large),
        out_specs=[pl.BlockSpec(memory_space=pltpu.VMEM)] * len(outs),
        out_shape=[pltpu.VMEM(shape, kind) for shape, kind in outs],
        scratch_shapes=scratch,
        input_output_aliases=alias or {},
        compiler_params=pltpu.CompilerParams(vmem_limit_bytes=limit * MIB),
        cost_estimate=cost,
        name=name,
    )(*small, *(fast(a) for a in large))


def part_kernel(steps, pos, *refs):
    count = len(steps)
    pieces, x_ref, sum_ref, wbuf = refs[:count], refs[count], refs[-2], refs[-1]
    lay(steps, pieces, wbuf)
    rows = sum_ref.shape[0]

    def step(g, at):
        new = product(wbuf[:, :rows], rows_of(pos, steps, x_ref, at))
        sum_ref[:, at] = new + refs[count + 1][:, at] if len(refs) == count + 4 else new

    each_group(x_ref.shape[2], step)


def part_call(steps, pos, pieces, xp, rows, sums=None, name="part", cost=QUICK):
    earlier = [] if sums is None else [sums]
    (out,) = resident(
        functools.partial(part_kernel, steps),
        [pos],
        [*pieces, xp, *earlier],
        [((rows, xp.shape[2]), F32)],
        [pltpu.VMEM((rows_in(steps), pieces[0].shape[1]), BF)],
        16,
        name,
        {len(pieces) + 2: 0} if earlier else None,
        cost,
    )
    return out


def feature(raw):
    a = raw.astype(BF).astype(F32)
    return jnp.where(a > 0, a + 1.0, jnp.exp(jnp.minimum(a, 0.0))).astype(BF)


def kv_kernel(steps, pos, *refs):
    count = len(refs) - 8
    pieces = refs[:count]
    x_ref, sum_ref, fk_ref, v_ref, pre_ref, tot_ref, wbuf, run = refs[count:]
    lay(steps, pieces, wbuf)
    run[...] = jnp.zeros_like(run)
    half = HL * DH

    def step(g, at):
        x = rows_of(pos, steps, x_ref, at)
        raw = product(wbuf[:, : 2 * half], x) + sum_ref[:, at]
        fk = feature(raw[:half, :])
        tail = (lax.broadcasted_iota(jnp.int32, (VA - DH, GROUP), 0) == 0).astype(F32).astype(BF)
        for h in range(HL):
            kn = fk[h * DH : (h + 1) * DH, :].T
            fk_ref[h, at, :] = kn
            val = raw[half + h * DH : half + (h + 1) * DH, :].astype(BF)
            va = jnp.concatenate([val, tail], axis=0)
            v_ref[h, :, at] = va
            state = jnp.dot(va, kn, preferred_element_type=F32)
            before = run[h]
            pre_ref[g, h] = before
            run[h] = before + state

    each_group(x_ref.shape[2], step)
    tot_ref[...] = run[...].astype(BF)


def kv_call(steps, pos, pieces, xp, sums):
    n = xp.shape[2]
    return resident(
        functools.partial(kv_kernel, steps),
        [pos],
        [*pieces, xp, sums],
        [
            ((HL, n, DH), BF),
            ((HL, VA, n), BF),
            ((n // GROUP, HL, VA, DH), F32),
            ((HL, VA, DH), BF),
        ],
        [pltpu.VMEM((rows_in(steps), QCOL), BF), pltpu.VMEM((HL, VA, DH), F32)],
        20,
        "keys_values",
    )


def q_kernel(steps, pos, *refs):
    count = len(refs) - 4
    pieces, (x_ref, sum_ref, fq_ref, wbuf) = refs[:count], refs[count:]
    lay(steps, pieces, wbuf)

    def step(g, at):
        x = rows_of(pos, steps, x_ref, at)
        fq_ref[:, at] = feature(product(wbuf[:, : HL * DH], x) + sum_ref[:, at])

    each_group(x_ref.shape[2], step)


def q_call(steps, pos, pieces, xp, sums):
    (out,) = resident(
        functools.partial(q_kernel, steps),
        [pos],
        [*pieces, xp, sums],
        [(sums.shape, BF)],
        [pltpu.VMEM((rows_in(steps), COLS - QCOL), BF)],
        12,
        "queries",
    )
    return out


def mask_rows(code, j0, rows, t0, cols):
    parts = []
    for j in range(j0, j0 + rows // 64):
        t = lax.broadcasted_iota(jnp.int32, (64, cols), 1) + t0
        s = lax.broadcasted_iota(jnp.int32, (64, cols), 0)
        i = t >> 6
        bit = (jnp.full((64, cols), code, jnp.int32) >> (((i * (i - 1)) >> 1) + j)) & 1
        same = jnp.where(s <= (t & 63), 1, 0)
        keep = jnp.where(i > j, bit, jnp.where(i == j, same, 0))
        parts.append(keep.astype(F32).astype(BF))
    return jnp.concatenate(parts, axis=0)


def attend_kernel(codes, fk_ref, v_ref, fq_ref, num_ref):
    half = GROUP // 2

    def step(g, at):
        code = codes[g]
        start = pl.multiple_of(g * GROUP, GROUP)
        one, two = pl.ds(start, half), pl.ds(start + half, half)
        upper = mask_rows(code, 0, half, 0, GROUP)
        lower = mask_rows(code, 4, half, half, half)
        for h in range(HL):
            fq = fq_ref[h * DH : (h + 1) * DH, at]
            top = jnp.dot(fk_ref[h, one, :], fq, preferred_element_type=F32)
            top = top.astype(BF) * upper
            low = jnp.dot(fk_ref[h, two, :], fq[:, half:], preferred_element_type=F32)
            low = low.astype(BF) * lower
            num = jnp.dot(v_ref[h, :, one], top, preferred_element_type=F32)
            more = jnp.dot(v_ref[h, :, two], low, preferred_element_type=F32)
            num_ref[h, :, one] = num[:, :half]
            num_ref[h, :, two] = num[:, half:] + more

    each_group(fq_ref.shape[1], step)


def attend_call(codes, fk, v, fq):
    (out,) = resident(
        attend_kernel,
        [codes],
        [fk, v, fq],
        [((HL, VA, fq.shape[1]), F32)],
        [],
        12,
        "attend",
    )
    return out


def chip_kernel(tot_ref, other_ref, chip_ref):
    chip_ref[...] = (tot_ref[...].astype(F32) + other_ref[...].astype(F32)).astype(BF)


def row_kernel(a, b, c, d, row_ref):
    total = a[...].astype(F32) + b[...].astype(F32) + c[...].astype(F32) + d[...].astype(F32)
    row_ref[...] = total.astype(BF)


def small(kernel, args, name):
    (out,) = resident(kernel, [], args, [(args[0].shape, BF)], [], 4, name)
    return out


def join_kernel(pos, scale, *refs):
    other, near, far = refs[0], refs[1:4], refs[4:7]
    pre_ref, fq_ref, num_ref, out_ref, sq_ref, dev = refs[7:]
    total = far[0][...].astype(F32) + far[1][...].astype(F32) + far[2][...].astype(F32)
    total = total + jnp.where(pos[2] == 1, other[...].astype(F32), 0.0)
    for d, got in enumerate(near):
        total = total + jnp.where(pos[1] >= d + 1, got[...].astype(F32), 0.0)
    dev[...] = total

    def step(g, at):
        squares = jnp.zeros((1, GROUP), F32)
        for h in range(HL):
            prefix = (dev[h] + pre_ref[g, h]).astype(BF)
            fq = fq_ref[h * DH : (h + 1) * DH, at]
            num = num_ref[h, :, at] + jnp.dot(prefix, fq, preferred_element_type=F32)
            out = num[:DH, :] * (scale[h] / num[DH : DH + 1, :])
            out_ref[h * DH : (h + 1) * DH, at] = out
            squares = squares + jnp.sum(out * out, axis=0, keepdims=True)
        sq_ref[:, at] = squares

    each_group(fq_ref.shape[1], step)


def join_call(pos, scale, states, pre, fq, num):
    n = fq.shape[1]
    return resident(
        join_kernel,
        [pos, scale],
        [*states, pre, fq, num],
        [((HL * DH, n), F32), ((1, n), F32)],
        [pltpu.VMEM((HL, VA, DH), F32)],
        12,
        "join",
    )


def norm_kernel(out_ref, s0, s1, s2, s3, gain_ref, o_ref, buf, sem):
    eye = lax.broadcasted_iota(jnp.int32, (DH, DH), 0) == lax.broadcasted_iota(
        jnp.int32, (DH, DH), 1
    )
    gains = [
        jnp.sum(jnp.where(eye, gain_ref[h : h + 1, :], 0.0), axis=1, keepdims=True)
        for h in range(HL)
    ]
    copies = []
    for g in range(out_ref.shape[1] // GROUP):
        at = slice(g * GROUP, (g + 1) * GROUP)
        squares = s0[:, at] + s1[:, at] + s2[:, at] + s3[:, at]
        inv = lax.rsqrt(squares * (1.0 / (H * DH)) + 1e-06)
        for h in range(HL):
            rows = slice(h * DH, (h + 1) * DH)
            buf[rows, at] = (out_ref[rows, at] * inv * gains[h]).astype(BF)
        here = pl.ds(g * GROUP, GROUP)
        copies.append(pltpu.make_async_copy(buf.at[:, here], o_ref.at[:, here], sem.at[g]))
        copies[-1].start()
    for copy in copies:
        copy.wait()


def norm_call(out, squares, gain):
    n = out.shape[1]
    return pl.pallas_call(
        norm_kernel,
        in_specs=[pl.BlockSpec(memory_space=pltpu.VMEM)] * 6,
        out_specs=pl.BlockSpec(memory_space=pl.ANY),
        out_shape=jax.ShapeDtypeStruct((HL * DH, n), BF),
        scratch_shapes=[
            pltpu.VMEM((HL * DH, n), BF),
            pltpu.SemaphoreType.DMA((n // GROUP,)),
        ],
        compiler_params=pltpu.CompilerParams(vmem_limit_bytes=8 * MIB),
        cost_estimate=QUICK,
        name="norm",
    )(fast(out), *(fast(a) for a in squares), fast(gain))


def body(tokens, qkv_weight, block_mask, head_scale, norm_gain):
    me = lax.axis_index("tm").astype(jnp.int32)
    y, x, core = me // 8, (me // 2) % 4, me % 2
    pos = jnp.stack([y, x, core])
    pos, gain, xt = lax.optimization_barrier((pos, norm_gain.reshape(HL, DH), tokens.T))
    shards = [shift(qkv_weight, first_leg(d)) for d in (1, 2, 3)]
    xp, staged = spread(xt, qkv_weight)
    near_kv, near_q = pack(pos, [staged, *shards])
    own_kv = [near_kv] + [shift(near_kv, second_leg(d)) for d in (1, 2, 3)]
    sib_kv = [shift(near_kv, SIBLING)] + [None] * 3
    first_q = [near_q, shift(near_q, SIBLING)]

    def whole(mine, d):
        return (mine, d, 0, BLK)

    cut = 4 * 256 - 3 * BLK
    both = (whole(True, 0), whole(False, 0))
    beside = (whole(True, 1), whole(False, 1), whole(True, 3), (False, 3, 0, cut))
    across = (whole(True, 2), whole(False, 2), (False, 3, cut, BLK))
    rest = tuple(whole(mine, d) for mine in (True, False) for d in (1, 2, 3))
    half = HL * DH
    kv_sum = part_call(both, pos, [near_kv, sib_kv[0]], xp, 2 * half, name="part_kv")
    q_sum = part_call(both, pos, first_q, xp, half, name="part_q")
    own_kv[1], own_kv[3], kv_sum, q_sum = lax.optimization_barrier(
        (own_kv[1], own_kv[3], kv_sum, q_sum)
    )
    sib_kv[1], sib_kv[3] = shift(own_kv[1], SIBLING), shift(own_kv[3], SIBLING)
    kv_sum = part_call(
        beside,
        pos,
        [(own_kv if mine else sib_kv)[d] for mine, d, _, _ in beside],
        xp,
        2 * half,
        kv_sum,
        name="part_more",
    )
    near_q, own_kv[2], kv_sum = lax.optimization_barrier((near_q, own_kv[2], kv_sum))
    sib_kv[2] = shift(own_kv[2], SIBLING)
    own_q = [shift(near_q, second_leg(d)) for d in (1, 2, 3)]
    fk, v, pre, tot = kv_call(across, pos, [own_kv[2], sib_kv[2], sib_kv[3]], xp, kv_sum)

    other = shift(tot, SIBLING)
    *own_q, other = lax.optimization_barrier((*own_q, other))
    sib_q = [shift(a, SIBLING) for a in own_q]
    chip = small(chip_kernel, [tot, other], "chip")
    chip, q_sum = lax.optimization_barrier((chip, q_sum))
    fq = q_call(rest, pos, [*own_q, *sib_q], xp, q_sum)
    in_row = [shift(chip, along_x(d)) for d in (1, 2, 3)]
    *in_row, fq = lax.optimization_barrier((*in_row, fq))
    row = small(row_kernel, [chip, *in_row], "row")
    row, fq = lax.optimization_barrier((row, fq))
    num = attend_call(block_mask, fk, v, fq)
    above = [shift(row, later_y(d)) for d in (1, 2, 3)]

    out, squares = join_call(pos, head_scale, [other, *in_row, *above], pre, fq, num)
    squares = [squares] + [
        lax.ppermute(squares, "head", [(i, (i + d) % 4) for i in range(4)]) for d in (1, 2, 3)
    ]
    return norm_call(out, squares, gain).T


def solution(mesh):
    in_specs = (P("tm", None), P("tm", "head"), P("tm"), P("head"), P("head"))
    out_specs = P("tm", "head")
    return jax.shard_map(body, mesh=mesh, in_specs=in_specs, out_specs=out_specs, check_vma=False)
```

```python
import functools

import jax
import jax.numpy as jnp
from jax import lax
from jax.experimental import pallas as pl
from jax.experimental.pallas import tpu as pltpu
from jax.sharding import PartitionSpec as P

H = 20
DH = 112
GROUP = 512
D = 2240
HL = 5
SHARD = 70
PAD = 72
BLK = 4 * PAD
VA = 128
QCOL = 1152
COLS = 1792
BF = jnp.bfloat16
F32 = jnp.float32
MIB = 1 << 20
QUICK = pl.CostEstimate(flops=1, bytes_accessed=1, transcendentals=0)


def place(y, x, c):
    return (y % 4) * 8 + (x % 4) * 2 + c


def perm(move):
    return [
        (place(y, x, c), place(*move(y, x, c)))
        for y in range(4)
        for x in range(4)
        for c in range(2)
    ]


SIBLING = perm(lambda y, x, c: (y, x, 1 - c))


def first_leg(d):
    return perm(lambda y, x, c: (y, x + d, c) if c == 0 else (y + d, x, c))


def second_leg(d):
    return perm(lambda y, x, c: (y + d, x, c) if c == 0 else (y, x + d, c))


def along_x(d):
    return perm(lambda y, x, c: (y, x + d, c))


def later_y(d):
    return [
        (place(y, x, c), place(y + d, x, c))
        for y in range(4 - d)
        for x in range(4)
        for c in range(2)
    ]


def shift(a, moves):
    return lax.ppermute(a, "tm", moves)


def pack_kernel(pos, a0, a1, a2, a3, kv_ref, q_ref, wide):
    coord = jnp.where(pos[2] == 0, pos[1], pos[0])
    wide[...] = jnp.zeros_like(wide)
    for r, a in enumerate((a0, a1, a2, a3)):
        at = pl.multiple_of(((coord + 4 - r) & 3) * PAD, 8)
        shard = a[...].astype(F32)
        for kind, base in ((0, QCOL), (1, 0), (2, HL * DH)):
            for h in range(HL):
                col = h * 3 * DH + kind * DH
                to = base + h * DH
                wide[pl.ds(at, SHARD), to : to + DH] = shard[:, col : col + DH]
    kv_ref[...] = wide[:, :QCOL].astype(BF)
    q_ref[...] = wide[:, QCOL:].astype(BF)


def pack(pos, shards):
    return resident(
        pack_kernel,
        [pos],
        shards,
        [((BLK, QCOL), BF), ((BLK, COLS - QCOL), BF)],
        [pltpu.VMEM((BLK, COLS), F32)],
        10,
        "pack",
    )


def spread_kernel(x_ref, o_ref):
    gap = jnp.zeros((PAD - SHARD, x_ref.shape[1]), BF)
    for y in range(4):
        for x in range(4):
            for c in range(2):
                block, slot = (y, x) if c == 0 else (4 + x, y)
                dev = place(y, x, c)
                at = slot * PAD
                o_ref[block, at : at + SHARD, :] = x_ref[dev * SHARD : (dev + 1) * SHARD, :]
                o_ref[block, at + SHARD : at + PAD, :] = gap


def spread(xt):
    n = xt.shape[1]
    blk = 256
    return pl.pallas_call(
        spread_kernel,
        grid=(n // blk,),
        in_specs=[pl.BlockSpec((D, blk), lambda g: (0, g))],
        out_specs=pl.BlockSpec((8, BLK, blk), lambda g: (0, 0, g)),
        out_shape=jax.ShapeDtypeStruct((8, BLK, n), BF),
        compiler_params=pltpu.CompilerParams(vmem_limit_bytes=8 * MIB),
        cost_estimate=QUICK,
        name="spread",
    )(xt)


def product(w, x):
    return lax.dot_general(w, x, (((0,), (0,)), ((), ())), preferred_element_type=F32)


def fast(a):
    return pltpu.with_memory_space_constraint(a, pltpu.VMEM)


def lay(pieces, wbuf):
    for i, piece in enumerate(pieces):
        wbuf[i * BLK : (i + 1) * BLK, :] = piece[...]


def block(pos, mine, d):
    which = pos[2] if mine else 1 - pos[2]
    return which * 4 + ((jnp.where(which == 0, pos[0], pos[1]) + 4 - d) & 3)


def rows_of(pos, steps, x_ref, at):
    return jnp.concatenate([x_ref[block(pos, *step), :, at] for step in steps], axis=0)


def each_group(n, step):
    for g in range(n // GROUP):
        step(g, pl.ds(g * GROUP, GROUP))


def resident(kernel, small, large, outs, scratch, limit, name, alias=None):
    return pl.pallas_call(
        kernel,
        in_specs=[pl.BlockSpec(memory_space=pltpu.SMEM)] * len(small)
        + [pl.BlockSpec(memory_space=pltpu.VMEM)] * len(large),
        out_specs=[pl.BlockSpec(memory_space=pltpu.VMEM)] * len(outs),
        out_shape=[pltpu.VMEM(shape, kind) for shape, kind in outs],
        scratch_shapes=scratch,
        input_output_aliases=alias or {},
        compiler_params=pltpu.CompilerParams(vmem_limit_bytes=limit * MIB),
        cost_estimate=QUICK,
        name=name,
    )(*small, *(fast(a) for a in large))


def part_kernel(steps, pos, *refs):
    count = len(steps)
    kv_pieces, q_pieces = refs[:count], refs[count : 2 * count]
    x_ref, kv_ref, q_ref, kv_buf, q_buf = refs[2 * count :]
    lay(kv_pieces, kv_buf)
    lay(q_pieces, q_buf)

    def step(g, at):
        x = rows_of(pos, steps, x_ref, at)
        kv_ref[:, at] = product(kv_buf[:, : 2 * HL * DH], x)
        q_ref[:, at] = product(q_buf[:, : HL * DH], x)

    each_group(x_ref.shape[2], step)


def part_call(steps, pos, kv_pieces, q_pieces, xp):
    n = xp.shape[2]
    return resident(
        functools.partial(part_kernel, steps),
        [pos],
        [*kv_pieces, *q_pieces, xp],
        [((2 * HL * DH, n), F32), ((HL * DH, n), F32)],
        [
            pltpu.VMEM((len(steps) * BLK, QCOL), BF),
            pltpu.VMEM((len(steps) * BLK, COLS - QCOL), BF),
        ],
        16,
        "part_first",
    )


def feature(raw):
    a = raw.astype(BF).astype(F32)
    return jnp.where(a > 0, a + 1.0, jnp.exp(jnp.minimum(a, 0.0))).astype(BF)


def kv_kernel(steps, pos, *refs):
    count = len(refs) - 8
    pieces = refs[:count]
    x_ref, sum_ref, fk_ref, v_ref, pre_ref, tot_ref, wbuf, run = refs[count:]
    lay(pieces, wbuf)
    run[...] = jnp.zeros_like(run)
    half = HL * DH

    def step(g, at):
        x = rows_of(pos, steps, x_ref, at)
        raw = product(wbuf[:, : 2 * half], x) + sum_ref[:, at]
        fk = feature(raw[:half, :])
        tail = (lax.broadcasted_iota(jnp.int32, (VA - DH, GROUP), 0) == 0).astype(F32).astype(BF)
        for h in range(HL):
            kn = fk[h * DH : (h + 1) * DH, :].T
            fk_ref[h, at, :] = kn
            val = raw[half + h * DH : half + (h + 1) * DH, :].astype(BF)
            va = jnp.concatenate([val, tail], axis=0)
            v_ref[h, :, at] = va
            state = jnp.dot(va, kn, preferred_element_type=F32)
            before = run[h]
            pre_ref[g, h] = before
            run[h] = before + state

    each_group(x_ref.shape[2], step)
    tot_ref[...] = run[...].astype(BF)


def kv_call(steps, pos, pieces, xp, sums):
    n = xp.shape[2]
    return resident(
        functools.partial(kv_kernel, steps),
        [pos],
        [*pieces, xp, sums],
        [
            ((HL, n, DH), BF),
            ((HL, VA, n), BF),
            ((n // GROUP, HL, VA, DH), F32),
            ((HL, VA, DH), BF),
        ],
        [pltpu.VMEM((len(pieces) * BLK, QCOL), BF), pltpu.VMEM((HL, VA, DH), F32)],
        20,
        "keys_values",
    )


def q_kernel(steps, pos, *refs):
    count = len(refs) - 4
    pieces, (x_ref, sum_ref, fq_ref, wbuf) = refs[:count], refs[count:]
    lay(pieces, wbuf)

    def step(g, at):
        x = rows_of(pos, steps, x_ref, at)
        fq_ref[:, at] = feature(product(wbuf[:, : HL * DH], x) + sum_ref[:, at])

    each_group(x_ref.shape[2], step)


def q_call(steps, pos, pieces, xp, sums):
    (out,) = resident(
        functools.partial(q_kernel, steps),
        [pos],
        [*pieces, xp, sums],
        [(sums.shape, BF)],
        [pltpu.VMEM((len(pieces) * BLK, COLS - QCOL), BF)],
        12,
        "queries",
    )
    return out


def mask_rows(code, j0, rows, t0, cols):
    parts = []
    for j in range(j0, j0 + rows // 64):
        t = lax.broadcasted_iota(jnp.int32, (64, cols), 1) + t0
        s = lax.broadcasted_iota(jnp.int32, (64, cols), 0)
        i = t >> 6
        bit = (jnp.full((64, cols), code, jnp.int32) >> (((i * (i - 1)) >> 1) + j)) & 1
        same = jnp.where(s <= (t & 63), 1, 0)
        keep = jnp.where(i > j, bit, jnp.where(i == j, same, 0))
        parts.append(keep.astype(F32).astype(BF))
    return jnp.concatenate(parts, axis=0)


def attend_kernel(codes, fk_ref, v_ref, fq_ref, num_ref):
    half = GROUP // 2

    def step(g, at):
        code = codes[g]
        start = g * GROUP
        one, two = pl.ds(start, half), pl.ds(start + half, half)
        upper = mask_rows(code, 0, half, 0, GROUP)
        lower = mask_rows(code, 4, half, half, half)
        for h in range(HL):
            fq = fq_ref[h * DH : (h + 1) * DH, at]
            top = jnp.dot(fk_ref[h, one, :], fq, preferred_element_type=F32)
            top = top.astype(BF) * upper
            low = jnp.dot(fk_ref[h, two, :], fq[:, half:], preferred_element_type=F32)
            low = low.astype(BF) * lower
            num = jnp.dot(v_ref[h, :, one], top, preferred_element_type=F32)
            more = jnp.dot(v_ref[h, :, two], low, preferred_element_type=F32)
            num_ref[h, :, one] = num[:, :half]
            num_ref[h, :, two] = num[:, half:] + more

    each_group(fq_ref.shape[1], step)


def attend_call(codes, fk, v, fq):
    (out,) = resident(
        attend_kernel,
        [codes],
        [fk, v, fq],
        [((HL, VA, fq.shape[1]), F32)],
        [],
        12,
        "attend",
    )
    return out


def chip_kernel(tot_ref, other_ref, chip_ref):
    chip_ref[...] = (tot_ref[...].astype(F32) + other_ref[...].astype(F32)).astype(BF)


def row_kernel(a, b, c, d, row_ref):
    total = a[...].astype(F32) + b[...].astype(F32) + c[...].astype(F32) + d[...].astype(F32)
    row_ref[...] = total.astype(BF)


def small(kernel, args, name):
    (out,) = resident(kernel, [], args, [(args[0].shape, BF)], [], 4, name)
    return out


def join_kernel(pos, scale, *refs):
    other, near, far = refs[0], refs[1:4], refs[4:7]
    pre_ref, fq_ref, num_ref, out_ref, sq_ref, dev = refs[7:]
    total = far[0][...].astype(F32) + far[1][...].astype(F32) + far[2][...].astype(F32)
    total = total + jnp.where(pos[2] == 1, other[...].astype(F32), 0.0)
    for d, got in enumerate(near):
        total = total + jnp.where(pos[1] >= d + 1, got[...].astype(F32), 0.0)
    dev[...] = total

    def step(g, at):
        squares = jnp.zeros((1, GROUP), F32)
        for h in range(HL):
            prefix = (dev[h] + pre_ref[g, h]).astype(BF)
            fq = fq_ref[h * DH : (h + 1) * DH, at]
            num = num_ref[h, :, at] + jnp.dot(prefix, fq, preferred_element_type=F32)
            out = num[:DH, :] * (scale[h] / num[DH : DH + 1, :])
            out_ref[h * DH : (h + 1) * DH, at] = out
            squares = squares + jnp.sum(out * out, axis=0, keepdims=True)
        sq_ref[:, at] = squares

    each_group(fq_ref.shape[1], step)


def join_call(pos, scale, states, pre, fq, num):
    n = fq.shape[1]
    return resident(
        join_kernel,
        [pos, scale],
        [*states, pre, fq, num],
        [((HL * DH, n), F32), ((1, n), F32)],
        [pltpu.VMEM((HL, VA, DH), F32)],
        12,
        "join",
    )


def norm_kernel(out_ref, s0, s1, s2, s3, gain_ref, o_ref, buf, sem):
    eye = lax.broadcasted_iota(jnp.int32, (DH, DH), 0) == lax.broadcasted_iota(
        jnp.int32, (DH, DH), 1
    )
    gains = [
        jnp.sum(jnp.where(eye, gain_ref[h : h + 1, :], 0.0), axis=1, keepdims=True)
        for h in range(HL)
    ]
    copies = []
    for g in range(out_ref.shape[1] // GROUP):
        at = slice(g * GROUP, (g + 1) * GROUP)
        squares = s0[:, at] + s1[:, at] + s2[:, at] + s3[:, at]
        inv = lax.rsqrt(squares * (1.0 / (H * DH)) + 1e-06)
        for h in range(HL):
            rows = slice(h * DH, (h + 1) * DH)
            buf[rows, at] = (out_ref[rows, at] * inv * gains[h]).astype(BF)
        here = pl.ds(g * GROUP, GROUP)
        copies.append(pltpu.make_async_copy(buf.at[:, here], o_ref.at[:, here], sem.at[g]))
        copies[-1].start()
    for copy in copies:
        copy.wait()


def norm_call(out, squares, gain):
    n = out.shape[1]
    return pl.pallas_call(
        norm_kernel,
        in_specs=[pl.BlockSpec(memory_space=pltpu.VMEM)] * 6,
        out_specs=pl.BlockSpec(memory_space=pl.ANY),
        out_shape=jax.ShapeDtypeStruct((HL * DH, n), BF),
        scratch_shapes=[
            pltpu.VMEM((HL * DH, n), BF),
            pltpu.SemaphoreType.DMA((n // GROUP,)),
        ],
        compiler_params=pltpu.CompilerParams(vmem_limit_bytes=8 * MIB),
        cost_estimate=QUICK,
        name="norm",
    )(fast(out), *(fast(a) for a in squares), fast(gain))


def body(tokens, qkv_weight, block_mask, head_scale, norm_gain):
    me = lax.axis_index("tm").astype(jnp.int32)
    y, x, core = me // 8, (me // 2) % 4, me % 2
    pos = jnp.stack([y, x, core])
    pos, gain = lax.optimization_barrier((pos, norm_gain.reshape(HL, DH)))
    shards = [qkv_weight] + [shift(qkv_weight, first_leg(d)) for d in (1, 2, 3)]
    near_kv, near_q = pack(pos, shards)
    near_kv, xt = lax.optimization_barrier((near_kv, tokens.T))
    own_kv = [near_kv] + [shift(near_kv, second_leg(d)) for d in (1, 2, 3)]
    sib_kv, first_q = [shift(near_kv, SIBLING)], [near_q, shift(near_q, SIBLING)]
    xp = spread(pltpu.with_memory_space_constraint(xt, pltpu.HBM))

    both = ((True, 0), (False, 0))
    mine = tuple((True, d) for d in (1, 2, 3))
    last = tuple((False, d) for d in (1, 2, 3))
    kv_sum, q_sum = part_call(both, pos, [near_kv, sib_kv[0]], first_q, xp)
    near_q, kv_sum, q_sum = lax.optimization_barrier((near_q, kv_sum, q_sum))
    own_q = [shift(near_q, second_leg(d)) for d in (1, 2, 3)]
    *own_kv, kv_sum = lax.optimization_barrier((*own_kv, kv_sum))
    sib_kv = [shift(a, SIBLING) for a in own_kv[1:]]
    fk, v, pre, tot = kv_call(mine + last, pos, [*own_kv[1:], *sib_kv], xp, kv_sum)

    other = shift(tot, SIBLING)
    *own_q, other = lax.optimization_barrier((*own_q, other))
    sib_q = [shift(a, SIBLING) for a in own_q]
    chip = small(chip_kernel, [tot, other], "chip")
    chip, q_sum = lax.optimization_barrier((chip, q_sum))
    fq = q_call(mine + last, pos, [*own_q, *sib_q], xp, q_sum)
    in_row = [shift(chip, along_x(d)) for d in (1, 2, 3)]
    *in_row, fq = lax.optimization_barrier((*in_row, fq))
    row = small(row_kernel, [chip, *in_row], "row")
    row, fq = lax.optimization_barrier((row, fq))
    num = attend_call(block_mask, fk, v, fq)
    above = [shift(row, later_y(d)) for d in (1, 2, 3)]

    out, squares = join_call(pos, head_scale, [other, *in_row, *above], pre, fq, num)
    squares = [squares] + [
        lax.ppermute(squares, "head", [(i, (i + d) % 4) for i in range(4)]) for d in (1, 2, 3)
    ]
    return norm_call(out, squares, gain).T


def solution(mesh):
    in_specs = (P("tm", None), P("tm", "head"), P("tm"), P("head"), P("head"))
    out_specs = P("tm", "head")
    return jax.shard_map(body, mesh=mesh, in_specs=in_specs, out_specs=out_specs, check_vma=False)
```

```python
import functools

import jax
import jax.numpy as jnp
from jax import lax
from jax.experimental import pallas as pl
from jax.experimental.pallas import tpu as pltpu
from jax.sharding import PartitionSpec as P

H = 20
DH = 112
GROUP = 512
D = 2240
HL = 5
SHARD = 70
PAD = 72
BLK = 4 * PAD
VA = 128
QCOL = 1152
COLS = 1792
BF = jnp.bfloat16
F32 = jnp.float32
MIB = 1 << 20
QUICK = pl.CostEstimate(flops=1, bytes_accessed=1, transcendentals=0)


def place(y, x, c):
    return (y % 4) * 8 + (x % 4) * 2 + c


def perm(move):
    return [
        (place(y, x, c), place(*move(y, x, c)))
        for y in range(4)
        for x in range(4)
        for c in range(2)
    ]


SIBLING = perm(lambda y, x, c: (y, x, 1 - c))


def first_leg(d):
    return perm(lambda y, x, c: (y, x + d, c) if c == 0 else (y + d, x, c))


def second_leg(d):
    return perm(lambda y, x, c: (y + d, x, c) if c == 0 else (y, x + d, c))


def along_x(d):
    return perm(lambda y, x, c: (y, x + d, c))


def later_y(d):
    return [
        (place(y, x, c), place(y + d, x, c))
        for y in range(4 - d)
        for x in range(4)
        for c in range(2)
    ]


def shift(a, moves):
    return lax.ppermute(a, "tm", moves)


def pack_kernel(pos, a0, a1, a2, a3, kv_ref, q_ref, wide):
    coord = jnp.where(pos[2] == 0, pos[1], pos[0])
    wide[...] = jnp.zeros_like(wide)
    for r, a in enumerate((a0, a1, a2, a3)):
        at = pl.multiple_of(((coord + 4 - r) & 3) * PAD, 8)
        shard = a[...].astype(F32)
        for kind, base in ((0, QCOL), (1, 0), (2, HL * DH)):
            for h in range(HL):
                col = h * 3 * DH + kind * DH
                to = base + h * DH
                wide[pl.ds(at, SHARD), to : to + DH] = shard[:, col : col + DH]
    kv_ref[...] = wide[:, :QCOL].astype(BF)
    q_ref[...] = wide[:, QCOL:].astype(BF)


def pack(pos, shards):
    return resident(
        pack_kernel,
        [pos],
        shards,
        [((BLK, QCOL), BF), ((BLK, COLS - QCOL), BF)],
        [pltpu.VMEM((BLK, COLS), F32)],
        10,
        "pack",
    )


def stage_kernel(w_ref, o_ref, sem):
    copy = pltpu.make_async_copy(w_ref, o_ref, sem)
    copy.start()
    copy.wait()


def stage(w):
    return pl.pallas_call(
        stage_kernel,
        in_specs=[pl.BlockSpec(memory_space=pl.ANY)],
        out_specs=pl.BlockSpec(memory_space=pltpu.VMEM),
        out_shape=pltpu.VMEM(w.shape, w.dtype),
        scratch_shapes=[pltpu.SemaphoreType.DMA],
        compiler_params=pltpu.CompilerParams(vmem_limit_bytes=4 * MIB),
        cost_estimate=QUICK,
        name="stage",
    )(pltpu.with_memory_space_constraint(w, pltpu.HBM))


def spread_kernel(x_ref, o_ref):
    gap = jnp.zeros((PAD - SHARD, x_ref.shape[1]), BF)
    for y in range(4):
        for x in range(4):
            for c in range(2):
                block, slot = (y, x) if c == 0 else (4 + x, y)
                dev = place(y, x, c)
                at = slot * PAD
                o_ref[block, at : at + SHARD, :] = x_ref[dev * SHARD : (dev + 1) * SHARD, :]
                o_ref[block, at + SHARD : at + PAD, :] = gap


def spread(xt):
    n = xt.shape[1]
    blk = 256
    return pl.pallas_call(
        spread_kernel,
        grid=(n // blk,),
        in_specs=[pl.BlockSpec((D, blk), lambda g: (0, g))],
        out_specs=pl.BlockSpec((8, BLK, blk), lambda g: (0, 0, g)),
        out_shape=jax.ShapeDtypeStruct((8, BLK, n), BF),
        compiler_params=pltpu.CompilerParams(vmem_limit_bytes=8 * MIB),
        cost_estimate=QUICK,
        name="spread",
    )(xt)


def product(w, x):
    return lax.dot_general(w, x, (((0,), (0,)), ((), ())), preferred_element_type=F32)


def fast(a):
    return pltpu.with_memory_space_constraint(a, pltpu.VMEM)


def lay(pieces, wbuf):
    for i, piece in enumerate(pieces):
        wbuf[i * BLK : (i + 1) * BLK, :] = piece[...]


def block(pos, mine, d):
    which = pos[2] if mine else 1 - pos[2]
    return which * 4 + ((jnp.where(which == 0, pos[0], pos[1]) + 4 - d) & 3)


def rows_of(pos, steps, x_ref, at):
    return jnp.concatenate([x_ref[block(pos, *step), :, at] for step in steps], axis=0)


def each_group(n, step):
    for g in range(n // GROUP):
        step(g, pl.ds(g * GROUP, GROUP))


def resident(kernel, small, large, outs, scratch, limit, name, alias=None):
    return pl.pallas_call(
        kernel,
        in_specs=[pl.BlockSpec(memory_space=pltpu.SMEM)] * len(small)
        + [pl.BlockSpec(memory_space=pltpu.VMEM)] * len(large),
        out_specs=[pl.BlockSpec(memory_space=pltpu.VMEM)] * len(outs),
        out_shape=[pltpu.VMEM(shape, kind) for shape, kind in outs],
        scratch_shapes=scratch,
        input_output_aliases=alias or {},
        compiler_params=pltpu.CompilerParams(vmem_limit_bytes=limit * MIB),
        cost_estimate=QUICK,
        name=name,
    )(*small, *(fast(a) for a in large))


def part_kernel(steps, pos, *refs):
    count = len(steps)
    kv_pieces, q_pieces = refs[:count], refs[count : 2 * count]
    x_ref, kv_ref, q_ref, kv_buf, q_buf = refs[2 * count :]
    lay(kv_pieces, kv_buf)
    lay(q_pieces, q_buf)

    def step(g, at):
        x = rows_of(pos, steps, x_ref, at)
        kv_ref[:, at] = product(kv_buf[:, : 2 * HL * DH], x)
        q_ref[:, at] = product(q_buf[:, : HL * DH], x)

    each_group(x_ref.shape[2], step)


def part_call(steps, pos, kv_pieces, q_pieces, xp):
    n = xp.shape[2]
    return resident(
        functools.partial(part_kernel, steps),
        [pos],
        [*kv_pieces, *q_pieces, xp],
        [((2 * HL * DH, n), F32), ((HL * DH, n), F32)],
        [
            pltpu.VMEM((len(steps) * BLK, QCOL), BF),
            pltpu.VMEM((len(steps) * BLK, COLS - QCOL), BF),
        ],
        16,
        "part_first",
    )


def feature(raw):
    a = raw.astype(BF).astype(F32)
    return jnp.where(a > 0, a + 1.0, jnp.exp(jnp.minimum(a, 0.0))).astype(BF)


def kv_kernel(steps, pos, *refs):
    count = len(refs) - 8
    pieces = refs[:count]
    x_ref, sum_ref, fk_ref, v_ref, pre_ref, tot_ref, wbuf, run = refs[count:]
    lay(pieces, wbuf)
    run[...] = jnp.zeros_like(run)
    half = HL * DH

    def step(g, at):
        x = rows_of(pos, steps, x_ref, at)
        raw = product(wbuf[:, : 2 * half], x) + sum_ref[:, at]
        fk = feature(raw[:half, :])
        tail = (lax.broadcasted_iota(jnp.int32, (VA - DH, GROUP), 0) == 0).astype(F32).astype(BF)
        for h in range(HL):
            kn = fk[h * DH : (h + 1) * DH, :].T
            fk_ref[h, at, :] = kn
            val = raw[half + h * DH : half + (h + 1) * DH, :].astype(BF)
            va = jnp.concatenate([val, tail], axis=0)
            v_ref[h, :, at] = va
            state = jnp.dot(va, kn, preferred_element_type=F32)
            before = run[h]
            pre_ref[g, h] = before
            run[h] = before + state

    each_group(x_ref.shape[2], step)
    tot_ref[...] = run[...].astype(BF)


def kv_call(steps, pos, pieces, xp, sums):
    n = xp.shape[2]
    return resident(
        functools.partial(kv_kernel, steps),
        [pos],
        [*pieces, xp, sums],
        [
            ((HL, n, DH), BF),
            ((HL, VA, n), BF),
            ((n // GROUP, HL, VA, DH), F32),
            ((HL, VA, DH), BF),
        ],
        [pltpu.VMEM((len(pieces) * BLK, QCOL), BF), pltpu.VMEM((HL, VA, DH), F32)],
        20,
        "keys_values",
    )


def q_kernel(steps, pos, *refs):
    count = len(refs) - 4
    pieces, (x_ref, sum_ref, fq_ref, wbuf) = refs[:count], refs[count:]
    lay(pieces, wbuf)

    def step(g, at):
        x = rows_of(pos, steps, x_ref, at)
        fq_ref[:, at] = feature(product(wbuf[:, : HL * DH], x) + sum_ref[:, at])

    each_group(x_ref.shape[2], step)


def q_call(steps, pos, pieces, xp, sums):
    (out,) = resident(
        functools.partial(q_kernel, steps),
        [pos],
        [*pieces, xp, sums],
        [(sums.shape, BF)],
        [pltpu.VMEM((len(pieces) * BLK, COLS - QCOL), BF)],
        12,
        "queries",
    )
    return out


def mask_rows(code, j0, rows, t0, cols):
    parts = []
    for j in range(j0, j0 + rows // 64):
        t = lax.broadcasted_iota(jnp.int32, (64, cols), 1) + t0
        s = lax.broadcasted_iota(jnp.int32, (64, cols), 0)
        i = t >> 6
        bit = (jnp.full((64, cols), code, jnp.int32) >> (((i * (i - 1)) >> 1) + j)) & 1
        same = jnp.where(s <= (t & 63), 1, 0)
        keep = jnp.where(i > j, bit, jnp.where(i == j, same, 0))
        parts.append(keep.astype(F32).astype(BF))
    return jnp.concatenate(parts, axis=0)


def attend_kernel(codes, fk_ref, v_ref, fq_ref, num_ref):
    half = GROUP // 2

    def step(g, at):
        code = codes[g]
        start = g * GROUP
        one, two = pl.ds(start, half), pl.ds(start + half, half)
        upper = mask_rows(code, 0, half, 0, GROUP)
        lower = mask_rows(code, 4, half, half, half)
        for h in range(HL):
            fq = fq_ref[h * DH : (h + 1) * DH, at]
            top = jnp.dot(fk_ref[h, one, :], fq, preferred_element_type=F32)
            top = top.astype(BF) * upper
            low = jnp.dot(fk_ref[h, two, :], fq[:, half:], preferred_element_type=F32)
            low = low.astype(BF) * lower
            num = jnp.dot(v_ref[h, :, one], top, preferred_element_type=F32)
            more = jnp.dot(v_ref[h, :, two], low, preferred_element_type=F32)
            num_ref[h, :, one] = num[:, :half]
            num_ref[h, :, two] = num[:, half:] + more

    each_group(fq_ref.shape[1], step)


def attend_call(codes, fk, v, fq):
    (out,) = resident(
        attend_kernel,
        [codes],
        [fk, v, fq],
        [((HL, VA, fq.shape[1]), F32)],
        [],
        12,
        "attend",
    )
    return out


def chip_kernel(tot_ref, other_ref, chip_ref):
    chip_ref[...] = (tot_ref[...].astype(F32) + other_ref[...].astype(F32)).astype(BF)


def row_kernel(a, b, c, d, row_ref):
    total = a[...].astype(F32) + b[...].astype(F32) + c[...].astype(F32) + d[...].astype(F32)
    row_ref[...] = total.astype(BF)


def small(kernel, args, name):
    (out,) = resident(kernel, [], args, [(args[0].shape, BF)], [], 4, name)
    return out


def join_kernel(pos, scale, *refs):
    other, near, far = refs[0], refs[1:4], refs[4:7]
    pre_ref, fq_ref, num_ref, out_ref, sq_ref, dev = refs[7:]
    total = far[0][...].astype(F32) + far[1][...].astype(F32) + far[2][...].astype(F32)
    total = total + jnp.where(pos[2] == 1, other[...].astype(F32), 0.0)
    for d, got in enumerate(near):
        total = total + jnp.where(pos[1] >= d + 1, got[...].astype(F32), 0.0)
    dev[...] = total

    def step(g, at):
        squares = jnp.zeros((1, GROUP), F32)
        for h in range(HL):
            prefix = (dev[h] + pre_ref[g, h]).astype(BF)
            fq = fq_ref[h * DH : (h + 1) * DH, at]
            num = num_ref[h, :, at] + jnp.dot(prefix, fq, preferred_element_type=F32)
            out = num[:DH, :] * (scale[h] / num[DH : DH + 1, :])
            out_ref[h * DH : (h + 1) * DH, at] = out
            squares = squares + jnp.sum(out * out, axis=0, keepdims=True)
        sq_ref[:, at] = squares

    each_group(fq_ref.shape[1], step)


def join_call(pos, scale, states, pre, fq, num):
    n = fq.shape[1]
    return resident(
        join_kernel,
        [pos, scale],
        [*states, pre, fq, num],
        [((HL * DH, n), F32), ((1, n), F32)],
        [pltpu.VMEM((HL, VA, DH), F32)],
        12,
        "join",
    )


def norm_kernel(out_ref, s0, s1, s2, s3, gain_ref, o_ref, buf, sem):
    eye = lax.broadcasted_iota(jnp.int32, (DH, DH), 0) == lax.broadcasted_iota(
        jnp.int32, (DH, DH), 1
    )
    gains = [
        jnp.sum(jnp.where(eye, gain_ref[h : h + 1, :], 0.0), axis=1, keepdims=True)
        for h in range(HL)
    ]
    copies = []
    for g in range(out_ref.shape[1] // GROUP):
        at = slice(g * GROUP, (g + 1) * GROUP)
        squares = s0[:, at] + s1[:, at] + s2[:, at] + s3[:, at]
        inv = lax.rsqrt(squares * (1.0 / (H * DH)) + 1e-06)
        for h in range(HL):
            rows = slice(h * DH, (h + 1) * DH)
            buf[rows, at] = (out_ref[rows, at] * inv * gains[h]).astype(BF)
        here = pl.ds(g * GROUP, GROUP)
        copies.append(pltpu.make_async_copy(buf.at[:, here], o_ref.at[:, here], sem.at[g]))
        copies[-1].start()
    for copy in copies:
        copy.wait()


def norm_call(out, squares, gain):
    n = out.shape[1]
    return pl.pallas_call(
        norm_kernel,
        in_specs=[pl.BlockSpec(memory_space=pltpu.VMEM)] * 6,
        out_specs=pl.BlockSpec(memory_space=pl.ANY),
        out_shape=jax.ShapeDtypeStruct((HL * DH, n), BF),
        scratch_shapes=[
            pltpu.VMEM((HL * DH, n), BF),
            pltpu.SemaphoreType.DMA((n // GROUP,)),
        ],
        compiler_params=pltpu.CompilerParams(vmem_limit_bytes=8 * MIB),
        cost_estimate=QUICK,
        name="norm",
    )(fast(out), *(fast(a) for a in squares), fast(gain))


def body(tokens, qkv_weight, block_mask, head_scale, norm_gain):
    me = lax.axis_index("tm").astype(jnp.int32)
    y, x, core = me // 8, (me // 2) % 4, me % 2
    pos = jnp.stack([y, x, core])
    pos, gain = lax.optimization_barrier((pos, norm_gain.reshape(HL, DH)))
    shards = [stage(qkv_weight)] + [shift(qkv_weight, first_leg(d)) for d in (1, 2, 3)]
    near_kv, near_q = pack(pos, shards)
    near_kv, xt = lax.optimization_barrier((near_kv, tokens.T))
    own_kv = [near_kv] + [shift(near_kv, second_leg(d)) for d in (1, 2, 3)]
    sib_kv, first_q = [shift(near_kv, SIBLING)], [near_q, shift(near_q, SIBLING)]
    xp = spread(pltpu.with_memory_space_constraint(xt, pltpu.HBM))

    both = ((True, 0), (False, 0))
    mine = tuple((True, d) for d in (1, 2, 3))
    last = tuple((False, d) for d in (1, 2, 3))
    kv_sum, q_sum = part_call(both, pos, [near_kv, sib_kv[0]], first_q, xp)
    near_q, kv_sum, q_sum = lax.optimization_barrier((near_q, kv_sum, q_sum))
    own_q = [shift(near_q, second_leg(d)) for d in (1, 2, 3)]
    *own_kv, kv_sum = lax.optimization_barrier((*own_kv, kv_sum))
    sib_kv = [shift(a, SIBLING) for a in own_kv[1:]]
    fk, v, pre, tot = kv_call(mine + last, pos, [*own_kv[1:], *sib_kv], xp, kv_sum)

    other = shift(tot, SIBLING)
    *own_q, other = lax.optimization_barrier((*own_q, other))
    sib_q = [shift(a, SIBLING) for a in own_q]
    chip = small(chip_kernel, [tot, other], "chip")
    chip, q_sum = lax.optimization_barrier((chip, q_sum))
    fq = q_call(mine + last, pos, [*own_q, *sib_q], xp, q_sum)
    in_row = [shift(chip, along_x(d)) for d in (1, 2, 3)]
    *in_row, fq = lax.optimization_barrier((*in_row, fq))
    row = small(row_kernel, [chip, *in_row], "row")
    row, fq = lax.optimization_barrier((row, fq))
    num = attend_call(block_mask, fk, v, fq)
    above = [shift(row, later_y(d)) for d in (1, 2, 3)]

    out, squares = join_call(pos, head_scale, [other, *in_row, *above], pre, fq, num)
    squares = [squares] + [
        lax.ppermute(squares, "head", [(i, (i + d) % 4) for i in range(4)]) for d in (1, 2, 3)
    ]
    return norm_call(out, squares, gain).T


def solution(mesh):
    in_specs = (P("tm", None), P("tm", "head"), P("tm"), P("head"), P("head"))
    out_specs = P("tm", "head")
    return jax.shard_map(body, mesh=mesh, in_specs=in_specs, out_specs=out_specs, check_vma=False)
```

```python
import functools

import jax
import jax.numpy as jnp
from jax import lax
from jax.experimental import pallas as pl
from jax.experimental.pallas import tpu as pltpu
from jax.sharding import PartitionSpec as P

H = 20
DH = 112
GROUP = 512
D = 2240
HL = 5
SHARD = 70
PAD = 72
BLK = 4 * PAD
VA = 128
QCOL = 1152
COLS = 1792
BF = jnp.bfloat16
F32 = jnp.float32
MIB = 1 << 20
QUICK = pl.CostEstimate(flops=1, bytes_accessed=1, transcendentals=0)


def place(y, x, c):
    return (y % 4) * 8 + (x % 4) * 2 + c


def perm(move):
    return [
        (place(y, x, c), place(*move(y, x, c)))
        for y in range(4)
        for x in range(4)
        for c in range(2)
    ]


SIBLING = perm(lambda y, x, c: (y, x, 1 - c))


def first_leg(d):
    return perm(lambda y, x, c: (y, x + d, c) if c == 0 else (y + d, x, c))


def second_leg(d):
    return perm(lambda y, x, c: (y + d, x, c) if c == 0 else (y, x + d, c))


def along_x(d):
    return perm(lambda y, x, c: (y, x + d, c))


def later_y(d):
    return [
        (place(y, x, c), place(y + d, x, c))
        for y in range(4 - d)
        for x in range(4)
        for c in range(2)
    ]


def shift(a, moves):
    return lax.ppermute(a, "tm", moves)


def pack_kernel(pos, a0, a1, a2, a3, kv_ref, q_ref, wide):
    coord = jnp.where(pos[2] == 0, pos[1], pos[0])
    wide[...] = jnp.zeros_like(wide)
    for r, a in enumerate((a0, a1, a2, a3)):
        at = pl.multiple_of(((coord + 4 - r) & 3) * PAD, 8)
        shard = a[...].astype(F32)
        for kind, base in ((0, QCOL), (1, 0), (2, HL * DH)):
            for h in range(HL):
                col = h * 3 * DH + kind * DH
                to = base + h * DH
                wide[pl.ds(at, SHARD), to : to + DH] = shard[:, col : col + DH]
    kv_ref[...] = wide[:, :QCOL].astype(BF)
    q_ref[...] = wide[:, QCOL:].astype(BF)


def pack(pos, shards):
    return resident(
        pack_kernel,
        [pos],
        shards,
        [((BLK, QCOL), BF), ((BLK, COLS - QCOL), BF)],
        [pltpu.VMEM((BLK, COLS), F32)],
        10,
        "pack",
    )


def stage_kernel(w_ref, o_ref, sem):
    copy = pltpu.make_async_copy(w_ref, o_ref, sem)
    copy.start()
    copy.wait()


def stage(w):
    return pl.pallas_call(
        stage_kernel,
        in_specs=[pl.BlockSpec(memory_space=pl.ANY)],
        out_specs=pl.BlockSpec(memory_space=pltpu.VMEM),
        out_shape=pltpu.VMEM(w.shape, w.dtype),
        scratch_shapes=[pltpu.SemaphoreType.DMA],
        compiler_params=pltpu.CompilerParams(vmem_limit_bytes=4 * MIB),
        cost_estimate=QUICK,
        name="stage",
    )(pltpu.with_memory_space_constraint(w, pltpu.HBM))


def spread_kernel(x_ref, o_ref):
    gap = jnp.zeros((PAD - SHARD, x_ref.shape[1]), BF)
    for y in range(4):
        for x in range(4):
            for c in range(2):
                block, slot = (y, x) if c == 0 else (4 + x, y)
                dev = place(y, x, c)
                at = slot * PAD
                o_ref[block, at : at + SHARD, :] = x_ref[dev * SHARD : (dev + 1) * SHARD, :]
                o_ref[block, at + SHARD : at + PAD, :] = gap


def spread(xt):
    n = xt.shape[1]
    blk = 256
    return pl.pallas_call(
        spread_kernel,
        grid=(n // blk,),
        in_specs=[pl.BlockSpec((D, blk), lambda g: (0, g))],
        out_specs=pl.BlockSpec((8, BLK, blk), lambda g: (0, 0, g)),
        out_shape=jax.ShapeDtypeStruct((8, BLK, n), BF),
        compiler_params=pltpu.CompilerParams(vmem_limit_bytes=8 * MIB),
        cost_estimate=QUICK,
        name="spread",
    )(xt)


def product(w, x):
    return lax.dot_general(w, x, (((0,), (0,)), ((), ())), preferred_element_type=F32)


def fast(a):
    return pltpu.with_memory_space_constraint(a, pltpu.VMEM)


def lay(pieces, wbuf):
    for i, piece in enumerate(pieces):
        wbuf[i * BLK : (i + 1) * BLK, :] = piece[...]


def block(pos, mine, d):
    which = pos[2] if mine else 1 - pos[2]
    return which * 4 + ((jnp.where(which == 0, pos[0], pos[1]) + 4 - d) & 3)


def rows_of(pos, steps, x_ref, at):
    return jnp.concatenate([x_ref[block(pos, *step), :, at] for step in steps], axis=0)


def each_group(n, step):
    for g in range(n // GROUP):
        step(g, pl.ds(g * GROUP, GROUP))


def resident(kernel, small, large, outs, scratch, limit, name, alias=None):
    return pl.pallas_call(
        kernel,
        in_specs=[pl.BlockSpec(memory_space=pltpu.SMEM)] * len(small)
        + [pl.BlockSpec(memory_space=pltpu.VMEM)] * len(large),
        out_specs=[pl.BlockSpec(memory_space=pltpu.VMEM)] * len(outs),
        out_shape=[pltpu.VMEM(shape, kind) for shape, kind in outs],
        scratch_shapes=scratch,
        input_output_aliases=alias or {},
        compiler_params=pltpu.CompilerParams(vmem_limit_bytes=limit * MIB),
        cost_estimate=QUICK,
        name=name,
    )(*small, *(fast(a) for a in large))


def part_kernel(steps, pos, *refs):
    count = len(steps)
    kv_pieces, q_pieces = refs[:count], refs[count : 2 * count]
    x_ref, kv_ref, q_ref, kv_buf, q_buf = refs[2 * count :]
    lay(kv_pieces, kv_buf)
    lay(q_pieces, q_buf)

    def step(g, at):
        x = rows_of(pos, steps, x_ref, at)
        kv_ref[:, at] = product(kv_buf[:, : 2 * HL * DH], x)
        q_ref[:, at] = product(q_buf[:, : HL * DH], x)

    each_group(x_ref.shape[2], step)


def part_call(steps, pos, kv_pieces, q_pieces, xp):
    n = xp.shape[2]
    return resident(
        functools.partial(part_kernel, steps),
        [pos],
        [*kv_pieces, *q_pieces, xp],
        [((2 * HL * DH, n), F32), ((HL * DH, n), F32)],
        [
            pltpu.VMEM((len(steps) * BLK, QCOL), BF),
            pltpu.VMEM((len(steps) * BLK, COLS - QCOL), BF),
        ],
        16,
        "part_first",
    )


def feature(raw):
    a = raw.astype(BF).astype(F32)
    return jnp.where(a > 0, a + 1.0, jnp.exp(jnp.minimum(a, 0.0))).astype(BF)


def kv_kernel(steps, pos, *refs):
    count = len(refs) - 8
    pieces = refs[:count]
    x_ref, sum_ref, fk_ref, v_ref, pre_ref, tot_ref, wbuf, run = refs[count:]
    lay(pieces, wbuf)
    run[...] = jnp.zeros_like(run)
    half = HL * DH

    def step(g, at):
        x = rows_of(pos, steps, x_ref, at)
        raw = product(wbuf[:, : 2 * half], x) + sum_ref[:, at]
        fk = feature(raw[:half, :])
        tail = (lax.broadcasted_iota(jnp.int32, (VA - DH, GROUP), 0) == 0).astype(F32).astype(BF)
        for h in range(HL):
            kn = fk[h * DH : (h + 1) * DH, :].T
            fk_ref[h, at, :] = kn
            val = raw[half + h * DH : half + (h + 1) * DH, :].astype(BF)
            va = jnp.concatenate([val, tail], axis=0)
            v_ref[h, :, at] = va
            state = jnp.dot(va, kn, preferred_element_type=F32)
            before = run[h]
            pre_ref[g, h] = before
            run[h] = before + state

    each_group(x_ref.shape[2], step)
    tot_ref[...] = run[...].astype(BF)


def kv_call(steps, pos, pieces, xp, sums):
    n = xp.shape[2]
    return resident(
        functools.partial(kv_kernel, steps),
        [pos],
        [*pieces, xp, sums],
        [
            ((HL, n, DH), BF),
            ((HL, VA, n), BF),
            ((n // GROUP, HL, VA, DH), F32),
            ((HL, VA, DH), BF),
        ],
        [pltpu.VMEM((len(pieces) * BLK, QCOL), BF), pltpu.VMEM((HL, VA, DH), F32)],
        20,
        "keys_values",
    )


def q_kernel(steps, pos, *refs):
    count = len(refs) - 4
    pieces, (x_ref, sum_ref, fq_ref, wbuf) = refs[:count], refs[count:]
    lay(pieces, wbuf)

    def step(g, at):
        x = rows_of(pos, steps, x_ref, at)
        fq_ref[:, at] = feature(product(wbuf[:, : HL * DH], x) + sum_ref[:, at])

    each_group(x_ref.shape[2], step)


def q_call(steps, pos, pieces, xp, sums):
    (out,) = resident(
        functools.partial(q_kernel, steps),
        [pos],
        [*pieces, xp, sums],
        [(sums.shape, BF)],
        [pltpu.VMEM((len(pieces) * BLK, COLS - QCOL), BF)],
        12,
        "queries",
    )
    return out


def mask_rows(code, j0, rows, t0, cols):
    parts = []
    for j in range(j0, j0 + rows // 64):
        t = lax.broadcasted_iota(jnp.int32, (64, cols), 1) + t0
        s = lax.broadcasted_iota(jnp.int32, (64, cols), 0)
        i = t >> 6
        bit = (jnp.full((64, cols), code, jnp.int32) >> (((i * (i - 1)) >> 1) + j)) & 1
        same = jnp.where(s <= (t & 63), 1, 0)
        keep = jnp.where(i > j, bit, jnp.where(i == j, same, 0))
        parts.append(keep.astype(F32).astype(BF))
    return jnp.concatenate(parts, axis=0)


def attend_kernel(groups, codes, fk_ref, v_ref, fq_ref, num_ref):
    half = GROUP // 2

    for i, g in enumerate(groups):
        code = codes[g]
        start = g * GROUP
        at = pl.ds(start, GROUP)
        one, two = pl.ds(start, half), pl.ds(start + half, half)
        to = i * GROUP
        upper = mask_rows(code, 0, half, 0, GROUP)
        lower = mask_rows(code, 4, half, half, half)
        for h in range(HL):
            fq = fq_ref[h * DH : (h + 1) * DH, at]
            top = jnp.dot(fk_ref[h, one, :], fq, preferred_element_type=F32)
            top = top.astype(BF) * upper
            low = jnp.dot(fk_ref[h, two, :], fq[:, half:], preferred_element_type=F32)
            low = low.astype(BF) * lower
            num = jnp.dot(v_ref[h, :, one], top, preferred_element_type=F32)
            more = jnp.dot(v_ref[h, :, two], low, preferred_element_type=F32)
            num_ref[h, :, to : to + half] = num[:, :half]
            num_ref[h, :, to + half : to + GROUP] = num[:, half:] + more


def attend_call(groups, codes, fk, v, fq):
    (out,) = resident(
        functools.partial(attend_kernel, groups),
        [codes],
        [fk, v, fq],
        [((HL, VA, len(groups) * GROUP), F32)],
        [],
        12,
        "attend",
    )
    return out


def chip_kernel(tot_ref, other_ref, chip_ref):
    chip_ref[...] = (tot_ref[...].astype(F32) + other_ref[...].astype(F32)).astype(BF)


def row_kernel(a, b, c, d, row_ref):
    total = a[...].astype(F32) + b[...].astype(F32) + c[...].astype(F32) + d[...].astype(F32)
    row_ref[...] = total.astype(BF)


def small(kernel, args, name):
    (out,) = resident(kernel, [], args, [(args[0].shape, BF)], [], 4, name)
    return out


def join_kernel(pos, scale, *refs):
    other, near, far = refs[0], refs[1:4], refs[4:7]
    pre_ref, fq_ref, num_one, num_rest, out_ref, sq_ref, dev = refs[7:]
    total = far[0][...].astype(F32) + far[1][...].astype(F32) + far[2][...].astype(F32)
    total = total + jnp.where(pos[2] == 1, other[...].astype(F32), 0.0)
    for d, got in enumerate(near):
        total = total + jnp.where(pos[1] >= d + 1, got[...].astype(F32), 0.0)
    dev[...] = total

    def step(g, at):
        squares = jnp.zeros((1, GROUP), F32)
        for h in range(HL):
            prefix = (dev[h] + pre_ref[g, h]).astype(BF)
            fq = fq_ref[h * DH : (h + 1) * DH, at]
            from_ref, to = (num_one, 0) if g == 0 else (num_rest, (g - 1) * GROUP)
            num = from_ref[h, :, to : to + GROUP] + jnp.dot(prefix, fq, preferred_element_type=F32)
            out = num[:DH, :] * (scale[h] / num[DH : DH + 1, :])
            out_ref[h * DH : (h + 1) * DH, at] = out
            squares = squares + jnp.sum(out * out, axis=0, keepdims=True)
        sq_ref[:, at] = squares

    each_group(fq_ref.shape[1], step)


def join_call(pos, scale, states, pre, fq, nums):
    n = fq.shape[1]
    return resident(
        join_kernel,
        [pos, scale],
        [*states, pre, fq, *nums],
        [((HL * DH, n), F32), ((1, n), F32)],
        [pltpu.VMEM((HL, VA, DH), F32)],
        12,
        "join",
    )


def norm_kernel(out_ref, s0, s1, s2, s3, gain_ref, o_ref, buf, sem):
    eye = lax.broadcasted_iota(jnp.int32, (DH, DH), 0) == lax.broadcasted_iota(
        jnp.int32, (DH, DH), 1
    )
    gains = [
        jnp.sum(jnp.where(eye, gain_ref[h : h + 1, :], 0.0), axis=1, keepdims=True)
        for h in range(HL)
    ]
    copies = []
    for g in range(out_ref.shape[1] // GROUP):
        at = slice(g * GROUP, (g + 1) * GROUP)
        squares = s0[:, at] + s1[:, at] + s2[:, at] + s3[:, at]
        inv = lax.rsqrt(squares * (1.0 / (H * DH)) + 1e-06)
        for h in range(HL):
            rows = slice(h * DH, (h + 1) * DH)
            buf[rows, at] = (out_ref[rows, at] * inv * gains[h]).astype(BF)
        here = pl.ds(g * GROUP, GROUP)
        copies.append(pltpu.make_async_copy(buf.at[:, here], o_ref.at[:, here], sem.at[g]))
        copies[-1].start()
    for copy in copies:
        copy.wait()


def norm_call(out, squares, gain):
    n = out.shape[1]
    return pl.pallas_call(
        norm_kernel,
        in_specs=[pl.BlockSpec(memory_space=pltpu.VMEM)] * 6,
        out_specs=pl.BlockSpec(memory_space=pl.ANY),
        out_shape=jax.ShapeDtypeStruct((HL * DH, n), BF),
        scratch_shapes=[
            pltpu.VMEM((HL * DH, n), BF),
            pltpu.SemaphoreType.DMA((n // GROUP,)),
        ],
        compiler_params=pltpu.CompilerParams(vmem_limit_bytes=8 * MIB),
        cost_estimate=QUICK,
        name="norm",
    )(fast(out), *(fast(a) for a in squares), fast(gain))


def body(tokens, qkv_weight, block_mask, head_scale, norm_gain):
    me = lax.axis_index("tm").astype(jnp.int32)
    y, x, core = me // 8, (me // 2) % 4, me % 2
    pos = jnp.stack([y, x, core])
    pos, gain = lax.optimization_barrier((pos, norm_gain.reshape(HL, DH)))
    shards = [stage(qkv_weight)] + [shift(qkv_weight, first_leg(d)) for d in (1, 2, 3)]
    near_kv, near_q = pack(pos, shards)
    near_kv, xt = lax.optimization_barrier((near_kv, tokens.T))
    own_kv = [near_kv] + [shift(near_kv, second_leg(d)) for d in (1, 2, 3)]
    sib_kv, first_q = [shift(near_kv, SIBLING)], [near_q, shift(near_q, SIBLING)]
    xp = spread(pltpu.with_memory_space_constraint(xt, pltpu.HBM))

    both = ((True, 0), (False, 0))
    mine = tuple((True, d) for d in (1, 2, 3))
    last = tuple((False, d) for d in (1, 2, 3))
    kv_sum, q_sum = part_call(both, pos, [near_kv, sib_kv[0]], first_q, xp)
    near_q, kv_sum, q_sum = lax.optimization_barrier((near_q, kv_sum, q_sum))
    own_q = [shift(near_q, second_leg(d)) for d in (1, 2, 3)]
    *own_kv, kv_sum = lax.optimization_barrier((*own_kv, kv_sum))
    sib_kv = [shift(a, SIBLING) for a in own_kv[1:]]
    fk, v, pre, tot = kv_call(mine + last, pos, [*own_kv[1:], *sib_kv], xp, kv_sum)

    other = shift(tot, SIBLING)
    *own_q, other = lax.optimization_barrier((*own_q, other))
    sib_q = [shift(a, SIBLING) for a in own_q]
    chip = small(chip_kernel, [tot, other], "chip")
    chip, q_sum = lax.optimization_barrier((chip, q_sum))
    fq = q_call(mine + last, pos, [*own_q, *sib_q], xp, q_sum)
    in_row = [shift(chip, along_x(d)) for d in (1, 2, 3)]
    one = attend_call((0,), block_mask, fk, v, fq)
    *in_row, one = lax.optimization_barrier((*in_row, one))
    row = small(row_kernel, [chip, *in_row], "row")
    row, fq = lax.optimization_barrier((row, fq))
    rest = attend_call((1, 2, 3), block_mask, fk, v, fq)
    above = [shift(row, later_y(d)) for d in (1, 2, 3)]

    out, squares = join_call(pos, head_scale, [other, *in_row, *above], pre, fq, (one, rest))
    squares = [squares] + [
        lax.ppermute(squares, "head", [(i, (i + d) % 4) for i in range(4)]) for d in (1, 2, 3)
    ]
    return norm_call(out, squares, gain).T


def solution(mesh):
    in_specs = (P("tm", None), P("tm", "head"), P("tm"), P("head"), P("head"))
    out_specs = P("tm", "head")
    return jax.shard_map(body, mesh=mesh, in_specs=in_specs, out_specs=out_specs, check_vma=False)
```
